128 devices in a mesh: seq: 32 (over z, x, y_lo), wshard: 4 (over y_hi, core).
Axes of the slice: x: 4, y: 4 (y_hi: 2, y_lo: 2; y = y_hi * 2 + y_lo), z: 4, core: 2. Of those that a mesh axis runs over, the one named last changes fastest.
Arguments:
- layer_in: bfloat16 [8, 4096, 1024], P('wshard', 'seq'), may hold values from -6 to 6
- gain_in: float32 [1024], replicated, may hold values from 0.25 to 1.75
- w_z: bfloat16 [1024, 2048], P('wshard'), may hold values from -0.1875 to 0.1875
- w_x: bfloat16 [1024, 2048], P('wshard'), may hold values from -0.1875 to 0.1875
- w_bc: bfloat16 [1024, 256], P('wshard'), may hold values from -0.1875 to 0.1875
- w_dt: bfloat16 [1024, 32], P('wshard'), may hold values from -0.1875 to 0.1875
- conv_x_weight: float32 [4, 2048], P(None, 'seq'), may hold values from -3 to 3
- conv_x_bias: float32 [2048], P('seq'), may hold values from -3 to 3
- conv_bc_weight: float32 [4, 256], replicated, may hold values from -3 to 3
- conv_bc_bias: float32 [256], replicated, may hold values from -3 to 3
- dt_bias: float32 [32], P('seq'), may hold values from -6 to -2
- a_log: float32 [32], P('seq'), may hold values from -1 to 2
- d_skip: float32 [32], P('seq'), may hold values from -3 to 3
- gain_norm: float32 [2048], replicated, may hold values from 0.25 to 1.75
- w_out: bfloat16 [2048, 1024], P('wshard'), may hold values from -0.125 to 0.125
- cotangent: bfloat16 [8, 4096, 1024], P('wshard', 'seq'), may hold values from -6 to 6
Outputs:
- layer_out: bfloat16 [8, 4096, 1024], P('wshard', 'seq')
- input_grad: float32 [8, 4096, 1024], P('wshard', 'seq')
- grad_gain_in: float32 [1024], replicated
- grad_w_z: float32 [1024, 2048], P('wshard')
- grad_w_x: float32 [1024, 2048], P('wshard')
- grad_w_bc: float32 [1024, 256], P('wshard')
- grad_w_dt: float32 [1024, 32], P('wshard')
- grad_conv_x_weight: float32 [4, 2048], P(None, 'seq')
- grad_conv_x_bias: float32 [2048], P('seq')
- grad_conv_bc_weight: float32 [4, 256], replicated
- grad_conv_bc_bias: float32 [256], replicated
- grad_dt_bias: float32 [32], P('seq')
- grad_a_log: float32 [32], P('seq')
- grad_d_skip: float32 [32], P('seq')
- grad_gain_norm: float32 [2048], replicated
- grad_w_out: float32 [2048, 1024], P('wshard')
The draws below stay inside these ranges and needn't reach their ends.
All inputs are finite; a program needn't handle non-finite values.
Results may differ from the reference program's by a relative error of at most 0.035.
Values may be sent and summed in bfloat16 or wider, within the bound.
A program may use at most 192 MiB of HBM per device.

```python
import jax
import jax.numpy as jnp
from jax import lax

D = 1024
HEADDIM = 64
STATE = 128
KERNEL = 4
GROUP = 256
HEADS = 32
INNER = 2048
LEN = 4096
SEQS = 8


def block_scale(own_key, dims, pieces, least, high):
    def one(dim, blocks):
        draws = jax.random.uniform(jax.random.fold_in(jax.random.fold_in(own_key, 6), dim), (blocks,), jnp.float32, least / len(pieces), high / len(pieces))
        return jnp.repeat(jnp.exp(draws), dims[dim] // blocks).reshape((-1,) + (1,) * (len(dims) - dim - 1))

    level = one(*pieces[0])
    for cut in pieces[1:]:
        level = level * one(*cut)
    return level


def normal_values(key, dims, deviation, most, pieces=(), kind=jnp.bfloat16):
    factor_of = block_scale(key, dims, pieces, -0.22, 0.18) if pieces else 1.0
    values = jax.random.normal(key, dims, jnp.float32) * deviation * factor_of
    return jnp.minimum(jnp.maximum(values, -most), most).astype(kind)


def setup_inputs(seed: int = 0) -> dict:
    key_of = jax.random.split(jax.random.key(seed), 17)
    layer_in = normal_values(key_of[0], (SEQS, LEN, D), 1.0, 6.0, ((0, 4), (1, 32)))
    gain_in = jnp.clip(1.0 + 0.15 * jax.random.normal(key_of[1], (D,), jnp.float32), 0.25, 1.75)
    w_z = normal_values(key_of[2], (D, INNER), D ** -0.5, 0.1875, ((0, 4),))
    w_x = normal_values(key_of[3], (D, INNER), D ** -0.5, 0.1875, ((0, 4),))
    w_bc = normal_values(key_of[4], (D, 2 * STATE), D ** -0.5, 0.1875, ((0, 4),))
    w_dt = normal_values(key_of[5], (D, HEADS), D ** -0.5, 0.1875, ((0, 4),))
    conv_x_weight = normal_values(key_of[6], (KERNEL, INNER), KERNEL ** -0.5, 3.0, ((1, 32),), jnp.float32)
    conv_x_bias = normal_values(key_of[7], (INNER,), 0.5, 3.0, ((0, 32),), jnp.float32)
    conv_bc_weight = normal_values(key_of[8], (KERNEL, 2 * STATE), KERNEL ** -0.5, 3.0, (), jnp.float32)
    conv_bc_bias = normal_values(key_of[9], (2 * STATE,), 0.5, 3.0, (), jnp.float32)
    dt_bias = jnp.clip(-6.0 + 4.0 * jax.random.uniform(key_of[10], (HEADS,), jnp.float32) ** block_scale(key_of[10], (HEADS,), ((0, 32),), -0.2, 0.2), -6.0, -2.0)
    a_log = jnp.clip(-1.0 + 3.0 * jax.random.uniform(key_of[11], (HEADS,), jnp.float32) ** block_scale(key_of[11], (HEADS,), ((0, 32),), -0.2, 0.2), -1.0, 2.0)
    d_skip = normal_values(key_of[12], (HEADS,), 1.0, 3.0, ((0, 32),), jnp.float32)
    gain_norm = jnp.clip(1.0 + 0.15 * jax.random.normal(key_of[13], (INNER,), jnp.float32), 0.25, 1.75)
    w_out = normal_values(key_of[14], (INNER, D), INNER ** -0.5, 0.125, ((0, 4),))
    cotangent = normal_values(key_of[15], (SEQS, LEN, D), 1.0, 6.0, ((0, 4), (1, 32)))
    return {"layer_in": layer_in, "gain_in": gain_in, "w_z": w_z, "w_x": w_x, "w_bc": w_bc, "w_dt": w_dt, "conv_x_weight": conv_x_weight, "conv_x_bias": conv_x_bias, "conv_bc_weight": conv_bc_weight, "conv_bc_bias": conv_bc_bias, "dt_bias": dt_bias, "a_log": a_log, "d_skip": d_skip, "gain_norm": gain_norm, "w_out": w_out, "cotangent": cotangent}


epsilon = 1e-05
highest = lax.Precision.HIGHEST

@jax.custom_vjp
def low(v):
    return lax.optimization_barrier(v.astype(jnp.bfloat16)).astype(jnp.float32)

@jax.custom_vjp
def low_back(v):
    return v

def low_keep(v):
    return (low(v), None)

def low_pass(kept, grad):
    return (grad,)

def back_keep(v):
    return (v, None)

def back_low(kept, grad):
    return (low(grad),)
low.defvjp(low_keep, low_pass)
low_back.defvjp(back_keep, back_low)

def conv_silu(values, kernel_taps, bias_vec):
    seq_rows = values.shape[0]
    taps_count = kernel_taps.shape[0]
    padded = jnp.pad(values, ((taps_count - 1, 0), (0, 0)))
    summed_in = bias_vec[None, :] + kernel_taps[0][None, :] * padded[0:seq_rows]
    for offset in range(1, taps_count):
        summed_in = summed_in + kernel_taps[offset][None, :] * padded[offset:offset + seq_rows]
    return jax.nn.silu(summed_in)

def group_step(carry_state, inputs, b_block, c_block, dt_block, dt_bias, a_log, d_skip):
    steps_dt = jax.nn.softplus(dt_block + dt_bias[None, :])
    log_decay = steps_dt * (-jnp.exp(a_log))[None, :]
    running = jnp.cumsum(log_decay, axis=0)
    length = inputs.shape[0]
    causal = (jnp.arange(length)[:, None] >= jnp.arange(length)[None, :])[:, :, None]
    spread = running[:, None, :] - running[None, :, :]
    decays = jnp.where(causal, jnp.exp(jnp.where(causal, spread, 0.0)), 0.0)
    intersection = jnp.dot(c_block, b_block.T, precision=highest)
    mixing = intersection[:, :, None] * decays * steps_dt[None, :, :]
    output = jnp.einsum('ijh,jhp->ihp', mixing, inputs, precision=highest)
    carried = jnp.einsum('in,hpn->ihp', c_block, carry_state, precision=highest)
    output = output + jnp.exp(running)[:, :, None] * carried + d_skip[None, :, None] * inputs
    to_end = jnp.exp(running[-1][None, :] - running) * steps_dt
    update = jnp.einsum('jhp,jn->hpn', inputs * to_end[:, :, None], b_block, precision=highest)
    new_state = jnp.exp(running[-1])[:, None, None] * carry_state + update
    return (new_state, output)

def scan_heads(inputs, conv_bc, dt_raw, dt_bias, a_log, d_skip):
    blocks_count = inputs.shape[0] // GROUP
    blocks = (inputs.reshape(blocks_count, GROUP, HEADS, HEADDIM), conv_bc[:, :STATE].reshape(blocks_count, GROUP, STATE), conv_bc[:, STATE:].reshape(blocks_count, GROUP, STATE), dt_raw.reshape(blocks_count, GROUP, HEADS))

    def advance(carry_state, block):
        x_block, b_block, c_block, t_block = block
        return group_step(carry_state, x_block, b_block, c_block, t_block, dt_bias, a_log, d_skip)
    zero_state = jnp.zeros((HEADS, HEADDIM, STATE), jnp.float32)
    last_state, outputs = lax.scan(jax.checkpoint(advance), zero_state, blocks)
    return outputs.reshape(inputs.shape[0], INNER)

def block_forward(hidden, gain_in, w_z, w_x, w_bc, w_dt, conv_x_weight, conv_x_bias, conv_bc_weight, conv_bc_bias, dt_bias, a_log, d_skip, gain_norm, w_out):
    scale_in = lax.rsqrt(lax.optimization_barrier(jnp.mean(hidden * hidden, axis=-1, keepdims=True)) + epsilon)
    normed = low(hidden * scale_in * gain_in[None, :])
    gate_lin = low_back(jnp.dot(normed, w_z, precision=highest))
    x_raw = low_back(low(jnp.dot(normed, w_x, precision=highest)))
    bc_raw = low_back(low(jnp.dot(normed, w_bc, precision=highest)))
    dt_raw = low_back(low(jnp.dot(normed, w_dt, precision=highest)))
    conv_x = low(conv_silu(x_raw, conv_x_weight, conv_x_bias))
    conv_bc = low(conv_silu(bc_raw, conv_bc_weight, conv_bc_bias))
    mixer_out = scan_heads(conv_x.reshape(-1, HEADS, HEADDIM), conv_bc, dt_raw, dt_bias, a_log, d_skip)
    mixer_out = low_back(low(mixer_out))
    gated = mixer_out * jax.nn.silu(gate_lin)
    scale_out = lax.rsqrt(lax.optimization_barrier(jnp.mean(gated * gated, axis=-1, keepdims=True)) + epsilon)
    mixed = low(gated * scale_out * gain_norm[None, :])
    return hidden + jnp.dot(mixed, w_out, precision=highest)

def reference(layer_in, gain_in, w_z, w_x, w_bc, w_dt, conv_x_weight, conv_x_bias, conv_bc_weight, conv_bc_bias, dt_bias, a_log, d_skip, gain_norm, w_out, cotangent):
    float_params = tuple((item.astype(jnp.float32) for item in (gain_in, w_z, w_x, w_bc, w_dt, conv_x_weight, conv_x_bias, conv_bc_weight, conv_bc_bias, dt_bias, a_log, d_skip, gain_norm, w_out)))

    def per_sequence(totals, sequence):
        seq_input, seq_cot = sequence
        result, pullback = jax.vjp(block_forward, seq_input.astype(jnp.float32), *float_params)
        gradients = pullback(seq_cot.astype(jnp.float32))
        totals = tuple((total + part for total, part in zip(totals, gradients[1:])))
        return (totals, (result.astype(jnp.bfloat16), gradients[0]))
    zero_totals = tuple((jnp.zeros_like(item) for item in float_params))
    totals, (outputs, input_grads) = lax.scan(per_sequence, zero_totals, (layer_in, cotangent))
    return (outputs, input_grads, totals[0], totals[1], totals[2], totals[3], totals[4], totals[5], totals[6], totals[7], totals[8], totals[9], totals[10], totals[11], totals[12], totals[13])
```

```python
import functools

import jax
import jax.numpy as jnp
from jax import lax
from jax.experimental import pallas as pl
from jax.experimental.pallas import tpu as pltpu
from jax.sharding import PartitionSpec as P

F32 = jnp.float32
BF16 = jnp.bfloat16
EPS = 1e-05
HIGHEST = lax.Precision.HIGHEST
HEADS = 32
HEAD = 64
STATE = 128
TOK = 128
SEQS = 2
ROWS = SEQS * TOK
HALO = 8
ALL = ROWS + SEQS * HALO
PAIRS = HEADS // 2
INNER = HEADS * HEAD
TAPS = 4


def mm(a, b, dims, precision=None):
    return lax.dot_general(a, b, ((dims[0], dims[1]), ((), ())), precision=precision, preferred_element_type=F32)


NN = ((1,), (0,))
NT = ((1,), (1,))
TN = ((0,), (0,))


def iota(shape, dim):
    return lax.broadcasted_iota(jnp.int32, shape, dim)


def pair_matrix(pair):
    upper = (iota((HEADS, 128), 1) >= HEAD).astype(jnp.int32)
    return (iota((HEADS, 128), 0) == 2 * pair + upper).astype(F32)


def pair_rows(pair):
    return (iota((8, HEADS), 1) == 2 * pair + iota((8, HEADS), 0)).astype(F32)


def causal_mask():
    return iota((TOK, TOK), 0) >= iota((TOK, TOK), 1)


def shifted(padded, k):
    back = TAPS - 1 - k
    if back:
        padded = pltpu.roll(padded, back, 0)
    return padded[HALO:, :]


def padded_of(rows, b):
    return jnp.concatenate(
        [rows[ROWS + HALO * b : ROWS + HALO * (b + 1), :], rows[TOK * b : TOK * (b + 1), :]], axis=0
    )


def conv_pre(padded, taps, bias):
    total = bias
    for k in range(TAPS):
        total = total + taps[k : k + 1, :] * shifted(padded, k)
    return total


def conv_back(padded, taps, bias, grad):
    pre = conv_pre(padded, taps, bias)
    sig = jax.nn.sigmoid(pre)
    d_pre = grad * (sig * (1.0 + pre * (1.0 - sig)))
    low = jnp.concatenate([jnp.zeros((HALO, d_pre.shape[1]), F32), d_pre], axis=0)
    d_pad = taps[TAPS - 1 : TAPS, :] * low
    for k in range(TAPS - 1):
        d_pad = d_pad + taps[k : k + 1, :] * pltpu.roll(low, HALO + TOK - (TAPS - 1 - k), 0)
    d_taps = [jnp.sum(d_pre * shifted(padded, k), axis=0, keepdims=True) for k in range(TAPS)]
    return d_pad, d_taps, jnp.sum(d_pre, axis=0, keepdims=True)


def block_diagonal(pair_values):
    first = iota(pair_values.shape, 1) < HEAD
    zero = jnp.zeros_like(pair_values)
    return jnp.concatenate(
        [jnp.where(first, pair_values, zero), jnp.where(first, zero, pair_values)], axis=0
    )


def decay_pair(r_lanes, r_rows):
    mask = causal_mask()
    out = []
    for q in range(2):
        spread = r_lanes[:, HEAD * q : HEAD * q + 1] - r_rows[q : q + 1, :]
        out.append(jnp.exp(jnp.where(mask, spread, -1e30)))
    return out


def front_kernel(x_raw, bc_raw, dt_raw, taps_x, bias_x, taps_bc, bias_bc, dt_bias, a_log, xc, bcc, dt, r, u):
    pair = pl.program_id(0)

    @pl.when(pair == 0)
    def _():
        raw = bc_raw[...].astype(F32)
        steps = dt_raw[0:ROWS, :].astype(F32) + dt_bias[...]
        dt[...] = jax.nn.softplus(steps)
        tri = causal_mask().astype(F32)
        decay = dt[...] * (-jnp.exp(a_log[...]))
        for b in range(SEQS):
            pre = conv_pre(padded_of(raw, b), taps_bc[...], bias_bc[...])
            bcc[TOK * b : TOK * (b + 1), :] = (pre * jax.nn.sigmoid(pre)).astype(BF16)
            r[TOK * b : TOK * (b + 1), :] = mm(tri, decay[TOK * b : TOK * (b + 1), :], NN, HIGHEST)

    raw = x_raw[...].astype(F32)
    ex = pair_matrix(pair)
    for b in range(SEQS):
        span = slice(TOK * b, TOK * (b + 1))
        pre = conv_pre(padded_of(raw, b), taps_x[...], bias_x[...])
        low = (pre * jax.nn.sigmoid(pre)).astype(BF16)
        xc[span, :] = low
        r_lanes = mm(r[span, :], ex, NN, HIGHEST)
        dt_lanes = mm(dt[span, :], ex, NN, HIGHEST)
        to_end = jnp.exp(r_lanes[TOK - 1 : TOK, :] - r_lanes)
        scaled = (to_end * (dt_lanes * low.astype(F32))).astype(BF16)
        state = mm(scaled, bcc[span, 0:STATE], TN).astype(BF16)
        u[0, b] = state[0:HEAD, :]
        u[1, b] = state[HEAD:, :]


def whole(shape):
    return pl.BlockSpec(shape, lambda *_: (0,) * len(shape))


def lanes(rows):
    return pl.BlockSpec((rows, 128), lambda j: (0, j))


STATES = pl.BlockSpec((2, SEQS, HEAD, STATE), lambda j: (j, 0, 0, 0))
STATES_SHAPE = (HEADS, SEQS, HEAD, STATE)
VMEM_LIMIT = 48 * 1024 * 1024


def call(kernel, outs, out_specs, in_specs, grid=(PAIRS,), scratch=(), cost=None):
    return pl.pallas_call(
        kernel,
        grid=grid,
        out_shape=[jax.ShapeDtypeStruct(s, d) for s, d in outs],
        in_specs=in_specs,
        out_specs=out_specs,
        scratch_shapes=scratch,
        compiler_params=pltpu.CompilerParams(
            vmem_limit_bytes=VMEM_LIMIT, dimension_semantics=("arbitrary",) * len(grid)
        ),
        cost_estimate=cost or pl.CostEstimate(flops=int(1e9), bytes_accessed=int(1e7), transcendentals=0),
    )


def front(x_raw, bc_raw, dt_raw, taps_x, bias_x, taps_bc, bias_bc, dt_bias, a_log):
    return call(
        front_kernel,
        [((ROWS, INNER), BF16), ((ROWS, 2 * STATE), BF16), ((ROWS, HEADS), F32), ((ROWS, HEADS), F32), (STATES_SHAPE, BF16)],
        [lanes(ROWS), whole((ROWS, 2 * STATE)), whole((ROWS, HEADS)), whole((ROWS, HEADS)), STATES],
        [
            lanes(ALL), whole((ALL, 2 * STATE)), whole((ALL, HEADS)), lanes(TAPS), lanes(1),
            whole((TAPS, 2 * STATE)), whole((1, 2 * STATE)), whole((1, HEADS)), whole((1, HEADS)),
        ],
    )(x_raw, bc_raw, dt_raw, taps_x, bias_x, taps_bc, bias_bc, dt_bias, a_log)


def states_kernel(reverse, decay, own, before):
    chunks = own.shape[0]

    def step(i, carry):
        c = chunks - 1 - i if reverse else i
        after = []
        for b in range(SEQS):
            before[c, b] = carry[b].astype(BF16)
            after.append(decay[c, b] * carry[b] + own[c, b].astype(F32))
        return tuple(after)

    lax.fori_loop(0, chunks, step, tuple(jnp.zeros((HEAD, STATE), F32) for _ in range(SEQS)))


def states(decay, own, reverse):
    return pl.pallas_call(
        functools.partial(states_kernel, reverse),
        out_shape=jax.ShapeDtypeStruct(own.shape, BF16),
        in_specs=[pl.BlockSpec(memory_space=pltpu.SMEM), pl.BlockSpec(memory_space=pltpu.VMEM)],
        out_specs=pl.BlockSpec(memory_space=pltpu.VMEM),
        compiler_params=pltpu.CompilerParams(vmem_limit_bytes=VMEM_LIMIT),
        cost_estimate=pl.CostEstimate(flops=int(1e6), bytes_accessed=int(2e6), transcendentals=0),
    )(decay, own)


def inside_kernel(xc, bcc, dt, r, y, scores):
    pair = pl.program_id(0)

    @pl.when(pair == 0)
    def _():
        for b in range(SEQS):
            span = slice(TOK * b, TOK * (b + 1))
            scores[b] = mm(bcc[span, STATE:], bcc[span, 0:STATE], NT)

    ex = pair_matrix(pair)
    rows = pair_rows(pair)
    for b in range(SEQS):
        span = slice(TOK * b, TOK * (b + 1))
        r_lanes = mm(r[span, :], ex, NN, HIGHEST)
        dt_lanes = mm(dt[span, :], ex, NN, HIGHEST)
        r_rows = mm(rows, r[span, :], NT, HIGHEST)
        first, second = decay_pair(r_lanes, r_rows)
        both = jnp.concatenate([scores[b] * first, scores[b] * second], axis=1).astype(BF16)
        stepped = (dt_lanes * xc[span, :].astype(F32)).astype(BF16)
        y[span, :] = mm(both, block_diagonal(stepped), NN)


def inside(xc, bcc, dt, r):
    return call(
        inside_kernel,
        [((ROWS, INNER), F32)],
        [lanes(ROWS)],
        [lanes(ROWS), whole((ROWS, 2 * STATE)), whole((ROWS, HEADS)), whole((ROWS, HEADS))],
        scratch=[pltpu.VMEM((SEQS, TOK, TOK), F32)],
    )(xc, bcc, dt, r)[0]


def middle_kernel(
    y_in, xc, bcc, r, start, d_skip, gate, d_mixed, gain,
    mixed, d_y, d_gate, own, d_gain, row_dot,
    y_all, square, cross, scale, slope,
):
    phase = pl.program_id(0)
    pair = pl.program_id(1)
    ex = pair_matrix(pair)
    skip = mm(jnp.broadcast_to(d_skip[...], (8, HEADS)), ex, NN, HIGHEST)[0:1, :]
    z = gate[...]
    sig = jax.nn.sigmoid(z)
    pulled = d_mixed[...] * gain[...]

    @pl.when(phase == 0)
    def _():
        @pl.when(pair == 0)
        def _():
            square[...] = jnp.zeros_like(square)
            cross[...] = jnp.zeros_like(cross)

        for b in range(SEQS):
            span = slice(TOK * b, TOK * (b + 1))
            before = jnp.concatenate([start[0, b], start[1, b]], axis=0)
            grown = jnp.exp(mm(r[span, :], ex, NN, HIGHEST))
            y_all[pair, span, :] = y_in[span, :] + grown * mm(bcc[span, STATE:], before, NT)
        y = (y_all[pair] + skip * xc[...].astype(F32)).astype(BF16).astype(F32)
        gated = y * (z * sig)
        square[...] += gated * gated
        cross[...] += pulled * gated

    @pl.when(phase == 1)
    def _():
        @pl.when(pair == 0)
        def _():
            inv = lax.rsqrt(jnp.sum(square[...], axis=1, keepdims=True) * (1.0 / INNER) + EPS)
            mean = jnp.sum(cross[...], axis=1, keepdims=True) * (1.0 / INNER)
            scale[...] = jnp.broadcast_to(inv, scale.shape)
            slope[...] = jnp.broadcast_to(inv * inv * inv * mean, slope.shape)
            row_dot[...] = jnp.zeros_like(row_dot)

        y = (y_all[pair] + skip * xc[...].astype(F32)).astype(BF16).astype(F32)
        silu = z * sig
        gated = y * silu
        unit = gated * scale[...]
        mixed[...] = (unit * gain[...]).astype(BF16)
        d_gain[...] = jnp.sum(d_mixed[...] * unit, axis=0, keepdims=True)
        d_gated = scale[...] * pulled - gated * slope[...]
        low = (d_gated * silu).astype(BF16)
        d_y[...] = low
        d_gate[...] = (d_gated * y * (sig * (1.0 + z * (1.0 - sig)))).astype(BF16)
        row_dot[...] += mm(low.astype(F32) * y_all[pair], ex, NT, HIGHEST)
        for b in range(SEQS):
            span = slice(TOK * b, TOK * (b + 1))
            grown = jnp.exp(mm(r[span, :], ex, NN, HIGHEST))
            state = mm((grown * low[span, :].astype(F32)).astype(BF16), bcc[span, STATE:], TN).astype(BF16)
            own[0, b] = state[0:HEAD, :]
            own[1, b] = state[HEAD:, :]


def middle(y_in, xc, bcc, r, start, d_skip, gate, d_mixed, gain):
    def cols(rows):
        return pl.BlockSpec((rows, 128), lambda p, j: (0, j))

    def first(rows):
        return pl.BlockSpec((rows, 128), lambda p, j: (0, jnp.where(p == 0, j, PAIRS - 1)))

    def second(rows):
        return pl.BlockSpec((rows, 128), lambda p, j: (0, jnp.where(p == 1, j, 0)))

    states_in = pl.BlockSpec((2, SEQS, HEAD, STATE), lambda p, j: (jnp.where(p == 0, j, PAIRS - 1), 0, 0, 0))
    states_out = pl.BlockSpec((2, SEQS, HEAD, STATE), lambda p, j: (jnp.where(p == 1, j, 0), 0, 0, 0))
    return call(
        middle_kernel,
        [((ROWS, INNER), BF16), ((ROWS, INNER), BF16), ((ROWS, INNER), BF16), (STATES_SHAPE, BF16), ((1, INNER), F32), ((ROWS, HEADS), F32)],
        [second(ROWS), second(ROWS), second(ROWS), states_out, second(1), whole((ROWS, HEADS))],
        [first(ROWS), cols(ROWS), whole((ROWS, 2 * STATE)), whole((ROWS, HEADS)), states_in, whole((1, HEADS)), cols(ROWS), cols(ROWS), cols(1)],
        grid=(2, PAIRS),
        scratch=[pltpu.VMEM((PAIRS, ROWS, 128), F32)] + [pltpu.VMEM((ROWS, 128), F32)] * 4,
    )(y_in, xc, bcc, r, start, d_skip, gate, d_mixed, gain)


def inside_back_kernel(xc, d_y, bcc, dt, r, d_stepped, d_bc, scores, d_scores):
    pair = pl.program_id(0)

    @pl.when(pair == 0)
    def _():
        d_scores[...] = jnp.zeros_like(d_scores)
        for b in range(SEQS):
            span = slice(TOK * b, TOK * (b + 1))
            scores[b] = mm(bcc[span, STATE:], bcc[span, 0:STATE], NT)

    ex = pair_matrix(pair)
    rows = pair_rows(pair)
    for b in range(SEQS):
        span = slice(TOK * b, TOK * (b + 1))
        r_lanes = mm(r[span, :], ex, NN, HIGHEST)
        dt_lanes = mm(dt[span, :], ex, NN, HIGHEST)
        r_rows = mm(rows, r[span, :], NT, HIGHEST)
        first, second = decay_pair(r_lanes, r_rows)
        both = jnp.concatenate([scores[b] * first, scores[b] * second], axis=0).astype(BF16)
        stepped = (dt_lanes * xc[span, :].astype(F32)).astype(BF16)
        wide = block_diagonal(d_y[span, :])
        d_stepped[span, :] = mm(both, wide, TN)
        d_both = mm(wide, stepped, NT)
        d_scores[b] += d_both[0:TOK, :] * first + d_both[TOK:, :] * second

    @pl.when(pair == PAIRS - 1)
    def _():
        for b in range(SEQS):
            span = slice(TOK * b, TOK * (b + 1))
            low = d_scores[b].astype(BF16)
            d_bc[span, 0:STATE] = mm(low, bcc[span, STATE:], TN)
            d_bc[span, STATE:] = mm(low, bcc[span, 0:STATE], NN)


def inside_back(xc, d_y, bcc, dt, r):
    return call(
        inside_back_kernel,
        [((ROWS, INNER), F32), ((ROWS, 2 * STATE), F32)],
        [lanes(ROWS), whole((ROWS, 2 * STATE))],
        [lanes(ROWS), lanes(ROWS), whole((ROWS, 2 * STATE)), whole((ROWS, HEADS)), whole((ROWS, HEADS))],
        scratch=[pltpu.VMEM((SEQS, TOK, TOK), F32)] * 2,
    )(xc, d_y, bcc, dt, r)


def back_kernel(
    d_stepped, xc, d_y, x_raw, start, end, bcc, dt, r, bc_raw, dt_raw, d_bc_in, row_dot,
    taps_x, bias_x, taps_bc, bias_bc, dt_bias, a_log, d_skip,
    d_x_raw, d_bc_raw, d_dt_raw, g_x, g_bc, g_heads,
    d_bc, d_dt, col_dot, ends, skips,
):
    pair = pl.program_id(0)

    @pl.when(pair == 0)
    def _():
        d_bc[...] = d_bc_in[...]
        d_dt[...] = jnp.zeros_like(d_dt)
        col_dot[...] = jnp.zeros_like(col_dot)
        ends[...] = jnp.zeros_like(ends)
        skips[...] = jnp.zeros_like(skips)

    ex = pair_matrix(pair)
    skip = mm(jnp.broadcast_to(d_skip[...], (8, HEADS)), ex, NN, HIGHEST)[0:1, :]
    raw = x_raw[...].astype(F32)
    ones = jnp.ones((8, STATE), F32)
    halos, grads = [], None
    skip_sum = jnp.zeros((1, 128), F32)
    for b in range(SEQS):
        span = slice(TOK * b, TOK * (b + 1))
        r_lanes = mm(r[span, :], ex, NN, HIGHEST)
        dt_lanes = mm(dt[span, :], ex, NN, HIGHEST)
        last = r_lanes[TOK - 1 : TOK, :]
        grown = jnp.exp(r_lanes)
        to_end = jnp.exp(last - r_lanes)
        before = jnp.concatenate([start[0, b], start[1, b]], axis=0)
        after = jnp.concatenate([end[0, b], end[1, b]], axis=0)
        x = xc[span, :].astype(F32)
        dy = d_y[span, :].astype(F32)
        stepped = (dt_lanes * x).astype(BF16).astype(F32)
        carried = to_end * mm(bcc[span, 0:STATE], after, NT)
        d_step = d_stepped[span, :] + carried
        col_dot[span, :] += mm(stepped * d_step, ex, NT, HIGHEST)
        d_x = dt_lanes * d_step + skip * dy
        d_dt[span, :] += mm(x * d_step, ex, NT, HIGHEST)
        inner = mm(ones, before.astype(F32) * after.astype(F32), NT, HIGHEST)[0:1, :]
        end_row = jnp.sum(stepped * carried, axis=0, keepdims=True) + jnp.exp(last) * inner
        ends[b] += mm(jnp.broadcast_to(end_row, (8, 128)), ex, NT, HIGHEST)
        d_bc[span, STATE:] += mm((grown * dy).astype(BF16), before, NN)
        d_bc[span, 0:STATE] += mm((to_end * stepped).astype(BF16), after, NN)
        skip_sum = skip_sum + jnp.sum(dy * x, axis=0, keepdims=True)
        d_pad, d_taps, d_bias = conv_back(padded_of(raw, b), taps_x[...], bias_x[...], d_x)
        d_x_raw[span, :] = d_pad[HALO:, :].astype(BF16)
        halos.append(d_pad[0:HALO, :])
        parts = [*d_taps, d_bias]
        grads = parts if grads is None else [g + p for g, p in zip(grads, parts)]
    d_x_raw[ROWS:, :] = jnp.concatenate(halos, axis=0).astype(BF16)
    g_x[...] = jnp.concatenate([*grads, jnp.zeros((8 - TAPS - 1, 128), F32)], axis=0)
    skips[...] += mm(jnp.broadcast_to(skip_sum, (8, 128)), ex, NT, HIGHEST)

    @pl.when(pair == PAIRS - 1)
    def _():
        raw = bc_raw[...].astype(F32)
        halos, grads = [], None
        for b in range(SEQS):
            span = slice(TOK * b, TOK * (b + 1))
            d_pad, d_taps, d_bias = conv_back(padded_of(raw, b), taps_bc[...], bias_bc[...], d_bc[span, :])
            d_bc_raw[span, :] = d_pad[HALO:, :].astype(BF16)
            halos.append(d_pad[0:HALO, :])
            parts = [*d_taps, d_bias]
            grads = parts if grads is None else [g + p for g, p in zip(grads, parts)]
        d_bc_raw[ROWS:, :] = jnp.concatenate(halos, axis=0).astype(BF16)
        g_bc[...] = jnp.concatenate([*grads, jnp.zeros((8 - TAPS - 1, 2 * STATE), F32)], axis=0)
        rate = -jnp.exp(a_log[...])
        tri = causal_mask().astype(F32)
        is_last = iota((TOK, HEADS), 0) == TOK - 1
        bias_sum = jnp.zeros((1, HEADS), F32)
        log_sum = jnp.zeros((1, HEADS), F32)
        for b in range(SEQS):
            span = slice(TOK * b, TOK * (b + 1))
            step = dt[span, :]
            d_r = row_dot[span, :] - col_dot[span, :] + jnp.where(is_last, ends[b][0:1, :], 0.0)
            d_log = mm(tri, d_r, TN, HIGHEST)
            d_pre = (d_dt[span, :] + rate * d_log) * jax.nn.sigmoid(dt_raw[span, :].astype(F32) + dt_bias[...])
            d_dt_raw[span, :] = d_pre.astype(BF16)
            bias_sum = bias_sum + jnp.sum(d_pre, axis=0, keepdims=True)
            log_sum = log_sum + jnp.sum(d_log * step, axis=0, keepdims=True) * rate
        d_dt_raw[ROWS:, :] = jnp.zeros((ALL - ROWS, HEADS), BF16)
        g_heads[...] = jnp.concatenate([bias_sum, log_sum, skips[0:1, :], jnp.zeros((5, HEADS), F32)], axis=0)


def back(d_stepped, xc, d_y, x_raw, start, end, bcc, dt, r, bc_raw, dt_raw, d_bc_in, row_dot, taps_x, bias_x, taps_bc, bias_bc, dt_bias, a_log, d_skip):
    return call(
        back_kernel,
        [((ALL, INNER), BF16), ((ALL, 2 * STATE), BF16), ((ALL, HEADS), BF16), ((8, INNER), F32), ((8, 2 * STATE), F32), ((8, HEADS), F32)],
        [lanes(ALL), whole((ALL, 2 * STATE)), whole((ALL, HEADS)), lanes(8), whole((8, 2 * STATE)), whole((8, HEADS))],
        [
            lanes(ROWS), lanes(ROWS), lanes(ROWS), lanes(ALL), STATES, STATES,
            whole((ROWS, 2 * STATE)), whole((ROWS, HEADS)), whole((ROWS, HEADS)), whole((ALL, 2 * STATE)),
            whole((ALL, HEADS)), whole((ROWS, 2 * STATE)), whole((ROWS, HEADS)),
            lanes(TAPS), lanes(1), whole((TAPS, 2 * STATE)), whole((1, 2 * STATE)),
            whole((1, HEADS)), whole((1, HEADS)), whole((1, HEADS)),
        ],
        scratch=[
            pltpu.VMEM((ROWS, 2 * STATE), F32), pltpu.VMEM((ROWS, HEADS), F32), pltpu.VMEM((ROWS, HEADS), F32),
            pltpu.VMEM((SEQS, 8, HEADS), F32), pltpu.VMEM((8, HEADS), F32),
        ],
    )(d_stepped, xc, d_y, x_raw, start, end, bcc, dt, r, bc_raw, dt_raw, d_bc_in, row_dot, taps_x, bias_x, taps_bc, bias_bc, dt_bias, a_log, d_skip)


def swap(values):
    return lax.all_to_all(values, "seq", split_axis=0, concat_axis=0, tiled=True)


def gather_rows(shard):
    return lax.all_gather(shard, "wshard", axis=0, tiled=True)


def reduce_rows(term):
    part = lax.psum_scatter(term.astype(BF16), "wshard", scatter_dimension=0, tiled=True)
    return lax.psum(part, "seq").astype(F32)


def shards(
    layer_in, gain_in, w_z, w_x, w_bc, w_dt, conv_x_weight, conv_x_bias, conv_bc_weight, conv_bc_bias,
    dt_bias, a_log, d_skip, gain_norm, w_out, cotangent,
):
    width = layer_in.shape[2]
    chunks = lax.axis_size("seq")
    place = lax.axis_index("seq")
    tail = lax.ppermute(layer_in[:, TOK - (TAPS - 1) :, :], "seq", [(i, i + 1) for i in range(chunks - 1)])
    full_x = gather_rows(w_x)
    full_small = gather_rows(jnp.concatenate([w_bc, w_dt], axis=1))
    full_bc, full_dt = full_small[:, : 2 * STATE], full_small[:, 2 * STATE :]
    full_z = gather_rows(w_z)
    full_out = gather_rows(w_out)
    own = jnp.concatenate([conv_x_weight.reshape(-1), conv_x_bias, dt_bias, a_log, d_skip, jnp.zeros((61,), F32)])
    params = lax.all_gather(own, "seq", axis=0, tiled=False)
    taps_x = params[:, : TAPS * HEAD].reshape(HEADS, TAPS, HEAD).swapaxes(0, 1).reshape(TAPS, INNER)
    bias_x = params[:, TAPS * HEAD : (TAPS + 1) * HEAD].reshape(1, INNER)
    bias_dt, log_a, skip = (params[:, (TAPS + 1) * HEAD + i].reshape(1, HEADS) for i in range(3))
    bias_bc = conv_bc_bias.reshape(1, -1)

    hidden = layer_in.astype(F32).reshape(ROWS, width)
    upstream = cotangent.reshape(ROWS, width)
    halo = jnp.pad(tail, ((0, 0), (HALO - (TAPS - 1), 0), (0, 0))).reshape(SEQS * HALO, width).astype(F32)
    tokens = jnp.concatenate([hidden, halo], axis=0)
    inv = lax.rsqrt(jnp.mean(tokens * tokens, axis=-1, keepdims=True) + EPS)
    normed = (tokens * inv * gain_in[None, :]).astype(BF16)
    inv = inv[:ROWS]

    x_raw = mm(normed, full_x, NN).astype(BF16)
    bc_raw = mm(normed, full_bc, NN).astype(BF16)
    dt_raw = mm(normed, full_dt, NN).astype(BF16)
    xc, bcc, dt, r, u = front(x_raw, bc_raw, dt_raw, taps_x, bias_x, conv_bc_weight, bias_bc, bias_dt, log_a)
    decay = jnp.exp(swap(r[TOK - 1 :: TOK].T))
    u_all = swap(u)
    y_in = inside(xc, bcc, dt, r)
    gate = mm(normed[:ROWS], full_z, NN)
    d_mixed = mm(upstream, full_out, NT)
    start = swap(states(decay, u_all, False))
    mixed, d_y, d_gate, v, g_norm, row_dot = middle(
        y_in, xc, bcc, r, start, skip, gate, d_mixed, gain_norm.reshape(1, INNER)
    )
    v_all = swap(v)
    layer_out = (hidden + mm(mixed, full_out, NN)).astype(BF16).reshape(SEQS, TOK, width)
    grad_w_out = reduce_rows(mm(mixed, upstream, TN))
    grad_w_z = reduce_rows(mm(normed[:ROWS], d_gate, TN))
    d_stepped, d_bc_in = inside_back(xc, d_y, bcc, dt, r)
    d_normed_z = mm(d_gate, full_z, NT)
    end = swap(states(decay, v_all, True))
    d_x_raw, d_bc_raw, d_dt_raw, g_x, g_bc, g_heads = back(
        d_stepped, xc, d_y, x_raw, start, end, bcc, dt, r, bc_raw, dt_raw, d_bc_in, row_dot,
        taps_x, bias_x, conv_bc_weight, bias_bc, bias_dt, log_a, skip,
    )
    grad_w_x = reduce_rows(mm(normed, d_x_raw, TN))
    grad_small = reduce_rows(jnp.concatenate([mm(normed, d_bc_raw, TN), mm(normed, d_dt_raw, TN)], axis=1))
    d_normed = mm(d_x_raw, full_x, NT) + mm(d_bc_raw, full_bc, NT) + mm(d_dt_raw, full_dt, NT)
    back_tail = d_normed[ROWS:].reshape(SEQS, HALO, width)[:, HALO - (TAPS - 1) :]
    back_tail = lax.ppermute(back_tail, "seq", [(i + 1, i) for i in range(chunks - 1)])
    d_normed = d_normed[:ROWS] + d_normed_z
    d_normed = d_normed + jnp.pad(back_tail, ((0, 0), (TOK - (TAPS - 1), 0), (0, 0))).reshape(ROWS, width)
    unit = hidden * inv
    g_in = jnp.sum(d_normed * unit, axis=0)
    pulled = d_normed * gain_in[None, :]
    d_hidden = inv * (pulled - unit * jnp.mean(pulled * unit, axis=-1, keepdims=True))
    input_grad = (upstream.astype(F32) + d_hidden).reshape(SEQS, TOK, width)

    pieces = (g_x[: TAPS + 1], g_bc[: TAPS + 1], g_heads[:3], g_in, g_norm)
    sizes = [p.size for p in pieces]
    total = lax.psum(jnp.concatenate([p.reshape(-1) for p in pieces]), ("seq", "wshard"))
    ends = [sum(sizes[: i + 1]) for i in range(len(sizes) - 1)]
    s_x, s_bc, s_heads, s_in, s_norm = jnp.split(total, ends)
    s_x = lax.dynamic_slice(s_x.reshape(TAPS + 1, INNER), (0, place * HEAD), (TAPS + 1, HEAD))
    s_bc = s_bc.reshape(TAPS + 1, 2 * STATE)
    s_heads = lax.dynamic_slice(s_heads.reshape(3, HEADS), (0, place), (3, 1))
    return (
        layer_out, input_grad, s_in, grad_w_z, grad_w_x, grad_small[:, : 2 * STATE], grad_small[:, 2 * STATE :],
        s_x[:TAPS], s_x[TAPS], s_bc[:TAPS], s_bc[TAPS], s_heads[0], s_heads[1], s_heads[2], s_norm, grad_w_out,
    )


def solution(mesh):
    rows, heads = P("wshard", None), P("seq")
    tokens = P("wshard", "seq", None)
    return jax.shard_map(
        shards,
        mesh=mesh,
        in_specs=(
            tokens, P(), rows, rows, rows, rows, P(None, "seq"), heads, P(), P(), heads, heads, heads, P(), rows, tokens,
        ),
        out_specs=(
            tokens, tokens, P(), rows, rows, rows, rows, P(None, "seq"), heads, P(), P(), heads, heads, heads, P(), rows,
        ),
        check_vma=False,
    )
```

```python
import functools

import jax
import jax.numpy as jnp
from jax import lax
from jax.experimental import pallas as pl
from jax.experimental.pallas import tpu as pltpu
from jax.sharding import PartitionSpec as P

F32 = jnp.float32
BF16 = jnp.bfloat16
EPS = 1e-05
HIGHEST = lax.Precision.HIGHEST
HEADS = 32
HEAD = 64
STATE = 128
TOK = 128
SEQS = 2
ROWS = SEQS * TOK
HALO = 8
ALL = ROWS + SEQS * HALO
PAIRS = HEADS // 2
INNER = HEADS * HEAD
TAPS = 4


def mm(a, b, dims, precision=None):
    return lax.dot_general(a, b, ((dims[0], dims[1]), ((), ())), precision=precision, preferred_element_type=F32)


NN = ((1,), (0,))
NT = ((1,), (1,))
TN = ((0,), (0,))


def iota(shape, dim):
    return lax.broadcasted_iota(jnp.int32, shape, dim)


def pair_matrix(pair):
    upper = (iota((HEADS, 128), 1) >= HEAD).astype(jnp.int32)
    return (iota((HEADS, 128), 0) == 2 * pair + upper).astype(F32)


def pair_rows(pair):
    return (iota((8, HEADS), 1) == 2 * pair + iota((8, HEADS), 0)).astype(F32)


def causal_mask():
    return iota((TOK, TOK), 0) >= iota((TOK, TOK), 1)


def shifted(padded, k):
    back = TAPS - 1 - k
    if back:
        padded = pltpu.roll(padded, back, 0)
    return padded[HALO:, :]


def padded_of(rows, b):
    return jnp.concatenate(
        [rows[ROWS + HALO * b : ROWS + HALO * (b + 1), :], rows[TOK * b : TOK * (b + 1), :]], axis=0
    )


def conv_pre(padded, taps, bias):
    total = bias
    for k in range(TAPS):
        total = total + taps[k : k + 1, :] * shifted(padded, k)
    return total


def conv_back(padded, taps, bias, grad):
    pre = conv_pre(padded, taps, bias)
    sig = jax.nn.sigmoid(pre)
    d_pre = grad * (sig * (1.0 + pre * (1.0 - sig)))
    low = jnp.concatenate([jnp.zeros((HALO, d_pre.shape[1]), F32), d_pre], axis=0)
    d_pad = taps[TAPS - 1 : TAPS, :] * low
    for k in range(TAPS - 1):
        d_pad = d_pad + taps[k : k + 1, :] * pltpu.roll(low, HALO + TOK - (TAPS - 1 - k), 0)
    d_taps = [jnp.sum(d_pre * shifted(padded, k), axis=0, keepdims=True) for k in range(TAPS)]
    return d_pad, d_taps, jnp.sum(d_pre, axis=0, keepdims=True)


def block_diagonal(pair_values):
    first = iota(pair_values.shape, 1) < HEAD
    zero = jnp.zeros_like(pair_values)
    return jnp.concatenate(
        [jnp.where(first, pair_values, zero), jnp.where(first, zero, pair_values)], axis=0
    )


def decay_pair(r_lanes, r_rows):
    mask = causal_mask()
    out = []
    for q in range(2):
        spread = r_lanes[:, HEAD * q : HEAD * q + 1] - r_rows[q : q + 1, :]
        out.append(jnp.exp(jnp.where(mask, spread, -1e30)))
    return out


def front_kernel(x_raw, bc_raw, dt_raw, taps_x, bias_x, taps_bc, bias_bc, dt_bias, a_log, xc, bcc, dt, r, u):
    pair = pl.program_id(0)

    @pl.when(pair == 0)
    def _():
        raw = bc_raw[...].astype(F32)
        steps = dt_raw[0:ROWS, :].astype(F32) + dt_bias[...]
        dt[...] = jax.nn.softplus(steps)
        tri = causal_mask().astype(F32)
        decay = dt[...] * (-jnp.exp(a_log[...]))
        for b in range(SEQS):
            pre = conv_pre(padded_of(raw, b), taps_bc[...], bias_bc[...])
            bcc[TOK * b : TOK * (b + 1), :] = (pre * jax.nn.sigmoid(pre)).astype(BF16)
            r[TOK * b : TOK * (b + 1), :] = mm(tri, decay[TOK * b : TOK * (b + 1), :], NN, HIGHEST)

    raw = x_raw[...].astype(F32)
    ex = pair_matrix(pair)
    for b in range(SEQS):
        span = slice(TOK * b, TOK * (b + 1))
        pre = conv_pre(padded_of(raw, b), taps_x[...], bias_x[...])
        low = (pre * jax.nn.sigmoid(pre)).astype(BF16)
        xc[span, :] = low
        r_lanes = mm(r[span, :], ex, NN, HIGHEST)
        dt_lanes = mm(dt[span, :], ex, NN, HIGHEST)
        to_end = jnp.exp(r_lanes[TOK - 1 : TOK, :] - r_lanes)
        scaled = (to_end * (dt_lanes * low.astype(F32))).astype(BF16)
        state = mm(scaled, bcc[span, 0:STATE], TN).astype(BF16)
        u[0, b] = state[0:HEAD, :]
        u[1, b] = state[HEAD:, :]


def whole(shape):
    return pl.BlockSpec(shape, lambda *_: (0,) * len(shape))


def lanes(rows):
    return pl.BlockSpec((rows, 128), lambda j: (0, j))


STATES = pl.BlockSpec((2, SEQS, HEAD, STATE), lambda j: (j, 0, 0, 0))
STATES_SHAPE = (HEADS, SEQS, HEAD, STATE)
VMEM_LIMIT = 48 * 1024 * 1024


def call(kernel, outs, out_specs, in_specs, grid=(PAIRS,), scratch=(), cost=None):
    return pl.pallas_call(
        kernel,
        grid=grid,
        out_shape=[jax.ShapeDtypeStruct(s, d) for s, d in outs],
        in_specs=in_specs,
        out_specs=out_specs,
        scratch_shapes=scratch,
        compiler_params=pltpu.CompilerParams(
            vmem_limit_bytes=VMEM_LIMIT, dimension_semantics=("arbitrary",) * len(grid)
        ),
        cost_estimate=cost or pl.CostEstimate(flops=int(1e9), bytes_accessed=int(1e7), transcendentals=0),
    )


def front(x_raw, bc_raw, dt_raw, taps_x, bias_x, taps_bc, bias_bc, dt_bias, a_log):
    return call(
        front_kernel,
        [((ROWS, INNER), BF16), ((ROWS, 2 * STATE), BF16), ((ROWS, HEADS), F32), ((ROWS, HEADS), F32), (STATES_SHAPE, BF16)],
        [lanes(ROWS), whole((ROWS, 2 * STATE)), whole((ROWS, HEADS)), whole((ROWS, HEADS)), STATES],
        [
            lanes(ALL), whole((ALL, 2 * STATE)), whole((ALL, HEADS)), lanes(TAPS), lanes(1),
            whole((TAPS, 2 * STATE)), whole((1, 2 * STATE)), whole((1, HEADS)), whole((1, HEADS)),
        ],
    )(x_raw, bc_raw, dt_raw, taps_x, bias_x, taps_bc, bias_bc, dt_bias, a_log)


def states_kernel(reverse, decay, own, before):
    chunks = own.shape[0]

    def step(i, carry):
        c = chunks - 1 - i if reverse else i
        after = []
        for b in range(SEQS):
            before[c, b] = carry[b].astype(BF16)
            after.append(decay[c, b] * carry[b] + own[c, b].astype(F32))
        return tuple(after)

    lax.fori_loop(0, chunks, step, tuple(jnp.zeros((HEAD, STATE), F32) for _ in range(SEQS)))


def states(decay, own, reverse):
    return pl.pallas_call(
        functools.partial(states_kernel, reverse),
        out_shape=jax.ShapeDtypeStruct(own.shape, BF16),
        in_specs=[pl.BlockSpec(memory_space=pltpu.SMEM), pl.BlockSpec(memory_space=pltpu.VMEM)],
        out_specs=pl.BlockSpec(memory_space=pltpu.VMEM),
        compiler_params=pltpu.CompilerParams(vmem_limit_bytes=VMEM_LIMIT),
        cost_estimate=pl.CostEstimate(flops=int(1e6), bytes_accessed=int(2e6), transcendentals=0),
    )(decay, own)


def inside_kernel(xc, bcc, dt, r, y, scores):
    pair = pl.program_id(0)

    @pl.when(pair == 0)
    def _():
        for b in range(SEQS):
            span = slice(TOK * b, TOK * (b + 1))
            scores[b] = mm(bcc[span, STATE:], bcc[span, 0:STATE], NT)

    ex = pair_matrix(pair)
    rows = pair_rows(pair)
    for b in range(SEQS):
        span = slice(TOK * b, TOK * (b + 1))
        r_lanes = mm(r[span, :], ex, NN, HIGHEST)
        dt_lanes = mm(dt[span, :], ex, NN, HIGHEST)
        r_rows = mm(rows, r[span, :], NT, HIGHEST)
        first, second = decay_pair(r_lanes, r_rows)
        both = jnp.concatenate([scores[b] * first, scores[b] * second], axis=1).astype(BF16)
        stepped = (dt_lanes * xc[span, :].astype(F32)).astype(BF16)
        y[span, :] = mm(both, block_diagonal(stepped), NN)


def inside(xc, bcc, dt, r):
    return call(
        inside_kernel,
        [((ROWS, INNER), F32)],
        [lanes(ROWS)],
        [lanes(ROWS), whole((ROWS, 2 * STATE)), whole((ROWS, HEADS)), whole((ROWS, HEADS))],
        scratch=[pltpu.VMEM((SEQS, TOK, TOK), F32)],
    )(xc, bcc, dt, r)[0]


def middle_kernel(
    y_in, xc, bcc, r, start, d_skip, gate, d_mixed, gain,
    mixed, d_y, d_gate, own, d_gain, row_dot,
    y_all, square, cross, scale, slope,
):
    phase = pl.program_id(0)
    pair = pl.program_id(1)
    ex = pair_matrix(pair)
    skip = mm(jnp.broadcast_to(d_skip[...], (8, HEADS)), ex, NN, HIGHEST)[0:1, :]
    z = gate[...]
    sig = jax.nn.sigmoid(z)
    pulled = d_mixed[...] * gain[...]

    @pl.when(phase == 0)
    def _():
        @pl.when(pair == 0)
        def _():
            square[...] = jnp.zeros_like(square)
            cross[...] = jnp.zeros_like(cross)

        for b in range(SEQS):
            span = slice(TOK * b, TOK * (b + 1))
            before = jnp.concatenate([start[0, b], start[1, b]], axis=0)
            grown = jnp.exp(mm(r[span, :], ex, NN, HIGHEST))
            y_all[pair, span, :] = y_in[span, :] + grown * mm(bcc[span, STATE:], before, NT)
        y = (y_all[pair] + skip * xc[...].astype(F32)).astype(BF16).astype(F32)
        gated = y * (z * sig)
        square[...] += gated * gated
        cross[...] += pulled * gated

    @pl.when(phase == 1)
    def _():
        @pl.when(pair == 0)
        def _():
            inv = lax.rsqrt(jnp.sum(square[...], axis=1, keepdims=True) * (1.0 / INNER) + EPS)
            mean = jnp.sum(cross[...], axis=1, keepdims=True) * (1.0 / INNER)
            scale[...] = jnp.broadcast_to(inv, scale.shape)
            slope[...] = jnp.broadcast_to(inv * inv * inv * mean, slope.shape)
            row_dot[...] = jnp.zeros_like(row_dot)

        y = (y_all[pair] + skip * xc[...].astype(F32)).astype(BF16).astype(F32)
        silu = z * sig
        gated = y * silu
        unit = gated * scale[...]
        mixed[...] = (unit * gain[...]).astype(BF16)
        d_gain[...] = jnp.sum(d_mixed[...] * unit, axis=0, keepdims=True)
        d_gated = scale[...] * pulled - gated * slope[...]
        low = (d_gated * silu).astype(BF16)
        d_y[...] = low
        d_gate[...] = (d_gated * y * (sig * (1.0 + z * (1.0 - sig)))).astype(BF16)
        row_dot[...] += mm(low.astype(F32) * y_all[pair], ex, NT, HIGHEST)
        for b in range(SEQS):
            span = slice(TOK * b, TOK * (b + 1))
            grown = jnp.exp(mm(r[span, :], ex, NN, HIGHEST))
            state = mm((grown * low[span, :].astype(F32)).astype(BF16), bcc[span, STATE:], TN).astype(BF16)
            own[0, b] = state[0:HEAD, :]
            own[1, b] = state[HEAD:, :]


def middle(y_in, xc, bcc, r, start, d_skip, gate, d_mixed, gain):
    def cols(rows):
        return pl.BlockSpec((rows, 128), lambda p, j: (0, j))

    def first(rows):
        return pl.BlockSpec((rows, 128), lambda p, j: (0, jnp.where(p == 0, j, PAIRS - 1)))

    def second(rows):
        return pl.BlockSpec((rows, 128), lambda p, j: (0, jnp.where(p == 1, j, 0)))

    states_in = pl.BlockSpec((2, SEQS, HEAD, STATE), lambda p, j: (jnp.where(p == 0, j, PAIRS - 1), 0, 0, 0))
    states_out = pl.BlockSpec((2, SEQS, HEAD, STATE), lambda p, j: (jnp.where(p == 1, j, 0), 0, 0, 0))
    return call(
        middle_kernel,
        [((ROWS, INNER), BF16), ((ROWS, INNER), BF16), ((ROWS, INNER), BF16), (STATES_SHAPE, BF16), ((1, INNER), F32), ((ROWS, HEADS), F32)],
        [second(ROWS), second(ROWS), second(ROWS), states_out, second(1), whole((ROWS, HEADS))],
        [first(ROWS), cols(ROWS), whole((ROWS, 2 * STATE)), whole((ROWS, HEADS)), states_in, whole((1, HEADS)), cols(ROWS), cols(ROWS), cols(1)],
        grid=(2, PAIRS),
        scratch=[pltpu.VMEM((PAIRS, ROWS, 128), F32)] + [pltpu.VMEM((ROWS, 128), F32)] * 4,
    )(y_in, xc, bcc, r, start, d_skip, gate, d_mixed, gain)


def inside_back_kernel(xc, d_y, bcc, dt, r, d_stepped, d_bc, scores, d_scores):
    pair = pl.program_id(0)

    @pl.when(pair == 0)
    def _():
        d_scores[...] = jnp.zeros_like(d_scores)
        for b in range(SEQS):
            span = slice(TOK * b, TOK * (b + 1))
            scores[b] = mm(bcc[span, STATE:], bcc[span, 0:STATE], NT)

    ex = pair_matrix(pair)
    rows = pair_rows(pair)
    for b in range(SEQS):
        span = slice(TOK * b, TOK * (b + 1))
        r_lanes = mm(r[span, :], ex, NN, HIGHEST)
        dt_lanes = mm(dt[span, :], ex, NN, HIGHEST)
        r_rows = mm(rows, r[span, :], NT, HIGHEST)
        first, second = decay_pair(r_lanes, r_rows)
        both = jnp.concatenate([scores[b] * first, scores[b] * second], axis=0).astype(BF16)
        stepped = (dt_lanes * xc[span, :].astype(F32)).astype(BF16)
        wide = block_diagonal(d_y[span, :])
        d_stepped[span, :] = mm(both, wide, TN)
        d_both = mm(wide, stepped, NT)
        d_scores[b] += d_both[0:TOK, :] * first + d_both[TOK:, :] * second

    @pl.when(pair == PAIRS - 1)
    def _():
        for b in range(SEQS):
            span = slice(TOK * b, TOK * (b + 1))
            low = d_scores[b].astype(BF16)
            d_bc[span, 0:STATE] = mm(low, bcc[span, STATE:], TN)
            d_bc[span, STATE:] = mm(low, bcc[span, 0:STATE], NN)


def inside_back(xc, d_y, bcc, dt, r):
    return call(
        inside_back_kernel,
        [((ROWS, INNER), F32), ((ROWS, 2 * STATE), F32)],
        [lanes(ROWS), whole((ROWS, 2 * STATE))],
        [lanes(ROWS), lanes(ROWS), whole((ROWS, 2 * STATE)), whole((ROWS, HEADS)), whole((ROWS, HEADS))],
        scratch=[pltpu.VMEM((SEQS, TOK, TOK), F32)] * 2,
    )(xc, d_y, bcc, dt, r)


def back_kernel(
    d_stepped, xc, d_y, x_raw, start, end, bcc, dt, r, bc_raw, dt_raw, d_bc_in, row_dot,
    taps_x, bias_x, taps_bc, bias_bc, dt_bias, a_log, d_skip,
    d_x_raw, d_bc_raw, d_dt_raw, g_x, g_bc, g_heads,
    d_bc, d_dt, col_dot, ends, skips,
):
    pair = pl.program_id(0)

    @pl.when(pair == 0)
    def _():
        d_bc[...] = d_bc_in[...]
        d_dt[...] = jnp.zeros_like(d_dt)
        col_dot[...] = jnp.zeros_like(col_dot)
        ends[...] = jnp.zeros_like(ends)
        skips[...] = jnp.zeros_like(skips)

    ex = pair_matrix(pair)
    skip = mm(jnp.broadcast_to(d_skip[...], (8, HEADS)), ex, NN, HIGHEST)[0:1, :]
    raw = x_raw[...].astype(F32)
    ones = jnp.ones((8, STATE), F32)
    halos, grads = [], None
    skip_sum = jnp.zeros((1, 128), F32)
    for b in range(SEQS):
        span = slice(TOK * b, TOK * (b + 1))
        r_lanes = mm(r[span, :], ex, NN, HIGHEST)
        dt_lanes = mm(dt[span, :], ex, NN, HIGHEST)
        last = r_lanes[TOK - 1 : TOK, :]
        grown = jnp.exp(r_lanes)
        to_end = jnp.exp(last - r_lanes)
        before = jnp.concatenate([start[0, b], start[1, b]], axis=0)
        after = jnp.concatenate([end[0, b], end[1, b]], axis=0)
        x = xc[span, :].astype(F32)
        dy = d_y[span, :].astype(F32)
        stepped = (dt_lanes * x).astype(BF16).astype(F32)
        carried = to_end * mm(bcc[span, 0:STATE], after, NT)
        d_step = d_stepped[span, :] + carried
        col_dot[span, :] += mm(stepped * d_step, ex, NT, HIGHEST)
        d_x = dt_lanes * d_step + skip * dy
        d_dt[span, :] += mm(x * d_step, ex, NT, HIGHEST)
        inner = mm(ones, before.astype(F32) * after.astype(F32), NT, HIGHEST)[0:1, :]
        end_row = jnp.sum(stepped * carried, axis=0, keepdims=True) + jnp.exp(last) * inner
        ends[b] += mm(jnp.broadcast_to(end_row, (8, 128)), ex, NT, HIGHEST)
        d_bc[span, STATE:] += mm((grown * dy).astype(BF16), before, NN)
        d_bc[span, 0:STATE] += mm((to_end * stepped).astype(BF16), after, NN)
        skip_sum = skip_sum + jnp.sum(dy * x, axis=0, keepdims=True)
        d_pad, d_taps, d_bias = conv_back(padded_of(raw, b), taps_x[...], bias_x[...], d_x)
        d_x_raw[span, :] = d_pad[HALO:, :].astype(BF16)
        halos.append(d_pad[0:HALO, :])
        parts = [*d_taps, d_bias]
        grads = parts if grads is None else [g + p for g, p in zip(grads, parts)]
    d_x_raw[ROWS:, :] = jnp.concatenate(halos, axis=0).astype(BF16)
    g_x[...] = jnp.concatenate([*grads, jnp.zeros((8 - TAPS - 1, 128), F32)], axis=0)
    skips[...] += mm(jnp.broadcast_to(skip_sum, (8, 128)), ex, NT, HIGHEST)

    @pl.when(pair == PAIRS - 1)
    def _():
        raw = bc_raw[...].astype(F32)
        halos, grads = [], None
        for b in range(SEQS):
            span = slice(TOK * b, TOK * (b + 1))
            d_pad, d_taps, d_bias = conv_back(padded_of(raw, b), taps_bc[...], bias_bc[...], d_bc[span, :])
            d_bc_raw[span, :] = d_pad[HALO:, :].astype(BF16)
            halos.append(d_pad[0:HALO, :])
            parts = [*d_taps, d_bias]
            grads = parts if grads is None else [g + p for g, p in zip(grads, parts)]
        d_bc_raw[ROWS:, :] = jnp.concatenate(halos, axis=0).astype(BF16)
        g_bc[...] = jnp.concatenate([*grads, jnp.zeros((8 - TAPS - 1, 2 * STATE), F32)], axis=0)
        rate = -jnp.exp(a_log[...])
        tri = causal_mask().astype(F32)
        is_last = iota((TOK, HEADS), 0) == TOK - 1
        bias_sum = jnp.zeros((1, HEADS), F32)
        log_sum = jnp.zeros((1, HEADS), F32)
        for b in range(SEQS):
            span = slice(TOK * b, TOK * (b + 1))
            step = dt[span, :]
            d_r = row_dot[span, :] - col_dot[span, :] + jnp.where(is_last, ends[b][0:1, :], 0.0)
            d_log = mm(tri, d_r, TN, HIGHEST)
            d_pre = (d_dt[span, :] + rate * d_log) * jax.nn.sigmoid(dt_raw[span, :].astype(F32) + dt_bias[...])
            d_dt_raw[span, :] = d_pre.astype(BF16)
            bias_sum = bias_sum + jnp.sum(d_pre, axis=0, keepdims=True)
            log_sum = log_sum + jnp.sum(d_log * step, axis=0, keepdims=True) * rate
        d_dt_raw[ROWS:, :] = jnp.zeros((ALL - ROWS, HEADS), BF16)
        g_heads[...] = jnp.concatenate([bias_sum, log_sum, skips[0:1, :], jnp.zeros((5, HEADS), F32)], axis=0)


def back(d_stepped, xc, d_y, x_raw, start, end, bcc, dt, r, bc_raw, dt_raw, d_bc_in, row_dot, taps_x, bias_x, taps_bc, bias_bc, dt_bias, a_log, d_skip):
    return call(
        back_kernel,
        [((ALL, INNER), BF16), ((ALL, 2 * STATE), BF16), ((ALL, HEADS), BF16), ((8, INNER), F32), ((8, 2 * STATE), F32), ((8, HEADS), F32)],
        [lanes(ALL), whole((ALL, 2 * STATE)), whole((ALL, HEADS)), lanes(8), whole((8, 2 * STATE)), whole((8, HEADS))],
        [
            lanes(ROWS), lanes(ROWS), lanes(ROWS), lanes(ALL), STATES, STATES,
            whole((ROWS, 2 * STATE)), whole((ROWS, HEADS)), whole((ROWS, HEADS)), whole((ALL, 2 * STATE)),
            whole((ALL, HEADS)), whole((ROWS, 2 * STATE)), whole((ROWS, HEADS)),
            lanes(TAPS), lanes(1), whole((TAPS, 2 * STATE)), whole((1, 2 * STATE)),
            whole((1, HEADS)), whole((1, HEADS)), whole((1, HEADS)),
        ],
        scratch=[
            pltpu.VMEM((ROWS, 2 * STATE), F32), pltpu.VMEM((ROWS, HEADS), F32), pltpu.VMEM((ROWS, HEADS), F32),
            pltpu.VMEM((SEQS, 8, HEADS), F32), pltpu.VMEM((8, HEADS), F32),
        ],
    )(d_stepped, xc, d_y, x_raw, start, end, bcc, dt, r, bc_raw, dt_raw, d_bc_in, row_dot, taps_x, bias_x, taps_bc, bias_bc, dt_bias, a_log, d_skip)


REDUCE = (("x", "y", "z"), ("y", "z", "x"), ("z", "x", "y"))
GATHER = (("l", "z", "x"), ("l", "x", "z"), ("x", "z", "l"))
PIECE = 128
EXTRA = 32
PIECE_ROWS = (PIECE, PIECE + EXTRA, PIECE)
SMALL = 3 * 128


def position():
    seq, shard = lax.axis_index("seq"), lax.axis_index("wshard")
    high, core = shard // 2, shard % 2
    low = seq % 2
    return {"z": seq // 8, "x": (seq // 2) % 4, "y": high * 2 + low, "l": low, "core": core}


def device(at):
    return {"seq": at["z"] * 8 + at["x"] * 2 + at["y"] % 2, "wshard": (at["y"] // 2) * 2 + at["core"]}


def moved(at, axis, to):
    new = dict(at)
    if axis == "l":
        new["y"] = (at["y"] // 2) * 2 + to
        new["l"] = to
    else:
        new[axis] = to
        if axis == "y":
            new["l"] = to % 2
    return new


def peers(at, axis):
    size = 2 if axis in ("l", "core") else 4
    return [moved(at, axis, lax.rem(at[axis] + d, size)) for d in range(1, size)]


def greet(everyone):
    barrier = pltpu.get_barrier_semaphore()
    for other in everyone:
        pl.semaphore_signal(barrier, inc=1, device_id=device(other), device_id_type=pl.DeviceIdType.MESH)
    pl.semaphore_wait(barrier, len(everyone))


def reduce_kernel(
    keep_n, give_n, d_gate, d_wide, d_small, keep_m, give_m, cot, vector,
    out_z, out_x, out_out,
    sib_n, sib_gate, sib_wide, sib_small, sib_m, sib_cot, sib_vector,
    parts_z, parts_x, parts_out,
    got_z1, got_x1, got_out1, sum_z1, sum_x1, sum_out1,
    got_z2, got_x2, got_out2, sum_z2, sum_x2, sum_out2,
    got_z3, got_x3, got_out3,
    sib_send, sib_recv, red_send, red_recv, all_send, all_recv,
):
    at = position()
    sibling = peers(at, "core")[0]
    everyone = [sibling] + [p for axis in ("x", "y", "z") for p in peers(at, axis)]
    greet(everyone)
    started = []

    def copy(src, dst, send, recv, to):
        one = pltpu.make_async_remote_copy(
            src_ref=src, dst_ref=dst, send_sem=send, recv_sem=recv,
            device_id=device(to), device_id_type=pl.DeviceIdType.MESH,
        )
        one.start()
        started.append(one)
        return one

    given = (give_n, d_gate, give_m, cot, d_wide, d_small, vector)
    taken = (sib_n, sib_gate, sib_m, sib_cot, sib_wide, sib_small, sib_vector)
    from_sibling = [
        copy(a, b, sib_send.at[i], sib_recv.at[i], sibling) for i, (a, b) in enumerate(zip(given, taken))
    ]

    parts = (parts_z, parts_x, parts_out)
    got = ((got_z1, got_x1, got_out1), (got_z2, got_x2, got_out2), (got_z3, got_x3, got_out3))
    sums = ((sum_z1, sum_x1, sum_out1), (sum_z2, sum_x2, sum_out2))
    outs = (out_z, out_x, out_out)

    def send_stage(stage, which, src):
        axis = REDUCE[which][stage]
        return [
            copy(
                src.at[to[axis]], got[stage][which].at[d],
                red_send.at[which, stage, d], red_recv.at[which, stage, d], to,
            )
            for d, to in enumerate(peers(at, axis))
        ]

    from_sibling[0].wait_recv()
    from_sibling[1].wait_recv()

    def tile_z(n, _):
        cols = pl.ds(pl.multiple_of(n * 256, 256), 256)
        res = mm(keep_n[:, 0:ROWS], d_gate[:, cols], NN) + mm(sib_n[:, 0:ROWS], sib_gate[:, cols], NN)
        for y in range(4):
            for k in range(2):
                parts_z[n // 2, y, (n % 2) * 2 + k] = res[128 * y : 128 * y + 128, 128 * k : 128 * k + 128].astype(BF16)
        return 0

    lax.fori_loop(0, 8, tile_z, 0)
    arriving = [send_stage(0, 0, parts_z), None, None]

    from_sibling[2].wait_recv()
    from_sibling[3].wait_recv()

    def tile_out(n, _):
        cols = pl.ds(pl.multiple_of(n * 256, 256), 256)
        res = mm(keep_m[...], cot[:, cols], NN) + mm(sib_m[...], sib_cot[:, cols], NN)
        for y in range(4):
            for half in range(2):
                for k in range(2):
                    row = 256 * y + 128 * half
                    parts_out[(n % 2) * 2 + k, half * 2 + n // 2, y] = res[row : row + 128, 128 * k : 128 * k + 128].astype(BF16)
        return 0

    lax.fori_loop(0, 4, tile_out, 0)
    arriving[2] = send_stage(0, 2, parts_out)

    for i in (4, 5, 6):
        from_sibling[i].wait_recv()

    def tile_x(n, _):
        cols = pl.ds(pl.multiple_of(n * 256, 256), 256)
        res = mm(keep_n[...], d_wide[:, cols], NN) + mm(sib_n[...], sib_wide[:, cols], NN)
        for y in range(4):
            for k in range(2):
                parts_x[y, (n % 2) * 2 + k, n // 2, 0:PIECE] = res[128 * y : 128 * y + 128, 128 * k : 128 * k + 128].astype(BF16)
        return 0

    lax.fori_loop(0, 8, tile_x, 0)
    res = mm(keep_n[...], d_small[...], NN) + mm(sib_n[...], sib_small[...], NN)
    total = (vector[...] + sib_vector[...]).astype(BF16)
    for y in range(4):
        for z in range(4):
            row = 128 * y + EXTRA * z
            for k in range(3):
                parts_x[y, z, k, PIECE:] = res[row : row + EXTRA, 128 * k : 128 * k + 128].astype(BF16)
            parts_x[y, z, 3, PIECE:] = total[EXTRA * z : EXTRA * z + EXTRA, :]
    arriving[1] = send_stage(0, 1, parts_x)

    order = (0, 2, 1)
    for stage in range(2):
        for which in order:
            for one in arriving[which]:
                one.wait_recv()
            src = parts[which] if stage == 0 else sums[0][which]
            dst, arrived = sums[stage][which], got[stage][which]
            mine = at[REDUCE[which][stage]]

            def add(i, _, src=src, dst=dst, arrived=arrived, mine=mine, stage=stage):
                if stage == 0:
                    for j in range(4):
                        value = src[mine, i, j].astype(F32)
                        for d in range(3):
                            value = value + arrived[d, i, j].astype(F32)
                        dst[i, j] = value.astype(BF16)
                else:
                    value = src[mine, i].astype(F32)
                    for d in range(3):
                        value = value + arrived[d, i].astype(F32)
                    dst[i] = value.astype(BF16)
                return 0

            lax.fori_loop(0, 4, add, 0)
            arriving[which] = send_stage(stage + 1, which, dst)

    def gather_stage(stage, which):
        first, second, third = GATHER[which]
        index = (at[third], at[second], at[first])[: 3 - stage]
        ref = outs[which].at[index]
        return [
            copy(ref, ref, all_send.at[which, stage, d], all_recv.at[which, stage, d], to)
            for d, to in enumerate(peers(at, (first, second, third)[stage]))
        ]

    for which in order:
        for one in arriving[which]:
            one.wait_recv()
        first, second, third = GATHER[which]
        value = sums[1][which][at[REDUCE[which][2]]].astype(F32)
        for d in range(3):
            value = value + got[2][which][d].astype(F32)
        outs[which][at[third], at[second], at[first]] = value.astype(BF16)
        arriving[which] = gather_stage(0, which)
    for stage in (1, 2):
        for which in order:
            for one in arriving[which]:
                one.wait_recv()
            arriving[which] = gather_stage(stage, which)
    for which in order:
        for one in arriving[which]:
            one.wait_recv()
    for one in started:
        one.wait_send()


def reduce_grads(keep_n, give_n, d_gate, d_wide, d_small, keep_m, give_m, cot, vector):
    vmem = pl.BlockSpec(memory_space=pltpu.VMEM)
    dims = {"x": 4, "z": 4, "l": 2}
    out_shape = [
        jax.ShapeDtypeStruct((*(dims[a] for a in reversed(GATHER[i])), PIECE_ROWS[i], 128), BF16) for i in range(3)
    ]
    like = [pltpu.VMEM(a.shape, a.dtype) for a in (give_n, d_gate, d_wide, d_small, give_m, cot, vector)]

    def bufs(*lead):
        return [pltpu.VMEM((*lead, PIECE_ROWS[i], 128), BF16) for i in range(3)]

    sems = [pltpu.SemaphoreType.DMA((7,))] * 2 + [pltpu.SemaphoreType.DMA((3, 3, 3))] * 4
    return pl.pallas_call(
        reduce_kernel,
        out_shape=out_shape,
        in_specs=[vmem] * 9,
        out_specs=[vmem] * 3,
        scratch_shapes=[
            *like, *bufs(4, 4, 4), *bufs(3, 4, 4), *bufs(4, 4), *bufs(3, 4), *bufs(4), *bufs(3), *sems,
        ],
        compiler_params=pltpu.CompilerParams(
            vmem_limit_bytes=VMEM_LIMIT, collective_id=1, has_side_effects=True
        ),
        cost_estimate=pl.CostEstimate(flops=int(4e9), bytes_accessed=int(4e7), transcendentals=0),
    )(keep_n, give_n, d_gate, d_wide, d_small, keep_m, give_m, cot, vector)


def swap(values):
    return lax.all_to_all(values, "seq", split_axis=0, concat_axis=0, tiled=True)


def gather_rows(shard):
    return lax.all_gather(shard, "wshard", axis=0, tiled=True)


def by_core(rows, core):
    cut = rows.reshape(2, 2, rows.shape[0] // 4, rows.shape[1])
    keep = lax.dynamic_index_in_dim(cut, core, 1, keepdims=False)
    give = lax.dynamic_index_in_dim(cut, 1 - core, 1, keepdims=False)
    return keep.reshape(-1, rows.shape[1]), give.reshape(-1, rows.shape[1])


def shards(
    layer_in, gain_in, w_z, w_x, w_bc, w_dt, conv_x_weight, conv_x_bias, conv_bc_weight, conv_bc_bias,
    dt_bias, a_log, d_skip, gain_norm, w_out, cotangent,
):
    width = layer_in.shape[2]
    chunks = lax.axis_size("seq")
    place = lax.axis_index("seq")
    tail = lax.ppermute(layer_in[:, TOK - (TAPS - 1) :, :], "seq", [(i, i + 1) for i in range(chunks - 1)])
    full_x = gather_rows(w_x)
    full_small = gather_rows(jnp.concatenate([w_bc, w_dt], axis=1))
    full_bc, full_dt = full_small[:, : 2 * STATE], full_small[:, 2 * STATE :]
    full_z = gather_rows(w_z)
    full_out = gather_rows(w_out)
    own = jnp.concatenate([conv_x_weight.reshape(-1), conv_x_bias, dt_bias, a_log, d_skip, jnp.zeros((61,), F32)])
    params = lax.all_gather(own, "seq", axis=0, tiled=False)
    taps_x = params[:, : TAPS * HEAD].reshape(HEADS, TAPS, HEAD).swapaxes(0, 1).reshape(TAPS, INNER)
    bias_x = params[:, TAPS * HEAD : (TAPS + 1) * HEAD].reshape(1, INNER)
    bias_dt, log_a, skip = (params[:, (TAPS + 1) * HEAD + i].reshape(1, HEADS) for i in range(3))
    bias_bc = conv_bc_bias.reshape(1, -1)

    hidden = layer_in.astype(F32).reshape(ROWS, width)
    upstream = cotangent.reshape(ROWS, width)
    halo = jnp.pad(tail, ((0, 0), (HALO - (TAPS - 1), 0), (0, 0))).reshape(SEQS * HALO, width).astype(F32)
    tokens = jnp.concatenate([hidden, halo], axis=0)
    inv = lax.rsqrt(jnp.mean(tokens * tokens, axis=-1, keepdims=True) + EPS)
    normed = (tokens * inv * gain_in[None, :]).astype(BF16)
    inv = inv[:ROWS]

    x_raw = mm(normed, full_x, NN).astype(BF16)
    bc_raw = mm(normed, full_bc, NN).astype(BF16)
    dt_raw = mm(normed, full_dt, NN).astype(BF16)
    xc, bcc, dt, r, u = front(x_raw, bc_raw, dt_raw, taps_x, bias_x, conv_bc_weight, bias_bc, bias_dt, log_a)
    decay = jnp.exp(swap(r[TOK - 1 :: TOK].T))
    u_all = swap(u)
    y_in = inside(xc, bcc, dt, r)
    gate = mm(normed[:ROWS], full_z, NN)
    d_mixed = mm(upstream, full_out, NT)
    start = swap(states(decay, u_all, False))
    mixed, d_y, d_gate, v, g_norm, row_dot = middle(
        y_in, xc, bcc, r, start, skip, gate, d_mixed, gain_norm.reshape(1, INNER)
    )
    v_all = swap(v)
    layer_out = (hidden + mm(mixed, full_out, NN)).astype(BF16).reshape(SEQS, TOK, width)
    d_stepped, d_bc_in = inside_back(xc, d_y, bcc, dt, r)
    d_normed_z = mm(d_gate, full_z, NT)
    end = swap(states(decay, v_all, True))
    d_x_raw, d_bc_raw, d_dt_raw, g_x, g_bc, g_heads = back(
        d_stepped, xc, d_y, x_raw, start, end, bcc, dt, r, bc_raw, dt_raw, d_bc_in, row_dot,
        taps_x, bias_x, conv_bc_weight, bias_bc, bias_dt, log_a, skip,
    )
    d_normed = mm(d_x_raw, full_x, NT) + mm(d_bc_raw, full_bc, NT) + mm(d_dt_raw, full_dt, NT)
    back_tail = d_normed[ROWS:].reshape(SEQS, HALO, width)[:, HALO - (TAPS - 1) :]
    back_tail = lax.ppermute(back_tail, "seq", [(i + 1, i) for i in range(chunks - 1)])
    d_normed = d_normed[:ROWS] + d_normed_z
    d_normed = d_normed + jnp.pad(back_tail, ((0, 0), (TOK - (TAPS - 1), 0), (0, 0))).reshape(ROWS, width)
    unit = hidden * inv
    g_in = jnp.sum(d_normed * unit, axis=0)
    pulled = d_normed * gain_in[None, :]
    d_hidden = inv * (pulled - unit * jnp.mean(pulled * unit, axis=-1, keepdims=True))
    input_grad = (upstream.astype(F32) + d_hidden).reshape(SEQS, TOK, width)

    pieces = (g_x[: TAPS + 1], g_bc[: TAPS + 1], g_heads[:3], g_in, g_norm)
    sizes = [p.size for p in pieces]
    vector = jnp.concatenate([*(p.reshape(-1) for p in pieces), jnp.zeros((PIECE * 128 - sum(sizes),), F32)])
    core = lax.axis_index("wshard") % 2
    keep_n, give_n = by_core(normed.T, core)
    keep_m, give_m = by_core(mixed.T, core)
    d_small = jnp.concatenate([d_bc_raw, d_dt_raw, jnp.zeros((ALL, SMALL - 2 * STATE - HEADS), BF16)], axis=1)
    sum_z, sum_x, sum_out = reduce_grads(
        keep_n, give_n, d_gate, d_x_raw, d_small, keep_m, give_m, upstream, vector.reshape(PIECE, 128)
    )
    grad_w_z = sum_z.transpose(2, 3, 0, 1, 4).reshape(2 * PIECE, INNER).astype(F32)
    grad_w_x = sum_x[:, :, :, :PIECE].transpose(2, 3, 1, 0, 4).reshape(2 * PIECE, INNER).astype(F32)
    extra = sum_x[:, :, :, PIECE:].transpose(1, 2, 0, 3, 4).reshape(4, 2 * PIECE, 128).astype(F32)
    grad_w_bc = jnp.concatenate([extra[0], extra[1]], axis=1)
    grad_w_dt = extra[2][:, :HEADS]
    total = extra[3][:PIECE].reshape(-1)[: sum(sizes)]
    grad_w_out = (
        sum_out.reshape(2, 4, 2, 2, PIECE, 128).transpose(0, 2, 4, 3, 1, 5).reshape(4 * PIECE, width).astype(F32)
    )
    ends = [sum(sizes[: i + 1]) for i in range(len(sizes) - 1)]
    s_x, s_bc, s_heads, s_in, s_norm = jnp.split(total, ends)
    s_x = lax.dynamic_slice(s_x.reshape(TAPS + 1, INNER), (0, place * HEAD), (TAPS + 1, HEAD))
    s_bc = s_bc.reshape(TAPS + 1, 2 * STATE)
    s_heads = lax.dynamic_slice(s_heads.reshape(3, HEADS), (0, place), (3, 1))
    return (
        layer_out, input_grad, s_in, grad_w_z, grad_w_x, grad_w_bc, grad_w_dt,
        s_x[:TAPS], s_x[TAPS], s_bc[:TAPS], s_bc[TAPS], s_heads[0], s_heads[1], s_heads[2], s_norm, grad_w_out,
    )


def solution(mesh):
    rows, heads = P("wshard", None), P("seq")
    tokens = P("wshard", "seq", None)
    return jax.shard_map(
        shards,
        mesh=mesh,
        in_specs=(
            tokens, P(), rows, rows, rows, rows, P(None, "seq"), heads, P(), P(), heads, heads, heads, P(), rows, tokens,
        ),
        out_specs=(
            tokens, tokens, P(), rows, rows, rows, rows, P(None, "seq"), heads, P(), P(), heads, heads, heads, P(), rows,
        ),
        check_vma=False,
    )
```

```python
import functools

import jax
import jax.numpy as jnp
from jax import lax
from jax.experimental import pallas as pl
from jax.experimental.pallas import tpu as pltpu
from jax.sharding import PartitionSpec as P

F32 = jnp.float32
BF16 = jnp.bfloat16
EPS = 1e-05
HIGHEST = lax.Precision.HIGHEST
HEADS = 32
HEAD = 64
STATE = 128
TOK = 128
SEQS = 2
ROWS = SEQS * TOK
HALO = 8
ALL = ROWS + SEQS * HALO
PAIRS = HEADS // 2
INNER = HEADS * HEAD
TAPS = 4


def mm(a, b, dims, precision=None):
    return lax.dot_general(a, b, ((dims[0], dims[1]), ((), ())), precision=precision, preferred_element_type=F32)


NN = ((1,), (0,))
NT = ((1,), (1,))
TN = ((0,), (0,))


def iota(shape, dim):
    return lax.broadcasted_iota(jnp.int32, shape, dim)


def pair_matrix(pair):
    upper = (iota((HEADS, 128), 1) >= HEAD).astype(jnp.int32)
    return (iota((HEADS, 128), 0) == 2 * pair + upper).astype(F32)


def pair_rows(pair):
    return (iota((8, HEADS), 1) == 2 * pair + iota((8, HEADS), 0)).astype(F32)


def head_sums(values, ex):
    high = values.astype(BF16)
    low = (values - high.astype(F32)).astype(BF16)
    ex = ex.astype(BF16)
    return mm(jnp.concatenate([high, low], axis=1), jnp.concatenate([ex, ex], axis=1), NT)


def lane_sums(values):
    high = values.astype(BF16)
    low = (values - high.astype(F32)).astype(BF16)
    return mm(jnp.ones((8, 256), BF16), jnp.concatenate([high, low], axis=1), NT)[0:1, :]


def causal_mask():
    return iota((TOK, TOK), 0) >= iota((TOK, TOK), 1)


def shifted(padded, k):
    back = TAPS - 1 - k
    if back:
        padded = pltpu.roll(padded, back, 0)
    return padded[HALO:, :]


def padded_of(rows, b):
    return jnp.concatenate(
        [rows[ROWS + HALO * b : ROWS + HALO * (b + 1), :], rows[TOK * b : TOK * (b + 1), :]], axis=0
    )


def conv_pre(padded, taps, bias):
    total = bias
    for k in range(TAPS):
        total = total + taps[k : k + 1, :] * shifted(padded, k)
    return total


def conv_back(padded, taps, bias, grad):
    pre = conv_pre(padded, taps, bias)
    sig = jax.nn.sigmoid(pre)
    d_pre = grad * (sig * (1.0 + pre * (1.0 - sig)))
    low = jnp.concatenate([jnp.zeros((HALO, d_pre.shape[1]), F32), d_pre], axis=0)
    d_pad = taps[TAPS - 1 : TAPS, :] * low
    for k in range(TAPS - 1):
        d_pad = d_pad + taps[k : k + 1, :] * pltpu.roll(low, HALO + TOK - (TAPS - 1 - k), 0)
    d_taps = [jnp.sum(d_pre * shifted(padded, k), axis=0, keepdims=True) for k in range(TAPS)]
    return d_pad, d_taps, jnp.sum(d_pre, axis=0, keepdims=True)


def block_diagonal(pair_values):
    first = iota(pair_values.shape, 1) < HEAD
    zero = jnp.zeros_like(pair_values)
    return jnp.concatenate(
        [jnp.where(first, pair_values, zero), jnp.where(first, zero, pair_values)], axis=0
    )


def decay_pair(r_lanes, r_rows):
    mask = causal_mask()
    out = []
    for q in range(2):
        spread = r_lanes[:, HEAD * q : HEAD * q + 1] - r_rows[q : q + 1, :]
        out.append(jnp.exp(jnp.where(mask, spread, -1e30)))
    return out


def front_kernel(x_raw, bc_raw, dt_raw, taps_x, bias_x, taps_bc, bias_bc, dt_bias, a_log, xc, bcc, dt, r, u, dt_wide, r_wide, r_rows):
    pair = pl.program_id(0)

    @pl.when(pair == 0)
    def _():
        raw = bc_raw[...].astype(F32)
        steps = dt_raw[0:ROWS, :].astype(F32) + dt_bias[...]
        dt[...] = jax.nn.softplus(steps)
        tri = causal_mask().astype(F32)
        decay = dt[...] * (-jnp.exp(a_log[...]))
        for b in range(SEQS):
            pre = conv_pre(padded_of(raw, b), taps_bc[...], bias_bc[...])
            bcc[TOK * b : TOK * (b + 1), :] = (pre * jax.nn.sigmoid(pre)).astype(BF16)
            r[TOK * b : TOK * (b + 1), :] = mm(tri, decay[TOK * b : TOK * (b + 1), :], NN, HIGHEST)

    raw = x_raw[...].astype(F32)
    ex = pair_matrix(pair)
    both = mm(jnp.concatenate([r[...], dt[...]], axis=0), ex, NN, HIGHEST)
    r_wide[...] = both[0:ROWS, :]
    dt_wide[...] = both[ROWS:, :]
    r_rows[0] = mm(pair_rows(pair), r[...], NT, HIGHEST)
    for b in range(SEQS):
        span = slice(TOK * b, TOK * (b + 1))
        pre = conv_pre(padded_of(raw, b), taps_x[...], bias_x[...])
        low = (pre * jax.nn.sigmoid(pre)).astype(BF16)
        xc[span, :] = low
        r_lanes = both[span, :]
        dt_lanes = both[ROWS + TOK * b : ROWS + TOK * (b + 1), :]
        to_end = jnp.exp(r_lanes[TOK - 1 : TOK, :] - r_lanes)
        scaled = (to_end * (dt_lanes * low.astype(F32))).astype(BF16)
        state = mm(scaled, bcc[span, 0:STATE], TN).astype(BF16)
        u[0, b] = state[0:HEAD, :]
        u[1, b] = state[HEAD:, :]


def whole(shape):
    return pl.BlockSpec(shape, lambda *_: (0,) * len(shape))


def lanes(rows):
    return pl.BlockSpec((rows, 128), lambda j: (0, j))


STATES = pl.BlockSpec((2, SEQS, HEAD, STATE), lambda j: (j, 0, 0, 0))
PAIR_ROWS = pl.BlockSpec((1, 8, ROWS), lambda j: (j, 0, 0))
STATES_SHAPE = (HEADS, SEQS, HEAD, STATE)
VMEM_LIMIT = 48 * 1024 * 1024


def call(kernel, outs, out_specs, in_specs, grid=(PAIRS,), scratch=(), cost=None):
    return pl.pallas_call(
        kernel,
        grid=grid,
        out_shape=[jax.ShapeDtypeStruct(s, d) for s, d in outs],
        in_specs=in_specs,
        out_specs=out_specs,
        scratch_shapes=scratch,
        compiler_params=pltpu.CompilerParams(
            vmem_limit_bytes=VMEM_LIMIT, dimension_semantics=("arbitrary",) * len(grid)
        ),
        cost_estimate=cost or pl.CostEstimate(flops=int(1e9), bytes_accessed=int(1e7), transcendentals=0),
    )


def front(x_raw, bc_raw, dt_raw, taps_x, bias_x, taps_bc, bias_bc, dt_bias, a_log):
    return call(
        front_kernel,
        [((ROWS, INNER), BF16), ((ROWS, 2 * STATE), BF16), ((ROWS, HEADS), F32), ((ROWS, HEADS), F32), (STATES_SHAPE, BF16), ((ROWS, INNER), F32), ((ROWS, INNER), F32), ((PAIRS, 8, ROWS), F32)],
        [lanes(ROWS), whole((ROWS, 2 * STATE)), whole((ROWS, HEADS)), whole((ROWS, HEADS)), STATES, lanes(ROWS), lanes(ROWS), PAIR_ROWS],
        [
            lanes(ALL), whole((ALL, 2 * STATE)), whole((ALL, HEADS)), lanes(TAPS), lanes(1),
            whole((TAPS, 2 * STATE)), whole((1, 2 * STATE)), whole((1, HEADS)), whole((1, HEADS)),
        ],
    )(x_raw, bc_raw, dt_raw, taps_x, bias_x, taps_bc, bias_bc, dt_bias, a_log)


def states_kernel(reverse, decay, own, before):
    chunks = own.shape[0]

    def step(i, carry):
        c = chunks - 1 - i if reverse else i
        after = []
        for b in range(SEQS):
            before[c, b] = carry[b].astype(BF16)
            after.append(decay[c, b] * carry[b] + own[c, b].astype(F32))
        return tuple(after)

    lax.fori_loop(0, chunks, step, tuple(jnp.zeros((HEAD, STATE), F32) for _ in range(SEQS)))


def states(decay, own, reverse):
    return pl.pallas_call(
        functools.partial(states_kernel, reverse),
        out_shape=jax.ShapeDtypeStruct(own.shape, BF16),
        in_specs=[pl.BlockSpec(memory_space=pltpu.SMEM), pl.BlockSpec(memory_space=pltpu.VMEM)],
        out_specs=pl.BlockSpec(memory_space=pltpu.VMEM),
        compiler_params=pltpu.CompilerParams(vmem_limit_bytes=VMEM_LIMIT),
        cost_estimate=pl.CostEstimate(flops=int(1e6), bytes_accessed=int(2e6), transcendentals=0),
    )(decay, own)


def inside_kernel(xc, bcc, dt_wide, r_wide, r_rows, y, scores):
    pair = pl.program_id(0)

    @pl.when(pair == 0)
    def _():
        for b in range(SEQS):
            span = slice(TOK * b, TOK * (b + 1))
            scores[b] = mm(bcc[span, STATE:], bcc[span, 0:STATE], NT)

    for b in range(SEQS):
        span = slice(TOK * b, TOK * (b + 1))
        dt_lanes = dt_wide[span, :]
        first, second = decay_pair(r_wide[span, :], r_rows[0, :, span])
        both = jnp.concatenate([scores[b] * first, scores[b] * second], axis=1).astype(BF16)
        stepped = (dt_lanes * xc[span, :].astype(F32)).astype(BF16)
        y[span, :] = mm(both, block_diagonal(stepped), NN)


def inside(xc, bcc, dt_wide, r_wide, r_rows):
    return call(
        inside_kernel,
        [((ROWS, INNER), F32)],
        [lanes(ROWS)],
        [lanes(ROWS), whole((ROWS, 2 * STATE)), lanes(ROWS), lanes(ROWS), PAIR_ROWS],
        scratch=[pltpu.VMEM((SEQS, TOK, TOK), F32)],
    )(xc, bcc, dt_wide, r_wide, r_rows)[0]


def middle_kernel(
    y_in, xc, bcc, r, start, d_skip, gate, d_mixed, gain,
    mixed, d_y, d_gate, own, d_gain, row_dot,
    y_all, square, cross, scale, slope,
):
    phase = pl.program_id(0)
    pair = pl.program_id(1)
    ex = pair_matrix(pair)
    skip = d_skip[...]
    z = gate[...]
    sig = jax.nn.sigmoid(z)
    pulled = d_mixed[...] * gain[...]

    @pl.when(phase == 0)
    def _():
        @pl.when(pair == 0)
        def _():
            square[...] = jnp.zeros_like(square)
            cross[...] = jnp.zeros_like(cross)

        for b in range(SEQS):
            span = slice(TOK * b, TOK * (b + 1))
            before = jnp.concatenate([start[0, b], start[1, b]], axis=0)
            grown = jnp.exp(r[span, :])
            y_all[pair, span, :] = y_in[span, :] + grown * mm(bcc[span, STATE:], before, NT)
        y = (y_all[pair] + skip * xc[...].astype(F32)).astype(BF16).astype(F32)
        gated = y * (z * sig)
        square[...] += gated * gated
        cross[...] += pulled * gated

    @pl.when(phase == 1)
    def _():
        @pl.when(pair == 0)
        def _():
            inv = lax.rsqrt(jnp.sum(square[...], axis=1, keepdims=True) * (1.0 / INNER) + EPS)
            mean = jnp.sum(cross[...], axis=1, keepdims=True) * (1.0 / INNER)
            scale[...] = jnp.broadcast_to(inv, scale.shape)
            slope[...] = jnp.broadcast_to(inv * inv * inv * mean, slope.shape)
            row_dot[...] = jnp.zeros_like(row_dot)

        y = (y_all[pair] + skip * xc[...].astype(F32)).astype(BF16).astype(F32)
        silu = z * sig
        gated = y * silu
        unit = gated * scale[...]
        mixed[...] = (unit * gain[...]).astype(BF16)
        d_gain[...] = jnp.sum(d_mixed[...] * unit, axis=0, keepdims=True)
        d_gated = scale[...] * pulled - gated * slope[...]
        low = (d_gated * silu).astype(BF16)
        d_y[...] = low
        d_gate[...] = (d_gated * y * (sig * (1.0 + z * (1.0 - sig)))).astype(BF16)
        row_dot[...] += head_sums(low.astype(F32) * y_all[pair], ex)
        for b in range(SEQS):
            span = slice(TOK * b, TOK * (b + 1))
            grown = jnp.exp(r[span, :])
            state = mm((grown * low[span, :].astype(F32)).astype(BF16), bcc[span, STATE:], TN).astype(BF16)
            own[0, b] = state[0:HEAD, :]
            own[1, b] = state[HEAD:, :]


def middle(y_in, xc, bcc, r, start, d_skip, gate, d_mixed, gain):
    def cols(rows):
        return pl.BlockSpec((rows, 128), lambda p, j: (0, j))

    def first(rows):
        return pl.BlockSpec((rows, 128), lambda p, j: (0, jnp.where(p == 0, j, PAIRS - 1)))

    def second(rows):
        return pl.BlockSpec((rows, 128), lambda p, j: (0, jnp.where(p == 1, j, 0)))

    states_in = pl.BlockSpec((2, SEQS, HEAD, STATE), lambda p, j: (jnp.where(p == 0, j, PAIRS - 1), 0, 0, 0))
    states_out = pl.BlockSpec((2, SEQS, HEAD, STATE), lambda p, j: (jnp.where(p == 1, j, 0), 0, 0, 0))
    return call(
        middle_kernel,
        [((ROWS, INNER), BF16), ((ROWS, INNER), BF16), ((ROWS, INNER), BF16), (STATES_SHAPE, BF16), ((1, INNER), F32), ((ROWS, HEADS), F32)],
        [second(ROWS), second(ROWS), second(ROWS), states_out, second(1), whole((ROWS, HEADS))],
        [first(ROWS), cols(ROWS), whole((ROWS, 2 * STATE)), cols(ROWS), states_in, cols(1), cols(ROWS), cols(ROWS), cols(1)],
        grid=(2, PAIRS),
        scratch=[pltpu.VMEM((PAIRS, ROWS, 128), F32)] + [pltpu.VMEM((ROWS, 128), F32)] * 4,
    )(y_in, xc, bcc, r, start, d_skip, gate, d_mixed, gain)


def inside_back_kernel(xc, d_y, bcc, dt_wide, r_wide, r_rows, d_stepped, d_bc, scores, d_scores):
    pair = pl.program_id(0)

    @pl.when(pair == 0)
    def _():
        d_scores[...] = jnp.zeros_like(d_scores)
        for b in range(SEQS):
            span = slice(TOK * b, TOK * (b + 1))
            scores[b] = mm(bcc[span, STATE:], bcc[span, 0:STATE], NT)

    for b in range(SEQS):
        span = slice(TOK * b, TOK * (b + 1))
        dt_lanes = dt_wide[span, :]
        first, second = decay_pair(r_wide[span, :], r_rows[0, :, span])
        both = jnp.concatenate([scores[b] * first, scores[b] * second], axis=0).astype(BF16)
        stepped = (dt_lanes * xc[span, :].astype(F32)).astype(BF16)
        wide = block_diagonal(d_y[span, :])
        d_stepped[span, :] = mm(both, wide, TN)
        d_both = mm(wide, stepped, NT)
        d_scores[b] += d_both[0:TOK, :] * first + d_both[TOK:, :] * second

    @pl.when(pair == PAIRS - 1)
    def _():
        for b in range(SEQS):
            span = slice(TOK * b, TOK * (b + 1))
            low = d_scores[b].astype(BF16)
            d_bc[span, 0:STATE] = mm(low, bcc[span, STATE:], TN)
            d_bc[span, STATE:] = mm(low, bcc[span, 0:STATE], NN)


def inside_back(xc, d_y, bcc, dt_wide, r_wide, r_rows):
    return call(
        inside_back_kernel,
        [((ROWS, INNER), F32), ((ROWS, 2 * STATE), F32)],
        [lanes(ROWS), whole((ROWS, 2 * STATE))],
        [lanes(ROWS), lanes(ROWS), whole((ROWS, 2 * STATE)), lanes(ROWS), lanes(ROWS), PAIR_ROWS],
        scratch=[pltpu.VMEM((SEQS, TOK, TOK), F32)] * 2,
    )(xc, d_y, bcc, dt_wide, r_wide, r_rows)


def back_kernel(
    d_stepped, xc, d_y, x_raw, start, end, bcc, dt, dt_wide, r_wide, bc_raw, dt_raw, d_bc_in, row_dot,
    taps_x, bias_x, taps_bc, bias_bc, dt_bias, a_log, d_skip,
    d_x_raw, d_bc_raw, d_dt_raw, g_x, g_bc, g_heads,
    d_bc, sums,
):
    pair = pl.program_id(0)

    @pl.when(pair == 0)
    def _():
        d_bc[...] = d_bc_in[...]
        sums[...] = jnp.zeros_like(sums)

    ex = pair_matrix(pair)
    skip = d_skip[...]
    raw = x_raw[...].astype(F32)
    halos, grads = [], None
    d_steps, cols, end_rows = [], [], []
    skip_sum = jnp.zeros((1, 128), F32)
    for b in range(SEQS):
        span = slice(TOK * b, TOK * (b + 1))
        r_lanes = r_wide[span, :]
        dt_lanes = dt_wide[span, :]
        last = r_lanes[TOK - 1 : TOK, :]
        grown = jnp.exp(r_lanes)
        to_end = jnp.exp(last - r_lanes)
        before = jnp.concatenate([start[0, b], start[1, b]], axis=0)
        after = jnp.concatenate([end[0, b], end[1, b]], axis=0)
        x = xc[span, :].astype(F32)
        dy = d_y[span, :].astype(F32)
        stepped = (dt_lanes * x).astype(BF16).astype(F32)
        carried = to_end * mm(bcc[span, 0:STATE], after, NT)
        d_step = d_stepped[span, :] + carried
        cols.append(stepped * d_step)
        d_x = dt_lanes * d_step + skip * dy
        d_steps.append(x * d_step)
        inner = lane_sums(before.astype(F32) * after.astype(F32))
        end_rows.append(jnp.sum(stepped * carried, axis=0, keepdims=True) + jnp.exp(last) * inner)
        d_bc[span, STATE:] += mm((grown * dy).astype(BF16), before, NN)
        d_bc[span, 0:STATE] += mm((to_end * stepped).astype(BF16), after, NN)
        skip_sum = skip_sum + jnp.sum(dy * x, axis=0, keepdims=True)
        d_pad, d_taps, d_bias = conv_back(padded_of(raw, b), taps_x[...], bias_x[...], d_x)
        d_x_raw[span, :] = d_pad[HALO:, :].astype(BF16)
        halos.append(d_pad[0:HALO, :])
        parts = [*d_taps, d_bias]
        grads = parts if grads is None else [g + p for g, p in zip(grads, parts)]
    d_x_raw[ROWS:, :] = jnp.concatenate(halos, axis=0).astype(BF16)
    g_x[...] = jnp.concatenate([*grads, jnp.zeros((8 - TAPS - 1, 128), F32)], axis=0)
    few = jnp.concatenate([*end_rows, skip_sum, jnp.zeros((5, 128), F32)], axis=0)
    sums[...] += head_sums(jnp.concatenate([*d_steps, *cols, few], axis=0), ex)

    @pl.when(pair == PAIRS - 1)
    def _():
        raw = bc_raw[...].astype(F32)
        halos, grads = [], None
        for b in range(SEQS):
            span = slice(TOK * b, TOK * (b + 1))
            d_pad, d_taps, d_bias = conv_back(padded_of(raw, b), taps_bc[...], bias_bc[...], d_bc[span, :])
            d_bc_raw[span, :] = d_pad[HALO:, :].astype(BF16)
            halos.append(d_pad[0:HALO, :])
            parts = [*d_taps, d_bias]
            grads = parts if grads is None else [g + p for g, p in zip(grads, parts)]
        d_bc_raw[ROWS:, :] = jnp.concatenate(halos, axis=0).astype(BF16)
        g_bc[...] = jnp.concatenate([*grads, jnp.zeros((8 - TAPS - 1, 2 * STATE), F32)], axis=0)
        rate = -jnp.exp(a_log[...])
        tri = causal_mask().astype(F32)
        is_last = iota((TOK, HEADS), 0) == TOK - 1
        bias_sum = jnp.zeros((1, HEADS), F32)
        log_sum = jnp.zeros((1, HEADS), F32)
        for b in range(SEQS):
            span = slice(TOK * b, TOK * (b + 1))
            step = dt[span, :]
            d_dt = sums[span, :]
            d_r = row_dot[span, :] - sums[ROWS + TOK * b : ROWS + TOK * (b + 1), :]
            d_r = d_r + jnp.where(is_last, sums[2 * ROWS + b : 2 * ROWS + b + 1, :], 0.0)
            d_log = mm(tri, d_r, TN, HIGHEST)
            d_pre = (d_dt + rate * d_log) * jax.nn.sigmoid(dt_raw[span, :].astype(F32) + dt_bias[...])
            d_dt_raw[span, :] = d_pre.astype(BF16)
            bias_sum = bias_sum + jnp.sum(d_pre, axis=0, keepdims=True)
            log_sum = log_sum + jnp.sum(d_log * step, axis=0, keepdims=True) * rate
        d_dt_raw[ROWS:, :] = jnp.zeros((ALL - ROWS, HEADS), BF16)
        g_heads[...] = jnp.concatenate([bias_sum, log_sum, sums[2 * ROWS + 2 : 2 * ROWS + 3, :], jnp.zeros((5, HEADS), F32)], axis=0)


def back(d_stepped, xc, d_y, x_raw, start, end, bcc, dt, dt_wide, r_wide, bc_raw, dt_raw, d_bc_in, row_dot, taps_x, bias_x, taps_bc, bias_bc, dt_bias, a_log, d_skip):
    return call(
        back_kernel,
        [((ALL, INNER), BF16), ((ALL, 2 * STATE), BF16), ((ALL, HEADS), BF16), ((8, INNER), F32), ((8, 2 * STATE), F32), ((8, HEADS), F32)],
        [lanes(ALL), whole((ALL, 2 * STATE)), whole((ALL, HEADS)), lanes(8), whole((8, 2 * STATE)), whole((8, HEADS))],
        [
            lanes(ROWS), lanes(ROWS), lanes(ROWS), lanes(ALL), STATES, STATES,
            whole((ROWS, 2 * STATE)), whole((ROWS, HEADS)), lanes(ROWS), lanes(ROWS), whole((ALL, 2 * STATE)),
            whole((ALL, HEADS)), whole((ROWS, 2 * STATE)), whole((ROWS, HEADS)),
            lanes(TAPS), lanes(1), whole((TAPS, 2 * STATE)), whole((1, 2 * STATE)),
            whole((1, HEADS)), whole((1, HEADS)), lanes(1),
        ],
        scratch=[
            pltpu.VMEM((ROWS, 2 * STATE), F32), pltpu.VMEM((2 * ROWS + 8, HEADS), F32),
        ],
    )(d_stepped, xc, d_y, x_raw, start, end, bcc, dt, dt_wide, r_wide, bc_raw, dt_raw, d_bc_in, row_dot, taps_x, bias_x, taps_bc, bias_bc, dt_bias, a_log, d_skip)


REDUCE = (("x", "y", "z"), ("y", "z", "x"), ("z", "x", "y"))
GATHER = (("l", "z", "x"), ("l", "x", "z"), ("x", "z", "l"))
PIECE = 128
EXTRA = 32
PIECE_ROWS = (PIECE, PIECE + EXTRA, PIECE)
SMALL = 3 * 128


def position():
    seq, shard = lax.axis_index("seq"), lax.axis_index("wshard")
    high, core = shard // 2, shard % 2
    low = seq % 2
    return {"z": seq // 8, "x": (seq // 2) % 4, "y": high * 2 + low, "l": low, "core": core}


def device(at):
    return {"seq": at["z"] * 8 + at["x"] * 2 + at["y"] % 2, "wshard": (at["y"] // 2) * 2 + at["core"]}


def moved(at, axis, to):
    new = dict(at)
    if axis == "l":
        new["y"] = (at["y"] // 2) * 2 + to
        new["l"] = to
    else:
        new[axis] = to
        if axis == "y":
            new["l"] = to % 2
    return new


def peers(at, axis):
    size = 2 if axis in ("l", "core") else 4
    return [moved(at, axis, lax.rem(at[axis] + d, size)) for d in range(1, size)]


def greet(everyone):
    barrier = pltpu.get_barrier_semaphore()
    for other in everyone:
        pl.semaphore_signal(barrier, inc=1, device_id=device(other), device_id_type=pl.DeviceIdType.MESH)
    pl.semaphore_wait(barrier, len(everyone))


def reduce_kernel(
    normed, d_gate, d_wide, d_small, mixed, cot, vector,
    out_z, out_x, out_out,
    keep_n, keep_m, next_n, next_m, sib_n, sib_gate, sib_wide, sib_small, sib_m, sib_cot, sib_vector,
    parts_z, parts_x, parts_out,
    got_z1, got_x1, got_out1, sum_z1, sum_x1, sum_out1,
    got_z2, got_x2, got_out2, sum_z2, sum_x2, sum_out2,
    got_z3, got_x3, got_out3,
    sib_send, sib_recv, red_send, red_recv, all_send, all_recv,
):
    at = position()
    sibling = peers(at, "core")[0]
    everyone = [sibling] + [p for axis in ("x", "y", "z") for p in peers(at, axis)]
    greet(everyone)
    started = []

    def copy(src, dst, send, recv, to):
        one = pltpu.make_async_remote_copy(
            src_ref=src, dst_ref=dst, send_sem=send, recv_sem=recv,
            device_id=device(to), device_id_type=pl.DeviceIdType.MESH,
        )
        one.start()
        started.append(one)
        return one

    def columns(ref, high, core, size):
        return ref.at[:, pl.ds(pl.multiple_of((2 * high + core) * size, size), size)]

    def transposed(ref, high, core, size):
        return ref[:, pl.ds(pl.multiple_of((2 * high + core) * size, size), size)].astype(F32).T.astype(BF16)

    core = at["core"]
    pairs = [(columns(normed, h, 1 - core, 256), sib_n.at[h]) for h in range(2)] + [(d_gate, sib_gate)]
    pairs += [(columns(mixed, h, 1 - core, 512), sib_m.at[h]) for h in range(2)]
    pairs += [(cot, sib_cot), (d_wide, sib_wide), (d_small, sib_small), (vector, sib_vector)]
    from_sibling = [copy(a, b, sib_send.at[i], sib_recv.at[i], sibling) for i, (a, b) in enumerate(pairs)]
    for h in range(2):
        keep_n[256 * h : 256 * (h + 1), :] = transposed(normed, h, core, 256)
    for h in range(2):
        keep_m[512 * h : 512 * (h + 1), :] = transposed(mixed, h, core, 512)

    parts = (parts_z, parts_x, parts_out)
    got = ((got_z1, got_x1, got_out1), (got_z2, got_x2, got_out2), (got_z3, got_x3, got_out3))
    sums = ((sum_z1, sum_x1, sum_out1), (sum_z2, sum_x2, sum_out2))
    outs = (out_z, out_x, out_out)

    def send_stage(stage, which, src):
        axis = REDUCE[which][stage]
        return [
            copy(
                src.at[to[axis]], got[stage][which].at[d],
                red_send.at[which, stage, d], red_recv.at[which, stage, d], to,
            )
            for d, to in enumerate(peers(at, axis))
        ]

    for i in (0, 1, 2):
        from_sibling[i].wait_recv()
    for h in range(2):
        next_n[256 * h : 256 * (h + 1), :] = sib_n[h].astype(F32).T.astype(BF16)

    def tile_z(n, _):
        cols = pl.ds(pl.multiple_of(n * 256, 256), 256)
        res = mm(keep_n[:, 0:ROWS], d_gate[:, cols], NN) + mm(next_n[:, 0:ROWS], sib_gate[:, cols], NN)
        for y in range(4):
            for k in range(2):
                parts_z[n // 2, y, (n % 2) * 2 + k] = res[128 * y : 128 * y + 128, 128 * k : 128 * k + 128].astype(BF16)
        return 0

    lax.fori_loop(0, 8, tile_z, 0)
    arriving = [send_stage(0, 0, parts_z), None, None]

    for i in (3, 4, 5):
        from_sibling[i].wait_recv()
    for h in range(2):
        next_m[512 * h : 512 * (h + 1), :] = sib_m[h].astype(F32).T.astype(BF16)

    def tile_out(n, _):
        cols = pl.ds(pl.multiple_of(n * 256, 256), 256)
        res = mm(keep_m[...], cot[:, cols], NN) + mm(next_m[...], sib_cot[:, cols], NN)
        for y in range(4):
            for half in range(2):
                for k in range(2):
                    row = 256 * y + 128 * half
                    parts_out[(n % 2) * 2 + k, half * 2 + n // 2, y] = res[row : row + 128, 128 * k : 128 * k + 128].astype(BF16)
        return 0

    lax.fori_loop(0, 4, tile_out, 0)
    arriving[2] = send_stage(0, 2, parts_out)

    for i in (6, 7, 8):
        from_sibling[i].wait_recv()

    def tile_x(n, _):
        cols = pl.ds(pl.multiple_of(n * 256, 256), 256)
        res = mm(keep_n[...], d_wide[:, cols], NN) + mm(next_n[...], sib_wide[:, cols], NN)
        for y in range(4):
            for k in range(2):
                parts_x[y, (n % 2) * 2 + k, n // 2, 0:PIECE] = res[128 * y : 128 * y + 128, 128 * k : 128 * k + 128].astype(BF16)
        return 0

    lax.fori_loop(0, 8, tile_x, 0)
    res = mm(keep_n[...], d_small[...], NN) + mm(next_n[...], sib_small[...], NN)
    total = (vector[...] + sib_vector[...]).astype(BF16)
    for y in range(4):
        for z in range(4):
            row = 128 * y + EXTRA * z
            for k in range(3):
                parts_x[y, z, k, PIECE:] = res[row : row + EXTRA, 128 * k : 128 * k + 128].astype(BF16)
            parts_x[y, z, 3, PIECE:] = total[EXTRA * z : EXTRA * z + EXTRA, :]
    arriving[1] = send_stage(0, 1, parts_x)

    order = (0, 2, 1)
    for stage in range(2):
        for which in order:
            for one in arriving[which]:
                one.wait_recv()
            src = parts[which] if stage == 0 else sums[0][which]
            dst, arrived = sums[stage][which], got[stage][which]
            mine = at[REDUCE[which][stage]]

            def add(i, _, src=src, dst=dst, arrived=arrived, mine=mine, stage=stage):
                if stage == 0:
                    for j in range(4):
                        value = src[mine, i, j].astype(F32)
                        for d in range(3):
                            value = value + arrived[d, i, j].astype(F32)
                        dst[i, j] = value.astype(BF16)
                else:
                    value = src[mine, i].astype(F32)
                    for d in range(3):
                        value = value + arrived[d, i].astype(F32)
                    dst[i] = value.astype(BF16)
                return 0

            lax.fori_loop(0, 4, add, 0)
            arriving[which] = send_stage(stage + 1, which, dst)

    def gather_stage(stage, which):
        first, second, third = GATHER[which]
        index = (at[third], at[second], at[first])[: 3 - stage]
        ref = outs[which].at[index]
        return [
            copy(ref, ref, all_send.at[which, stage, d], all_recv.at[which, stage, d], to)
            for d, to in enumerate(peers(at, (first, second, third)[stage]))
        ]

    for which in order:
        for one in arriving[which]:
            one.wait_recv()
        first, second, third = GATHER[which]
        value = sums[1][which][at[REDUCE[which][2]]].astype(F32)
        for d in range(3):
            value = value + got[2][which][d].astype(F32)
        outs[which][at[third], at[second], at[first]] = value.astype(BF16)
        arriving[which] = gather_stage(0, which)
    for stage in (1, 2):
        for which in order:
            for one in arriving[which]:
                one.wait_recv()
            arriving[which] = gather_stage(stage, which)
    for which in order:
        for one in arriving[which]:
            one.wait_recv()
    for one in started:
        one.wait_send()


def reduce_grads(normed, d_gate, d_wide, d_small, mixed, cot, vector):
    vmem = pl.BlockSpec(memory_space=pltpu.VMEM)
    dims = {"x": 4, "z": 4, "l": 2}
    out_shape = [
        jax.ShapeDtypeStruct((*(dims[a] for a in reversed(GATHER[i])), PIECE_ROWS[i], 128), BF16) for i in range(3)
    ]
    turned = [pltpu.VMEM((512, ALL), BF16), pltpu.VMEM((1024, ROWS), BF16)] * 2
    like = [pltpu.VMEM((2, ALL, 256), BF16)] + [pltpu.VMEM(a.shape, a.dtype) for a in (d_gate, d_wide, d_small)]
    like += [pltpu.VMEM((2, ROWS, 512), BF16)] + [pltpu.VMEM(a.shape, a.dtype) for a in (cot, vector)]

    def bufs(*lead):
        return [pltpu.VMEM((*lead, PIECE_ROWS[i], 128), BF16) for i in range(3)]

    sems = [pltpu.SemaphoreType.DMA((9,))] * 2 + [pltpu.SemaphoreType.DMA((3, 3, 3))] * 4
    return pl.pallas_call(
        reduce_kernel,
        out_shape=out_shape,
        in_specs=[vmem] * 7,
        out_specs=[vmem] * 3,
        scratch_shapes=[
            *turned, *like, *bufs(4, 4, 4), *bufs(3, 4, 4), *bufs(4, 4), *bufs(3, 4), *bufs(4), *bufs(3), *sems,
        ],
        compiler_params=pltpu.CompilerParams(
            vmem_limit_bytes=VMEM_LIMIT, collective_id=1, has_side_effects=True
        ),
        cost_estimate=pl.CostEstimate(flops=int(4e9), bytes_accessed=int(4e7), transcendentals=0),
    )(normed, d_gate, d_wide, d_small, mixed, cot, vector)


def gather_kernel(
    w_x, w_small, own, full_x, full_small, params, send, recv, here, own_send, own_recv,
):
    at = position()
    sibling = peers(at, "core")[0]
    partner = moved(at, "y", 3 - at["y"])
    everyone = [sibling, partner] + [p for axis in ("x", "z", "l") for p in peers(at, axis)]
    greet(everyone)
    started = []

    def copy(src, dst, which, to, sems=(send, recv)):
        one = pltpu.make_async_remote_copy(
            src_ref=src, dst_ref=dst, send_sem=sems[0].at[which], recv_sem=sems[1].at[which],
            device_id=device(to), device_id_type=pl.DeviceIdType.MESH,
        )
        one.start()
        started.append(one)
        return one

    high = at["y"] // 2
    mine, opposite = high * 2 + at["core"], (1 - high) * 2 + at["core"]
    half = INNER // 2
    flows = ((full_x, 0, half, "x", "z"), (full_x, half, half, "z", "x"), (full_small, 0, SMALL, "x", "z"))

    def view(ref, shard, row, count, first, size):
        row = pl.multiple_of(row, 16)
        if shard is None:
            return ref.at[pl.ds(row, count), first : first + size]
        return ref.at[shard, pl.ds(row, count), first : first + size]

    arriving = []
    for i, (ref, first, size, a, b) in enumerate(flows):
        row = (at[b] * 4 + at[a]) * 16
        src = w_small if i == 2 else w_x
        arriving.append(copy(view(src, None, row, 16, first, size), view(ref, mine, row, 16, first, size), i, partner))
    params_here = pltpu.make_async_copy(own, params.at[at["z"], at["x"], at["l"]], here.at[2])
    local = [
        pltpu.make_async_copy(w_x, full_x.at[mine], here.at[0]),
        pltpu.make_async_copy(w_small, full_small.at[mine], here.at[1]),
        params_here,
    ]
    for one in local:
        one.start()
    last = [
        copy(w_x, full_x.at[mine], 24, sibling),
        copy(w_small, full_small.at[mine], 25, sibling),
    ]
    params_here.wait()

    def share(stage):
        axis = ("l", "x", "z")[stage]
        ref = params.at[(at["z"], at["x"], at["l"])[: 3 - stage]]
        return [copy(ref, ref, 3 * stage + d, to, (own_send, own_recv)) for d, to in enumerate(peers(at, axis))]

    shared = share(0)
    second = []
    for i, (ref, first, size, a, b) in enumerate(flows):
        arriving[i].wait_recv()
        piece = view(ref, opposite, (at[b] * 4 + at[a]) * 16, 16, first, size)
        second.append([copy(piece, piece, 3 + 3 * i + d, to) for d, to in enumerate(peers(at, a))])
    for one in shared:
        one.wait_recv()
    shared = share(1)
    third = []
    for i, (ref, first, size, a, b) in enumerate(flows):
        for one in second[i]:
            one.wait_recv()
        block = view(ref, opposite, at[b] * 64, 64, first, size)
        third.append([copy(block, block, 12 + 3 * i + d, to) for d, to in enumerate(peers(at, b))])
        last.append(copy(block, block, 21 + i, sibling))
    for one in shared:
        one.wait_recv()
    shared = share(2)
    for i, (ref, first, size, a, b) in enumerate(flows):
        for d in range(3):
            third[i][d].wait_recv()
            block = view(ref, opposite, lax.rem(at[b] + 3 - d, 4) * 64, 64, first, size)
            last.append(copy(block, block, 26 + 3 * i + d, sibling))
    for one in last + shared:
        one.wait_recv()
    for one in local[:2]:
        one.wait()
    for one in started:
        one.wait_send()


def gather_weights(w_x, w_small, own):
    vmem = pl.BlockSpec(memory_space=pltpu.VMEM)
    return pl.pallas_call(
        gather_kernel,
        out_shape=[
            jax.ShapeDtypeStruct((4, *w_x.shape), BF16),
            jax.ShapeDtypeStruct((4, *w_small.shape), BF16),
            jax.ShapeDtypeStruct((4, 4, 2, 8, 128), F32),
        ],
        in_specs=[vmem] * 3,
        out_specs=[vmem] * 3,
        scratch_shapes=[
            pltpu.SemaphoreType.DMA((35,)), pltpu.SemaphoreType.DMA((35,)), pltpu.SemaphoreType.DMA((3,)),
            pltpu.SemaphoreType.DMA((9,)), pltpu.SemaphoreType.DMA((9,)),
        ],
        compiler_params=pltpu.CompilerParams(
            vmem_limit_bytes=VMEM_LIMIT, collective_id=2, has_side_effects=True
        ),
        cost_estimate=pl.CostEstimate(flops=int(1e6), bytes_accessed=int(4e7), transcendentals=0),
    )(w_x, w_small, own)


def unpack_kernel(sum_z, sum_x, sum_out, out_z, out_x, out_out, out_extra):
    for low in range(2):
        rows = slice(PIECE * low, PIECE * (low + 1))
        out_z[rows, :] = sum_z[0, 0, low].astype(F32)
        out_x[rows, :] = sum_x[0, 0, low, 0:PIECE, :].astype(F32)
        out_out[low, 0] = sum_out[low, 0, 0].astype(F32)
        out_extra[0, low] = sum_x[0, 0, low, PIECE:, :].astype(F32)


def unpack(sum_z, sum_x, sum_out):
    return call(
        unpack_kernel,
        [((2 * PIECE, INNER), F32), ((2 * PIECE, INNER), F32), ((2, 2, PIECE, 8 * 128), F32), ((4, 2, 4 * EXTRA, 128), F32)],
        [
            lanes(2 * PIECE), lanes(2 * PIECE),
            pl.BlockSpec((2, 1, PIECE, 128), lambda i: (0, i // 8, 0, ((i // 4) % 2) * 4 + i % 4)),
            pl.BlockSpec((1, 2, EXTRA, 128), lambda i: (i // 4, 0, i % 4, 0)),
        ],
        [
            pl.BlockSpec((1, 1, 2, PIECE, 128), lambda i: (i // 4, i % 4, 0, 0, 0)),
            pl.BlockSpec((1, 1, 2, PIECE + EXTRA, 128), lambda i: (i % 4, i // 4, 0, 0, 0)),
            pl.BlockSpec((2, 1, 1, PIECE, 128), lambda i: (0, i % 4, i // 4, 0, 0)),
        ],
    )(sum_z, sum_x, sum_out)


def swap(values):
    return lax.all_to_all(values, "seq", split_axis=0, concat_axis=0, tiled=True)


def gather_rows(shard):
    return lax.all_gather(shard, "wshard", axis=0, tiled=True)


def shards(
    layer_in, gain_in, w_z, w_x, w_bc, w_dt, conv_x_weight, conv_x_bias, conv_bc_weight, conv_bc_bias,
    dt_bias, a_log, d_skip, gain_norm, w_out, cotangent,
):
    width = layer_in.shape[2]
    chunks = lax.axis_size("seq")
    place = lax.axis_index("seq")
    tail = lax.ppermute(layer_in[:, TOK - (TAPS - 1) :, :], "seq", [(i, i + 1) for i in range(chunks - 1)])
    full_z = gather_rows(w_z)
    full_out = gather_rows(w_out)
    own = jnp.concatenate([conv_x_weight.reshape(-1), conv_x_bias, dt_bias, a_log, d_skip, jnp.zeros((701,), F32)])
    small = jnp.concatenate([w_bc, w_dt, jnp.zeros((w_bc.shape[0], SMALL - 2 * STATE - HEADS), BF16)], axis=1)
    full_x, full_small, params = gather_weights(w_x, small, own.reshape(8, 128))
    full_x = full_x.reshape(width, INNER)
    full_small = full_small.reshape(width, SMALL)
    params = params.reshape(HEADS, -1)
    taps_x = params[:, : TAPS * HEAD].reshape(HEADS, TAPS, HEAD).swapaxes(0, 1).reshape(TAPS, INNER)
    bias_x = params[:, TAPS * HEAD : (TAPS + 1) * HEAD].reshape(1, INNER)
    bias_dt, log_a, skip = (params[:, (TAPS + 1) * HEAD + i].reshape(1, HEADS) for i in range(3))
    bias_bc = conv_bc_bias.reshape(1, -1)
    skip_wide = jnp.repeat(skip, HEAD, axis=1)

    hidden = layer_in.astype(F32).reshape(ROWS, width)
    upstream = cotangent.reshape(ROWS, width)
    halo = jnp.pad(tail, ((0, 0), (HALO - (TAPS - 1), 0), (0, 0))).reshape(SEQS * HALO, width).astype(F32)
    tokens = jnp.concatenate([hidden, halo], axis=0)
    inv = lax.rsqrt(jnp.mean(tokens * tokens, axis=-1, keepdims=True) + EPS)
    normed = (tokens * inv * gain_in[None, :]).astype(BF16)
    inv = inv[:ROWS]

    x_raw = mm(normed, full_x, NN).astype(BF16)
    small_raw = mm(normed, full_small, NN).astype(BF16)
    bc_raw, dt_raw = small_raw[:, : 2 * STATE], small_raw[:, 2 * STATE : 2 * STATE + HEADS]
    xc, bcc, dt, r, u, dt_wide, r_wide, r_rows = front(x_raw, bc_raw, dt_raw, taps_x, bias_x, conv_bc_weight, bias_bc, bias_dt, log_a)
    decay = jnp.exp(swap(r[TOK - 1 :: TOK].T))
    u_all = swap(u)
    y_in = inside(xc, bcc, dt_wide, r_wide, r_rows)
    gate = mm(normed[:ROWS], full_z, NN)
    d_mixed = mm(upstream, full_out, NT)
    start = swap(states(decay, u_all, False))
    mixed, d_y, d_gate, v, g_norm, row_dot = middle(
        y_in, xc, bcc, r_wide, start, skip_wide, gate, d_mixed, gain_norm.reshape(1, INNER)
    )
    v_all = swap(v)
    layer_out = (hidden + mm(mixed, full_out, NN)).astype(BF16).reshape(SEQS, TOK, width)
    d_stepped, d_bc_in = inside_back(xc, d_y, bcc, dt_wide, r_wide, r_rows)
    d_normed_z = mm(d_gate, full_z, NT)
    end = swap(states(decay, v_all, True))
    d_x_raw, d_bc_raw, d_dt_raw, g_x, g_bc, g_heads = back(
        d_stepped, xc, d_y, x_raw, start, end, bcc, dt, dt_wide, r_wide, bc_raw, dt_raw, d_bc_in, row_dot,
        taps_x, bias_x, conv_bc_weight, bias_bc, bias_dt, log_a, skip_wide,
    )
    d_small = jnp.concatenate([d_bc_raw, d_dt_raw, jnp.zeros((ALL, SMALL - 2 * STATE - HEADS), BF16)], axis=1)
    d_normed = mm(d_x_raw, full_x, NT) + mm(d_small, full_small, NT)
    back_tail = d_normed[ROWS:].reshape(SEQS, HALO, width)[:, HALO - (TAPS - 1) :]
    back_tail = lax.ppermute(back_tail, "seq", [(i + 1, i) for i in range(chunks - 1)])
    d_normed = d_normed[:ROWS] + d_normed_z
    d_normed = d_normed + jnp.pad(back_tail, ((0, 0), (TOK - (TAPS - 1), 0), (0, 0))).reshape(ROWS, width)
    unit = hidden * inv
    g_in = jnp.sum(d_normed * unit, axis=0)
    pulled = d_normed * gain_in[None, :]
    d_hidden = inv * (pulled - unit * jnp.mean(pulled * unit, axis=-1, keepdims=True))
    input_grad = (upstream.astype(F32) + d_hidden).reshape(SEQS, TOK, width)

    pieces = (g_x[: TAPS + 1], g_bc[: TAPS + 1], g_heads[:3], g_in, g_norm)
    sizes = [p.size for p in pieces]
    vector = jnp.concatenate([*(p.reshape(-1) for p in pieces), jnp.zeros((PIECE * 128 - sum(sizes),), F32)])
    grad_w_z, grad_w_x, grad_w_out, extra = unpack(
        *reduce_grads(normed, d_gate, d_x_raw, d_small, mixed, upstream, vector.reshape(PIECE, 128))
    )
    grad_w_out = grad_w_out.reshape(4 * PIECE, width)
    extra = extra.reshape(4, 2 * PIECE, 128)
    grad_w_bc = jnp.concatenate([extra[0], extra[1]], axis=1)
    grad_w_dt = extra[2][:, :HEADS]
    total = extra[3][:PIECE].reshape(-1)[: sum(sizes)]
    ends = [sum(sizes[: i + 1]) for i in range(len(sizes) - 1)]
    s_x, s_bc, s_heads, s_in, s_norm = jnp.split(total, ends)
    s_x = lax.dynamic_slice(s_x.reshape(TAPS + 1, INNER), (0, place * HEAD), (TAPS + 1, HEAD))
    s_bc = s_bc.reshape(TAPS + 1, 2 * STATE)
    s_heads = lax.dynamic_slice(s_heads.reshape(3, HEADS), (0, place), (3, 1))
    return (
        layer_out, input_grad, s_in, grad_w_z, grad_w_x, grad_w_bc, grad_w_dt,
        s_x[:TAPS], s_x[TAPS], s_bc[:TAPS], s_bc[TAPS], s_heads[0], s_heads[1], s_heads[2], s_norm, grad_w_out,
    )


def solution(mesh):
    rows, heads = P("wshard", None), P("seq")
    tokens = P("wshard", "seq", None)
    return jax.shard_map(
        shards,
        mesh=mesh,
        in_specs=(
            tokens, P(), rows, rows, rows, rows, P(None, "seq"), heads, P(), P(), heads, heads, heads, P(), rows, tokens,
        ),
        out_specs=(
            tokens, tokens, P(), rows, rows, rows, rows, P(None, "seq"), heads, P(), P(), heads, heads, heads, P(), rows,
        ),
        check_vma=False,
    )
```

```python
import functools

import jax
import jax.numpy as jnp
from jax import lax
from jax.experimental import pallas as pl
from jax.experimental.pallas import tpu as pltpu
from jax.sharding import PartitionSpec as P

F32 = jnp.float32
BF16 = jnp.bfloat16
EPS = 1e-05
HIGHEST = lax.Precision.HIGHEST
HEADS = 32
HEAD = 64
STATE = 128
TOK = 128
SEQS = 2
ROWS = SEQS * TOK
HALO = 8
ALL = ROWS + SEQS * HALO
PAIRS = HEADS // 2
INNER = HEADS * HEAD
TAPS = 4


def mm(a, b, dims, precision=None):
    return lax.dot_general(a, b, ((dims[0], dims[1]), ((), ())), precision=precision, preferred_element_type=F32)


NN = ((1,), (0,))
NT = ((1,), (1,))
TN = ((0,), (0,))


def iota(shape, dim):
    return lax.broadcasted_iota(jnp.int32, shape, dim)


def pair_matrix(pair):
    upper = (iota((HEADS, 128), 1) >= HEAD).astype(jnp.int32)
    return (iota((HEADS, 128), 0) == 2 * pair + upper).astype(F32)


def pair_rows(pair):
    return (iota((8, HEADS), 1) == 2 * pair + iota((8, HEADS), 0)).astype(F32)


def head_sums(values, ex):
    high = values.astype(BF16)
    low = (values - high.astype(F32)).astype(BF16)
    ex = ex.astype(BF16)
    return mm(jnp.concatenate([high, low], axis=1), jnp.concatenate([ex, ex], axis=1), NT)


def lane_sums(values):
    high = values.astype(BF16)
    low = (values - high.astype(F32)).astype(BF16)
    return mm(jnp.ones((8, 256), BF16), jnp.concatenate([high, low], axis=1), NT)[0:1, :]


def causal_mask():
    return iota((TOK, TOK), 0) >= iota((TOK, TOK), 1)


def shifted(padded, k):
    back = TAPS - 1 - k
    if back:
        padded = pltpu.roll(padded, back, 0)
    return padded[HALO:, :]


def padded_of(rows, b):
    return jnp.concatenate(
        [rows[ROWS + HALO * b : ROWS + HALO * (b + 1), :], rows[TOK * b : TOK * (b + 1), :]], axis=0
    )


def conv_pre(padded, taps, bias):
    total = bias
    for k in range(TAPS):
        total = total + taps[k : k + 1, :] * shifted(padded, k)
    return total


def conv_back(padded, taps, bias, grad):
    pre = conv_pre(padded, taps, bias)
    sig = jax.nn.sigmoid(pre)
    d_pre = grad * (sig * (1.0 + pre * (1.0 - sig)))
    low = jnp.concatenate([jnp.zeros((HALO, d_pre.shape[1]), F32), d_pre], axis=0)
    d_pad = taps[TAPS - 1 : TAPS, :] * low
    for k in range(TAPS - 1):
        d_pad = d_pad + taps[k : k + 1, :] * pltpu.roll(low, HALO + TOK - (TAPS - 1 - k), 0)
    d_taps = [jnp.sum(d_pre * shifted(padded, k), axis=0, keepdims=True) for k in range(TAPS)]
    return d_pad, d_taps, jnp.sum(d_pre, axis=0, keepdims=True)


def block_diagonal(pair_values):
    first = iota(pair_values.shape, 1) < HEAD
    zero = jnp.zeros_like(pair_values)
    return jnp.concatenate(
        [jnp.where(first, pair_values, zero), jnp.where(first, zero, pair_values)], axis=0
    )


def decay_pair(r_lanes, r_rows):
    mask = causal_mask()
    out = []
    for q in range(2):
        spread = r_lanes[:, HEAD * q : HEAD * q + 1] - r_rows[q : q + 1, :]
        out.append(jnp.exp(jnp.where(mask, spread, -1e30)))
    return out


def front_kernel(x_raw, bc_raw, dt_raw, taps_x, bias_x, taps_bc, bias_bc, dt_bias, a_log, xc, bcc, dt, r, u, dt_wide, r_wide, r_rows):
    pair = pl.program_id(0)

    @pl.when(pair == 0)
    def _():
        raw = bc_raw[...].astype(F32)
        steps = dt_raw[0:ROWS, :].astype(F32) + dt_bias[...]
        dt[...] = jax.nn.softplus(steps)
        tri = causal_mask().astype(F32)
        decay = dt[...] * (-jnp.exp(a_log[...]))
        for b in range(SEQS):
            pre = conv_pre(padded_of(raw, b), taps_bc[...], bias_bc[...])
            bcc[TOK * b : TOK * (b + 1), :] = (pre * jax.nn.sigmoid(pre)).astype(BF16)
            r[TOK * b : TOK * (b + 1), :] = mm(tri, decay[TOK * b : TOK * (b + 1), :], NN, HIGHEST)

    raw = x_raw[...].astype(F32)
    ex = pair_matrix(pair)
    both = mm(jnp.concatenate([r[...], dt[...]], axis=0), ex, NN, HIGHEST)
    r_wide[...] = both[0:ROWS, :]
    dt_wide[...] = both[ROWS:, :]
    r_rows[0] = mm(pair_rows(pair), r[...], NT, HIGHEST)
    for b in range(SEQS):
        span = slice(TOK * b, TOK * (b + 1))
        pre = conv_pre(padded_of(raw, b), taps_x[...], bias_x[...])
        low = (pre * jax.nn.sigmoid(pre)).astype(BF16)
        xc[span, :] = low
        r_lanes = both[span, :]
        dt_lanes = both[ROWS + TOK * b : ROWS + TOK * (b + 1), :]
        to_end = jnp.exp(r_lanes[TOK - 1 : TOK, :] - r_lanes)
        scaled = (to_end * (dt_lanes * low.astype(F32))).astype(BF16)
        state = mm(scaled, bcc[span, 0:STATE], TN).astype(BF16)
        u[0, b] = state[0:HEAD, :]
        u[1, b] = state[HEAD:, :]


def whole(shape):
    return pl.BlockSpec(shape, lambda *_: (0,) * len(shape))


def lanes(rows):
    return pl.BlockSpec((rows, 128), lambda j: (0, j))


STATES = pl.BlockSpec((2, SEQS, HEAD, STATE), lambda j: (j, 0, 0, 0))
PAIR_ROWS = pl.BlockSpec((1, 8, ROWS), lambda j: (j, 0, 0))
STATES_SHAPE = (HEADS, SEQS, HEAD, STATE)
VMEM_LIMIT = 48 * 1024 * 1024


def call(kernel, outs, out_specs, in_specs, grid=(PAIRS,), scratch=(), cost=None):
    return pl.pallas_call(
        kernel,
        grid=grid,
        out_shape=[jax.ShapeDtypeStruct(s, d) for s, d in outs],
        in_specs=in_specs,
        out_specs=out_specs,
        scratch_shapes=scratch,
        compiler_params=pltpu.CompilerParams(
            vmem_limit_bytes=VMEM_LIMIT, dimension_semantics=("arbitrary",) * len(grid)
        ),
        cost_estimate=cost or pl.CostEstimate(flops=int(1e9), bytes_accessed=int(1e7), transcendentals=0),
    )


def front(x_raw, bc_raw, dt_raw, taps_x, bias_x, taps_bc, bias_bc, dt_bias, a_log):
    return call(
        front_kernel,
        [((ROWS, INNER), BF16), ((ROWS, 2 * STATE), BF16), ((ROWS, HEADS), F32), ((ROWS, HEADS), F32), (STATES_SHAPE, BF16), ((ROWS, INNER), F32), ((ROWS, INNER), F32), ((PAIRS, 8, ROWS), F32)],
        [lanes(ROWS), whole((ROWS, 2 * STATE)), whole((ROWS, HEADS)), whole((ROWS, HEADS)), STATES, lanes(ROWS), lanes(ROWS), PAIR_ROWS],
        [
            lanes(ALL), whole((ALL, 2 * STATE)), whole((ALL, HEADS)), lanes(TAPS), lanes(1),
            whole((TAPS, 2 * STATE)), whole((1, 2 * STATE)), whole((1, HEADS)), whole((1, HEADS)),
        ],
    )(x_raw, bc_raw, dt_raw, taps_x, bias_x, taps_bc, bias_bc, dt_bias, a_log)


def states_kernel(reverse, decay, own, before):
    chunks = own.shape[0]

    def step(i, carry):
        c = chunks - 1 - i if reverse else i
        after = []
        for b in range(SEQS):
            before[c, b] = carry[b].astype(BF16)
            after.append(decay[c, b] * carry[b] + own[c, b].astype(F32))
        return tuple(after)

    lax.fori_loop(0, chunks, step, tuple(jnp.zeros((HEAD, STATE), F32) for _ in range(SEQS)))


def states(decay, own, reverse):
    return pl.pallas_call(
        functools.partial(states_kernel, reverse),
        out_shape=jax.ShapeDtypeStruct(own.shape, BF16),
        in_specs=[pl.BlockSpec(memory_space=pltpu.SMEM), pl.BlockSpec(memory_space=pltpu.VMEM)],
        out_specs=pl.BlockSpec(memory_space=pltpu.VMEM),
        compiler_params=pltpu.CompilerParams(vmem_limit_bytes=VMEM_LIMIT),
        cost_estimate=pl.CostEstimate(flops=int(1e6), bytes_accessed=int(2e6), transcendentals=0),
    )(decay, own)


def inside_kernel(xc, bcc, dt_wide, r_wide, r_rows, y, scores):
    pair = pl.program_id(0)

    @pl.when(pair == 0)
    def _():
        for b in range(SEQS):
            span = slice(TOK * b, TOK * (b + 1))
            scores[b] = mm(bcc[span, STATE:], bcc[span, 0:STATE], NT)

    for b in range(SEQS):
        span = slice(TOK * b, TOK * (b + 1))
        dt_lanes = dt_wide[span, :]
        first, second = decay_pair(r_wide[span, :], r_rows[0, :, span])
        both = jnp.concatenate([scores[b] * first, scores[b] * second], axis=1).astype(BF16)
        stepped = (dt_lanes * xc[span, :].astype(F32)).astype(BF16)
        y[span, :] = mm(both, block_diagonal(stepped), NN)


def inside(xc, bcc, dt_wide, r_wide, r_rows):
    return call(
        inside_kernel,
        [((ROWS, INNER), F32)],
        [lanes(ROWS)],
        [lanes(ROWS), whole((ROWS, 2 * STATE)), lanes(ROWS), lanes(ROWS), PAIR_ROWS],
        scratch=[pltpu.VMEM((SEQS, TOK, TOK), F32)],
    )(xc, bcc, dt_wide, r_wide, r_rows)[0]


def middle_kernel(
    y_in, xc, bcc, r, start, d_skip, gate, d_mixed, gain,
    mixed, d_y, d_gate, own, d_gain, row_dot,
    y_all, square, cross, scale, slope,
):
    phase = pl.program_id(0)
    pair = pl.program_id(1)
    ex = pair_matrix(pair)
    skip = d_skip[...]
    z = gate[...]
    sig = jax.nn.sigmoid(z)
    pulled = d_mixed[...] * gain[...]

    @pl.when(phase == 0)
    def _():
        @pl.when(pair == 0)
        def _():
            square[...] = jnp.zeros_like(square)
            cross[...] = jnp.zeros_like(cross)

        for b in range(SEQS):
            span = slice(TOK * b, TOK * (b + 1))
            before = jnp.concatenate([start[0, b], start[1, b]], axis=0)
            grown = jnp.exp(r[span, :])
            y_all[pair, span, :] = y_in[span, :] + grown * mm(bcc[span, STATE:], before, NT)
        y = (y_all[pair] + skip * xc[...].astype(F32)).astype(BF16).astype(F32)
        gated = y * (z * sig)
        square[...] += gated * gated
        cross[...] += pulled * gated

    @pl.when(phase == 1)
    def _():
        @pl.when(pair == 0)
        def _():
            inv = lax.rsqrt(jnp.sum(square[...], axis=1, keepdims=True) * (1.0 / INNER) + EPS)
            mean = jnp.sum(cross[...], axis=1, keepdims=True) * (1.0 / INNER)
            scale[...] = jnp.broadcast_to(inv, scale.shape)
            slope[...] = jnp.broadcast_to(inv * inv * inv * mean, slope.shape)
            row_dot[...] = jnp.zeros_like(row_dot)

        y = (y_all[pair] + skip * xc[...].astype(F32)).astype(BF16).astype(F32)
        silu = z * sig
        gated = y * silu
        unit = gated * scale[...]
        mixed[...] = (unit * gain[...]).astype(BF16)
        d_gain[...] = jnp.sum(d_mixed[...] * unit, axis=0, keepdims=True)
        d_gated = scale[...] * pulled - gated * slope[...]
        low = (d_gated * silu).astype(BF16)
        d_y[...] = low
        d_gate[...] = (d_gated * y * (sig * (1.0 + z * (1.0 - sig)))).astype(BF16)
        row_dot[...] += head_sums(low.astype(F32) * y_all[pair], ex)
        for b in range(SEQS):
            span = slice(TOK * b, TOK * (b + 1))
            grown = jnp.exp(r[span, :])
            state = mm((grown * low[span, :].astype(F32)).astype(BF16), bcc[span, STATE:], TN).astype(BF16)
            own[0, b] = state[0:HEAD, :]
            own[1, b] = state[HEAD:, :]


def middle(y_in, xc, bcc, r, start, d_skip, gate, d_mixed, gain):
    def cols(rows):
        return pl.BlockSpec((rows, 128), lambda p, j: (0, j))

    def first(rows):
        return pl.BlockSpec((rows, 128), lambda p, j: (0, jnp.where(p == 0, j, PAIRS - 1)))

    def second(rows):
        return pl.BlockSpec((rows, 128), lambda p, j: (0, jnp.where(p == 1, j, 0)))

    states_in = pl.BlockSpec((2, SEQS, HEAD, STATE), lambda p, j: (jnp.where(p == 0, j, PAIRS - 1), 0, 0, 0))
    states_out = pl.BlockSpec((2, SEQS, HEAD, STATE), lambda p, j: (jnp.where(p == 1, j, 0), 0, 0, 0))
    return call(
        middle_kernel,
        [((ROWS, INNER), BF16), ((ROWS, INNER), BF16), ((ROWS, INNER), BF16), (STATES_SHAPE, BF16), ((1, INNER), F32), ((ROWS, HEADS), F32)],
        [second(ROWS), second(ROWS), second(ROWS), states_out, second(1), whole((ROWS, HEADS))],
        [first(ROWS), cols(ROWS), whole((ROWS, 2 * STATE)), cols(ROWS), states_in, cols(1), cols(ROWS), cols(ROWS), cols(1)],
        grid=(2, PAIRS),
        scratch=[pltpu.VMEM((PAIRS, ROWS, 128), F32)] + [pltpu.VMEM((ROWS, 128), F32)] * 4,
    )(y_in, xc, bcc, r, start, d_skip, gate, d_mixed, gain)


REDUCE = (("y", "z", "x"), ("x", "y", "z"), ("x", "y", "z"), ("y", "z", "x"), ("z", "x", "y"))
GATHER = (("l", "z", "x"), ("x", "z", "l"), ("l", "z", "x"), ("l", "x", "z"), ("x", "z", "l"))
PIECE = 128
EXTRA = 32
PIECE_ROWS = (PIECE, PIECE, 48, 48, 32 + EXTRA)
SETS = len(PIECE_ROWS)
SMALL = 3 * 128
VECTOR = (16, INNER)


def position():
    seq, shard = lax.axis_index("seq"), lax.axis_index("wshard")
    high, core = shard // 2, shard % 2
    low = seq % 2
    return {"z": seq // 8, "x": (seq // 2) % 4, "y": high * 2 + low, "l": low, "core": core}


def device(at):
    return {"seq": at["z"] * 8 + at["x"] * 2 + at["y"] % 2, "wshard": (at["y"] // 2) * 2 + at["core"]}


def moved(at, axis, to):
    new = dict(at)
    if axis == "l":
        new["y"] = (at["y"] // 2) * 2 + to
        new["l"] = to
    else:
        new[axis] = to
        if axis == "y":
            new["l"] = to % 2
    return new


def peers(at, axis):
    size = 2 if axis in ("l", "core") else 4
    return [moved(at, axis, lax.rem(at[axis] + d, size)) for d in range(1, size)]


def greet(everyone):
    barrier = pltpu.get_barrier_semaphore()
    for other in everyone:
        pl.semaphore_signal(barrier, inc=1, device_id=device(other), device_id_type=pl.DeviceIdType.MESH)
    pl.semaphore_wait(barrier, len(everyone))


def tail_kernel(
    v, decay, xc, d_y, bcc, dt, dt_wide, r_wide, r_rows, x_raw, start, bc_raw, dt_raw, row_dot,
    taps_x, bias_x, taps_bc, bias_bc, dt_bias, a_log, d_skip, g_norm,
    normed, d_gate, mixed, cot, layer_in, gain_in, full_z, full_x, full_small,
    out_z, out_out, out_xa, out_xb, out_xc, input_grad, vector,
    weights, v_all, g_own, end, d_stepped, scores, d_scores, d_bc, sums, d_x_raw, d_small, g_x, g_bc, g_heads,
    d_normed, halo_out, halo_in, few_own, few_got,
    keep_n, keep_m, next_n, next_m, sib_n, sib_gate, sib_m, sib_cot, sib_wide, sib_small,
    parts_z, parts_out, parts_xa, parts_xb, parts_xc,
    got_z1, got_out1, got_xa1, got_xb1, got_xc1, sum_z1, sum_out1, sum_xa1, sum_xb1, sum_xc1,
    got_z2, got_out2, got_xa2, got_xb2, got_xc2, sum_z2, sum_out2, sum_xa2, sum_xb2, sum_xc2,
    got_z3, got_out3, got_xa3, got_xb3, got_xc3,
    v_send, v_recv, g_send, g_recv, sib_send, sib_recv, red_send, red_recv, all_send, all_recv,
    few_send, few_recv, halo_sem, load_sem,
):
    at = position()
    me = lax.axis_index("seq")
    core = at["core"]
    sibling = peers(at, "core")[0]
    barrier = pltpu.get_barrier_semaphore()

    def greet_chunk(d, _):
        pl.semaphore_signal(
            barrier, inc=1, device_id={"seq": lax.rem(me + d, HEADS)}, device_id_type=pl.DeviceIdType.MESH
        )
        return 0

    lax.fori_loop(1, HEADS, greet_chunk, 0)
    others = [sibling] + peers(at, "y")
    for other in others:
        pl.semaphore_signal(barrier, inc=1, device_id=device(other), device_id_type=pl.DeviceIdType.MESH)
    pl.semaphore_wait(barrier, HEADS - 1 + len(others))
    started = []

    def copy(src, dst, send, recv, to):
        one = pltpu.make_async_remote_copy(
            src_ref=src, dst_ref=dst, send_sem=send, recv_sem=recv,
            device_id=device(to), device_id_type=pl.DeviceIdType.MESH,
        )
        one.start()
        started.append(one)
        return one

    def chunk_copy(src, dst, send, recv, to, at_dst):
        return pltpu.make_async_remote_copy(
            src_ref=src.at[to], dst_ref=dst.at[at_dst], send_sem=send.at[to], recv_sem=recv.at[at_dst],
            device_id={"seq": to}, device_id_type=pl.DeviceIdType.MESH,
        )

    def swap_start(src, dst, send, recv):
        def go(d, _):
            chunk_copy(src, dst, send, recv, lax.rem(me + d, HEADS), me).start()
            return 0

        lax.fori_loop(1, HEADS, go, 0)
        dst[me] = src[me]

    def swap_wait(src, dst, send, recv):
        def go(d, _):
            other = lax.rem(me + d, HEADS)
            chunk_copy(src, dst, send, recv, other, other).wait_recv()
            return 0

        lax.fori_loop(1, HEADS, go, 0)

    def swap_sent(src, dst, send, recv):
        def go(d, _):
            chunk_copy(src, dst, send, recv, lax.rem(me + d, HEADS), me).wait_send()
            return 0

        lax.fori_loop(1, HEADS, go, 0)

    def lane_block(j, size=128):
        return pl.ds(pl.multiple_of(j * size, size), size)

    swap_start(v, v_all, v_send, v_recv)

    def columns(ref, high, which, size):
        return ref.at[:, lane_block(2 * high + which, size)]

    def transposed(ref, high, which, size):
        return ref[:, lane_block(2 * high + which, size)].astype(F32).T.astype(BF16)

    pairs = [(columns(normed, h, 1 - core, 256), sib_n.at[h]) for h in range(2)] + [(d_gate, sib_gate)]
    pairs += [(columns(mixed, h, 1 - core, 512), sib_m.at[h]) for h in range(2)] + [(cot, sib_cot)]
    from_sibling = [copy(a, b, sib_send.at[i], sib_recv.at[i], sibling) for i, (a, b) in enumerate(pairs)]
    loading = pltpu.make_async_copy(full_z, weights, load_sem)
    loading.start()

    d_scores[...] = jnp.zeros_like(d_scores)
    for b in range(SEQS):
        span = slice(TOK * b, TOK * (b + 1))
        scores[b] = mm(bcc[span, STATE:], bcc[span, 0:STATE], NT)

    def inside_pair(j, _):
        cols = lane_block(j)
        for b in range(SEQS):
            span = slice(TOK * b, TOK * (b + 1))
            first, second = decay_pair(r_wide[span, cols], r_rows[j, :, span])
            both = jnp.concatenate([scores[b] * first, scores[b] * second], axis=0).astype(BF16)
            stepped = (dt_wide[span, cols] * xc[span, cols].astype(F32)).astype(BF16)
            wide = block_diagonal(d_y[span, cols])
            d_stepped[span, cols] = mm(both, wide, TN)
            d_both = mm(wide, stepped, NT)
            d_scores[b] += d_both[0:TOK, :] * first + d_both[TOK:, :] * second
        return 0

    lax.fori_loop(0, PAIRS, inside_pair, 0)
    for b in range(SEQS):
        span = slice(TOK * b, TOK * (b + 1))
        low = d_scores[b].astype(BF16)
        d_bc[span, 0:STATE] = mm(low, bcc[span, STATE:], TN)
        d_bc[span, STATE:] = mm(low, bcc[span, 0:STATE], NN)

    swap_wait(v, v_all, v_send, v_recv)

    def chunk_step(i, carry):
        c = HEADS - 1 - i
        after = []
        for b in range(SEQS):
            g_own[c, b] = carry[b].astype(BF16)
            after.append(decay[c, b] * carry[b] + v_all[c, b].astype(F32))
        return tuple(after)

    lax.fori_loop(0, HEADS, chunk_step, tuple(jnp.zeros((HEAD, STATE), F32) for _ in range(SEQS)))
    swap_start(g_own, end, g_send, g_recv)

    parts = (parts_z, parts_out, parts_xa, parts_xb, parts_xc)
    got = (
        (got_z1, got_out1, got_xa1, got_xb1, got_xc1),
        (got_z2, got_out2, got_xa2, got_xb2, got_xc2),
        (got_z3, got_out3, got_xa3, got_xb3, got_xc3),
    )
    partial = ((sum_z1, sum_out1, sum_xa1, sum_xb1, sum_xc1), (sum_z2, sum_out2, sum_xa2, sum_xb2, sum_xc2))
    outs = (out_z, out_out, out_xa, out_xb, out_xc)
    arriving = [None] * SETS

    def send_stage(stage, which, src):
        axis = REDUCE[which][stage]
        arriving[which] = [
            copy(
                src.at[to[axis]], got[stage][which].at[d],
                red_send.at[which, stage, d], red_recv.at[which, stage, d], to,
            )
            for d, to in enumerate(peers(at, axis))
        ]

    def arrived(which):
        for one in arriving[which]:
            one.wait_recv()

    def add_stage(stage, which):
        arrived(which)
        src = parts[which] if stage == 0 else partial[0][which]
        dst, came = partial[stage][which], got[stage][which]
        mine = at[REDUCE[which][stage]]

        def add(i, _):
            for j in range(4) if stage == 0 else ((),):
                index = (i, j) if stage == 0 else (i,)
                value = src[(mine, *index)].astype(F32)
                for d in range(3):
                    value = value + came[(d, *index)].astype(F32)
                dst[index] = value.astype(BF16)
            return 0

        lax.fori_loop(0, 4, add, 0)
        send_stage(stage + 1, which, dst)

    def gather_stage(stage, which):
        first, second, third = GATHER[which]
        index = (at[third], at[second], at[first])[: 3 - stage]
        ref = outs[which].at[index]
        arriving[which] = [
            copy(ref, ref, all_send.at[which, stage, d], all_recv.at[which, stage, d], to)
            for d, to in enumerate(peers(at, (first, second, third)[stage]))
        ]

    def last_add(which):
        arrived(which)
        first, second, third = GATHER[which]
        value = partial[1][which][at[REDUCE[which][2]]].astype(F32)
        for d in range(3):
            value = value + got[2][which][d].astype(F32)
        outs[which][at[third], at[second], at[first]] = value.astype(BF16)
        gather_stage(0, which)

    def gather_next(stage, which):
        arrived(which)
        gather_stage(stage, which)

    for h in range(2):
        keep_n[256 * h : 256 * (h + 1), :] = transposed(normed, h, core, 256)
        keep_m[512 * h : 512 * (h + 1), :] = transposed(mixed, h, core, 512)
    for one in from_sibling[:3]:
        one.wait_recv()
    for h in range(2):
        next_n[256 * h : 256 * (h + 1), :] = sib_n[h].astype(F32).T.astype(BF16)

    def tile_z(n, _):
        cols = lane_block(n, 256)
        res = mm(keep_n[:, 0:ROWS], d_gate[:, cols], NN) + mm(next_n[:, 0:ROWS], sib_gate[:, cols], NN)
        for y in range(4):
            for k in range(2):
                parts_z[y, (n % 2) * 2 + k, n // 2] = res[128 * y : 128 * y + 128, 128 * k : 128 * k + 128].astype(BF16)
        return 0

    lax.fori_loop(0, 8, tile_z, 0)
    send_stage(0, 0, parts_z)
    for one in from_sibling[3:]:
        one.wait_recv()
    for h in range(2):
        next_m[512 * h : 512 * (h + 1), :] = sib_m[h].astype(F32).T.astype(BF16)

    def tile_out(n, _):
        cols = lane_block(n, 256)
        res = mm(keep_m[...], cot[:, cols], NN) + mm(next_m[...], sib_cot[:, cols], NN)
        for y in range(4):
            for half in range(2):
                for k in range(2):
                    row = 256 * y + 128 * half
                    parts_out[half * 2 + n // 2, y, (n % 2) * 2 + k] = res[row : row + 128, 128 * k : 128 * k + 128].astype(BF16)
        return 0

    lax.fori_loop(0, 4, tile_out, 0)
    send_stage(0, 1, parts_out)

    loading.wait()
    for n in range(4):
        cols = slice(256 * n, 256 * (n + 1))
        d_normed[0:ROWS, cols] = mm(d_gate[...], weights[cols, :], NT)
    loading = pltpu.make_async_copy(full_x, weights, load_sem)
    loading.start()

    swap_wait(g_own, end, g_send, g_recv)
    sums[...] = jnp.zeros_like(sums)

    def back_pair(j, _):
        cols = lane_block(j)
        ex = pair_matrix(j)
        skip = d_skip[:, cols]
        raw = x_raw[:, cols].astype(F32)
        halos, grads = [], None
        d_steps, dots, end_rows = [], [], []
        skip_sum = jnp.zeros((1, 128), F32)
        for b in range(SEQS):
            span = slice(TOK * b, TOK * (b + 1))
            r_lanes = r_wide[span, cols]
            dt_lanes = dt_wide[span, cols]
            last = r_lanes[TOK - 1 : TOK, :]
            grown = jnp.exp(r_lanes)
            to_end = jnp.exp(last - r_lanes)
            before = jnp.concatenate([start[2 * j, b], start[2 * j + 1, b]], axis=0)
            after = jnp.concatenate([end[2 * j, b], end[2 * j + 1, b]], axis=0)
            x = xc[span, cols].astype(F32)
            dy = d_y[span, cols].astype(F32)
            stepped = (dt_lanes * x).astype(BF16).astype(F32)
            carried = to_end * mm(bcc[span, 0:STATE], after, NT)
            d_step = d_stepped[span, cols] + carried
            dots.append(stepped * d_step)
            d_x = dt_lanes * d_step + skip * dy
            d_steps.append(x * d_step)
            inner = lane_sums(before.astype(F32) * after.astype(F32))
            end_rows.append(jnp.sum(stepped * carried, axis=0, keepdims=True) + jnp.exp(last) * inner)
            d_bc[span, STATE:] += mm((grown * dy).astype(BF16), before, NN)
            d_bc[span, 0:STATE] += mm((to_end * stepped).astype(BF16), after, NN)
            skip_sum = skip_sum + jnp.sum(dy * x, axis=0, keepdims=True)
            d_pad, d_taps, d_bias = conv_back(padded_of(raw, b), taps_x[:, cols], bias_x[:, cols], d_x)
            d_x_raw[span, cols] = d_pad[HALO:, :].astype(BF16)
            halos.append(d_pad[0:HALO, :])
            found = [*d_taps, d_bias]
            grads = found if grads is None else [g + p for g, p in zip(grads, found)]
        d_x_raw[ROWS:, cols] = jnp.concatenate(halos, axis=0).astype(BF16)
        g_x[:, cols] = jnp.concatenate([*grads, jnp.zeros((8 - TAPS - 1, 128), F32)], axis=0)
        few = jnp.concatenate([*end_rows, skip_sum, jnp.zeros((5, 128), F32)], axis=0)
        sums[...] += head_sums(jnp.concatenate([*d_steps, *dots, few], axis=0), ex)
        return 0

    wide_coming = []
    for quarter in range(4):
        lax.fori_loop(4 * quarter, 4 * quarter + 4, back_pair, 0)
        cols = slice(512 * quarter, 512 * (quarter + 1))
        wide_coming.append(
            copy(d_x_raw.at[:, cols], sib_wide.at[:, cols], sib_send.at[6 + quarter], sib_recv.at[6 + quarter], sibling)
        )
    raw = bc_raw[...].astype(F32)
    halos, grads = [], None
    for b in range(SEQS):
        span = slice(TOK * b, TOK * (b + 1))
        d_pad, d_taps, d_bias = conv_back(padded_of(raw, b), taps_bc[...], bias_bc[...], d_bc[span, :])
        d_small[span, 0 : 2 * STATE] = d_pad[HALO:, :].astype(BF16)
        halos.append(d_pad[0:HALO, :])
        found = [*d_taps, d_bias]
        grads = found if grads is None else [g + p for g, p in zip(grads, found)]
    d_small[ROWS:, 0 : 2 * STATE] = jnp.concatenate(halos, axis=0).astype(BF16)
    d_small[ROWS:, 2 * STATE :] = jnp.zeros((ALL - ROWS, SMALL - 2 * STATE), BF16)
    g_bc[...] = jnp.concatenate([*grads, jnp.zeros((8 - TAPS - 1, 2 * STATE), F32)], axis=0)
    rate = -jnp.exp(a_log[...])
    tri = causal_mask().astype(F32)
    is_last = iota((TOK, HEADS), 0) == TOK - 1
    bias_sum = jnp.zeros((1, HEADS), F32)
    log_sum = jnp.zeros((1, HEADS), F32)
    for b in range(SEQS):
        span = slice(TOK * b, TOK * (b + 1))
        step = dt[span, :]
        d_dt = sums[span, :]
        d_r = row_dot[span, :] - sums[ROWS + TOK * b : ROWS + TOK * (b + 1), :]
        d_r = d_r + jnp.where(is_last, sums[2 * ROWS + b : 2 * ROWS + b + 1, :], 0.0)
        d_log = mm(tri, d_r, TN, HIGHEST)
        d_pre = (d_dt + rate * d_log) * jax.nn.sigmoid(dt_raw[span, :].astype(F32) + dt_bias[...])
        d_small[span, 2 * STATE :] = jnp.concatenate(
            [d_pre, jnp.zeros((TOK, SMALL - 2 * STATE - HEADS), F32)], axis=1
        ).astype(BF16)
        bias_sum = bias_sum + jnp.sum(d_pre, axis=0, keepdims=True)
        log_sum = log_sum + jnp.sum(d_log * step, axis=0, keepdims=True) * rate
    g_heads[...] = jnp.concatenate(
        [bias_sum, log_sum, sums[2 * ROWS + 2 : 2 * ROWS + 3, :], jnp.zeros((5, HEADS), F32)], axis=0
    )
    small_coming = copy(d_small, sib_small, sib_send.at[10], sib_recv.at[10], sibling)

    add_stage(0, 0)
    add_stage(0, 1)

    def tile_x(n, _):
        cols = lane_block(n, 256)
        res = mm(keep_n[...], d_x_raw[:, cols], NN) + mm(next_n[...], sib_wide[:, cols], NN)
        for y in range(4):
            for k in range(2):
                block = res[128 * y : 128 * y + 128, 128 * k : 128 * k + 128].astype(BF16)
                x, z = n // 2, (n % 2) * 2 + k
                parts_xa[x, y, z] = block[0:48]
                parts_xb[y, z, x] = block[48:96]
                parts_xc[z, x, y, 0:32] = block[96:128]
        return 0

    for quarter in range(4):
        wide_coming[quarter].wait_recv()
        lax.fori_loop(2 * quarter, 2 * quarter + 2, tile_x, 0)
    send_stage(0, 2, parts_xa)
    send_stage(0, 3, parts_xb)
    small_coming.wait_recv()
    res = mm(keep_n[...], d_small[...], NN) + mm(next_n[...], sib_small[...], NN)
    for y in range(4):
        for z in range(4):
            row = 128 * y + EXTRA * z
            for k in range(3):
                parts_xc[z, k, y, 32:] = res[row : row + EXTRA, 128 * k : 128 * k + 128].astype(BF16)
            parts_xc[z, 3, y, 32:] = jnp.zeros((EXTRA, 128), BF16)
    send_stage(0, 4, parts_xc)

    loading.wait()
    d_normed[ROWS:, :] = jnp.zeros((ALL - ROWS, d_normed.shape[1]), F32)
    for n in range(4):
        cols = slice(256 * n, 256 * (n + 1))
        d_normed[:, cols] += mm(d_x_raw[...], weights[cols, :], NT) + mm(d_small[...], full_small[cols, :], NT)
    halo_out[...] = d_normed[ROWS:, :]
    halo = pltpu.make_async_remote_copy(
        src_ref=halo_out, dst_ref=halo_in, send_sem=halo_sem.at[0], recv_sem=halo_sem.at[1],
        device_id={"seq": lax.rem(me + HEADS - 1, HEADS)}, device_id_type=pl.DeviceIdType.MESH,
    )
    halo.start()
    started.append(halo)
    add_stage(1, 0)
    add_stage(1, 1)
    halo.wait_recv()
    inner = jnp.where(me == HEADS - 1, 0.0, 1.0)
    for b in range(SEQS):
        near = slice(TOK * (b + 1) - HALO, TOK * (b + 1))
        d_normed[near, :] += inner * halo_in[HALO * b : HALO * (b + 1), :]
    g_in = jnp.zeros((1, d_normed.shape[1]), F32)
    for n in range(4):
        span = slice(64 * n, 64 * (n + 1))
        hidden = layer_in[span, :].astype(F32)
        inv = lax.rsqrt(jnp.mean(hidden * hidden, axis=1, keepdims=True) + EPS)
        unit = hidden * inv
        grad = d_normed[span, :]
        g_in = g_in + jnp.sum(grad * unit, axis=0, keepdims=True)
        pulled = grad * gain_in[...]
        d_hidden = inv * (pulled - unit * jnp.mean(pulled * unit, axis=1, keepdims=True))
        input_grad[span, :] = cot[span, :].astype(F32) + d_hidden

    few_axes = ("core", "x", "z", "y")
    rest = jnp.concatenate(
        [
            g_bc[...], jnp.concatenate([g_heads[...], jnp.zeros((8, 128 - HEADS), F32)], axis=1),
            jnp.zeros((8, INNER - 2 * STATE - 128), F32),
        ],
        axis=1,
    )
    wide_in = jnp.concatenate([g_in, jnp.zeros((1, INNER - g_in.shape[1]), F32)], axis=1)
    few = jnp.concatenate([g_x[...], g_norm[...], wide_in, rest[0 : TAPS + 1], jnp.zeros((1, INNER), F32)], axis=0)

    few_coming = [None]

    def few_start(stage, value):
        few_own[stage] = value.astype(BF16)
        axis = few_axes[stage]
        few_got[stage, at[axis]] = few_own[stage]
        few_coming[0] = [
            copy(
                few_own.at[stage], few_got.at[stage, at[axis]],
                few_send.at[stage, d], few_recv.at[stage, d], to,
            )
            for d, to in enumerate(peers(at, axis))
        ]

    def few_sum(stage):
        for one in few_coming[0]:
            one.wait_recv()
        value = few_got[stage, 0].astype(F32)
        for i in range(1, 2 if stage == 0 else 4):
            value = value + few_got[stage, i].astype(F32)
        return value

    few_start(0, few)
    last_add(0)
    last_add(1)
    few_start(1, few_sum(0))
    for which in (2, 3, 4):
        add_stage(0, which)
    gather_next(1, 0)
    gather_next(1, 1)
    few_start(2, few_sum(1))
    for which in (2, 3, 4):
        add_stage(1, which)
    gather_next(2, 0)
    gather_next(2, 1)
    few_start(3, few_sum(2))
    for which in (2, 3, 4):
        last_add(which)
    vector[...] = few_sum(3)
    for stage in (1, 2):
        for which in (2, 3, 4):
            gather_next(stage, which)
    for which in range(SETS):
        arrived(which)
    for one in started:
        one.wait_send()
    swap_sent(v, v_all, v_send, v_recv)
    swap_sent(g_own, end, g_send, g_recv)


def tail(*args):
    vmem = pl.BlockSpec(memory_space=pltpu.VMEM)
    hbm = pl.BlockSpec(memory_space=pl.ANY)
    specs = [vmem] * len(args)
    specs[1] = pl.BlockSpec(memory_space=pltpu.SMEM)
    specs[-3] = specs[-2] = hbm
    width = args[-2].shape[0]
    dims = {"x": 4, "z": 4, "l": 2}
    out_shape = [
        jax.ShapeDtypeStruct((*(dims[a] for a in reversed(GATHER[i])), PIECE_ROWS[i], 128), BF16) for i in range(SETS)
    ]
    out_shape += [jax.ShapeDtypeStruct((ROWS, width), F32), jax.ShapeDtypeStruct(VECTOR, F32)]

    def bufs(*lead):
        return [pltpu.VMEM((*lead, PIECE_ROWS[i], 128), BF16) for i in range(SETS)]

    def sems(*shape):
        return [pltpu.SemaphoreType.DMA(shape)] * 2

    scratch = [
        pltpu.VMEM((width, INNER), BF16), *[pltpu.VMEM(STATES_SHAPE, BF16)] * 3, pltpu.VMEM((ROWS, INNER), F32),
        *[pltpu.VMEM((SEQS, TOK, TOK), F32)] * 2, pltpu.VMEM((ROWS, 2 * STATE), F32),
        pltpu.VMEM((2 * ROWS + 8, HEADS), F32), pltpu.VMEM((ALL, INNER), BF16), pltpu.VMEM((ALL, SMALL), BF16),
        pltpu.VMEM((8, INNER), F32), pltpu.VMEM((8, 2 * STATE), F32), pltpu.VMEM((8, HEADS), F32),
        pltpu.VMEM((ALL, width), F32), *[pltpu.VMEM((SEQS * HALO, width), F32)] * 2,
        pltpu.VMEM((4, *VECTOR), BF16), pltpu.VMEM((4, 4, *VECTOR), BF16),
        *[pltpu.VMEM((512, ALL), BF16), pltpu.VMEM((1024, ROWS), BF16)] * 2,
        pltpu.VMEM((2, ALL, 256), BF16), pltpu.VMEM((ROWS, INNER), BF16), pltpu.VMEM((2, ROWS, 512), BF16),
        pltpu.VMEM((ROWS, width), BF16), pltpu.VMEM((ALL, INNER), BF16), pltpu.VMEM((ALL, SMALL), BF16),
        *bufs(4, 4, 4), *bufs(3, 4, 4), *bufs(4, 4), *bufs(3, 4), *bufs(4), *bufs(3),
        *sems(HEADS), *sems(HEADS), *sems(11), *sems(SETS, 3, 3), *sems(SETS, 3, 3), *sems(4, 3),
        pltpu.SemaphoreType.DMA((2,)), pltpu.SemaphoreType.DMA,
    ]
    return pl.pallas_call(
        tail_kernel,
        out_shape=out_shape,
        in_specs=specs,
        out_specs=[vmem] * len(out_shape),
        scratch_shapes=scratch,
        compiler_params=pltpu.CompilerParams(
            vmem_limit_bytes=62 * 1024 * 1024, collective_id=1, has_side_effects=True
        ),
        cost_estimate=pl.CostEstimate(flops=int(8e9), bytes_accessed=int(4e7), transcendentals=0),
    )(*args)


def unpack_kernel(sum_z, sum_out, sum_xa, sum_xb, sum_xc, out_z, out_x, out_out, out_extra):
    for low in range(2):
        base = PIECE * low
        out_z[base : base + PIECE, :] = sum_z[0, 0, low].astype(F32)
        out_x[base : base + 48, :] = sum_xa[0, 0, low].astype(F32)
        out_x[base + 48 : base + 96, :] = sum_xb[0, 0, low].astype(F32)
        out_x[base + 96 : base + 128, :] = sum_xc[low, 0, 0, 0:32, :].astype(F32)
        out_out[low, 0] = sum_out[low, 0, 0].astype(F32)
        out_extra[0, low] = sum_xc[low, 0, 0, 32:, :].astype(F32)


def unpack(*gathered):
    specs = []
    for i in range(SETS):
        def where(n, order=GATHER[i]):
            return tuple({"x": n // 4, "z": n % 4, "l": 0}[a] for a in reversed(order)) + (0, 0)

        block = tuple(2 if a == "l" else 1 for a in reversed(GATHER[i])) + (PIECE_ROWS[i], 128)
        specs.append(pl.BlockSpec(block, where))
    return call(
        unpack_kernel,
        [((2 * PIECE, INNER), F32), ((2 * PIECE, INNER), F32), ((2, 2, PIECE, 8 * 128), F32), ((4, 2, 4 * EXTRA, 128), F32)],
        [
            lanes(2 * PIECE), lanes(2 * PIECE),
            pl.BlockSpec((2, 1, PIECE, 128), lambda i: (0, i // 8, 0, ((i // 4) % 2) * 4 + i % 4)),
            pl.BlockSpec((1, 2, EXTRA, 128), lambda i: (i // 4, 0, i % 4, 0)),
        ],
        specs,
    )(*gathered)


def gather_kernel(
    w_x, w_small, own, full_x, full_small, params, send, recv, here, own_send, own_recv,
):
    at = position()
    sibling = peers(at, "core")[0]
    partner = moved(at, "y", 3 - at["y"])
    everyone = [sibling, partner] + [p for axis in ("x", "z", "l") for p in peers(at, axis)]
    greet(everyone)
    started = []

    def copy(src, dst, which, to, sems=(send, recv)):
        one = pltpu.make_async_remote_copy(
            src_ref=src, dst_ref=dst, send_sem=sems[0].at[which], recv_sem=sems[1].at[which],
            device_id=device(to), device_id_type=pl.DeviceIdType.MESH,
        )
        one.start()
        started.append(one)
        return one

    high = at["y"] // 2
    mine, opposite = high * 2 + at["core"], (1 - high) * 2 + at["core"]
    half = INNER // 2
    flows = ((full_x, 0, half, "x", "z"), (full_x, half, half, "z", "x"), (full_small, 0, SMALL, "x", "z"))

    def view(ref, shard, row, count, first, size):
        row = pl.multiple_of(row, 16)
        if shard is None:
            return ref.at[pl.ds(row, count), first : first + size]
        return ref.at[shard, pl.ds(row, count), first : first + size]

    arriving = []
    for i, (ref, first, size, a, b) in enumerate(flows):
        row = (at[b] * 4 + at[a]) * 16
        src = w_small if i == 2 else w_x
        arriving.append(copy(view(src, None, row, 16, first, size), view(ref, mine, row, 16, first, size), i, partner))
    params_here = pltpu.make_async_copy(own, params.at[at["z"], at["x"], at["l"]], here.at[2])
    local = [
        pltpu.make_async_copy(w_x, full_x.at[mine], here.at[0]),
        pltpu.make_async_copy(w_small, full_small.at[mine], here.at[1]),
        params_here,
    ]
    for one in local:
        one.start()
    last = [
        copy(w_x, full_x.at[mine], 24, sibling),
        copy(w_small, full_small.at[mine], 25, sibling),
    ]
    params_here.wait()

    def share(stage):
        axis = ("l", "x", "z")[stage]
        ref = params.at[(at["z"], at["x"], at["l"])[: 3 - stage]]
        return [copy(ref, ref, 3 * stage + d, to, (own_send, own_recv)) for d, to in enumerate(peers(at, axis))]

    shared = share(0)
    second = []
    for i, (ref, first, size, a, b) in enumerate(flows):
        arriving[i].wait_recv()
        piece = view(ref, opposite, (at[b] * 4 + at[a]) * 16, 16, first, size)
        second.append([copy(piece, piece, 3 + 3 * i + d, to) for d, to in enumerate(peers(at, a))])
    for one in shared:
        one.wait_recv()
    shared = share(1)
    third = []
    for i, (ref, first, size, a, b) in enumerate(flows):
        for one in second[i]:
            one.wait_recv()
        block = view(ref, opposite, at[b] * 64, 64, first, size)
        third.append([copy(block, block, 12 + 3 * i + d, to) for d, to in enumerate(peers(at, b))])
        last.append(copy(block, block, 21 + i, sibling))
    for one in shared:
        one.wait_recv()
    shared = share(2)
    for i, (ref, first, size, a, b) in enumerate(flows):
        for d in range(3):
            third[i][d].wait_recv()
            block = view(ref, opposite, lax.rem(at[b] + 3 - d, 4) * 64, 64, first, size)
            last.append(copy(block, block, 26 + 3 * i + d, sibling))
    for one in last + shared:
        one.wait_recv()
    for one in local[:2]:
        one.wait()
    for one in started:
        one.wait_send()


def gather_weights(w_x, w_small, own):
    vmem = pl.BlockSpec(memory_space=pltpu.VMEM)
    return pl.pallas_call(
        gather_kernel,
        out_shape=[
            jax.ShapeDtypeStruct((4, *w_x.shape), BF16),
            jax.ShapeDtypeStruct((4, *w_small.shape), BF16),
            jax.ShapeDtypeStruct((4, 4, 2, 8, 128), F32),
        ],
        in_specs=[vmem] * 3,
        out_specs=[vmem] * 3,
        scratch_shapes=[
            pltpu.SemaphoreType.DMA((35,)), pltpu.SemaphoreType.DMA((35,)), pltpu.SemaphoreType.DMA((3,)),
            pltpu.SemaphoreType.DMA((9,)), pltpu.SemaphoreType.DMA((9,)),
        ],
        compiler_params=pltpu.CompilerParams(
            vmem_limit_bytes=VMEM_LIMIT, collective_id=2, has_side_effects=True
        ),
        cost_estimate=pl.CostEstimate(flops=int(1e6), bytes_accessed=int(4e7), transcendentals=0),
    )(w_x, w_small, own)


def swap(values):
    return lax.all_to_all(values, "seq", split_axis=0, concat_axis=0, tiled=True)


def gather_rows(shard):
    return lax.all_gather(shard, "wshard", axis=0, tiled=True)


def shards(
    layer_in, gain_in, w_z, w_x, w_bc, w_dt, conv_x_weight, conv_x_bias, conv_bc_weight, conv_bc_bias,
    dt_bias, a_log, d_skip, gain_norm, w_out, cotangent,
):
    width = layer_in.shape[2]
    chunks = lax.axis_size("seq")
    place = lax.axis_index("seq")
    earlier = lax.ppermute(layer_in[:, TOK - (TAPS - 1) :, :], "seq", [(i, i + 1) for i in range(chunks - 1)])
    full_z = gather_rows(w_z)
    full_out = gather_rows(w_out)
    own = jnp.concatenate([conv_x_weight.reshape(-1), conv_x_bias, dt_bias, a_log, d_skip, jnp.zeros((701,), F32)])
    small = jnp.concatenate([w_bc, w_dt, jnp.zeros((w_bc.shape[0], SMALL - 2 * STATE - HEADS), BF16)], axis=1)
    full_x, full_small, params = gather_weights(w_x, small, own.reshape(8, 128))
    full_x = full_x.reshape(width, INNER)
    full_small = full_small.reshape(width, SMALL)
    params = params.reshape(HEADS, -1)
    taps_x = params[:, : TAPS * HEAD].reshape(HEADS, TAPS, HEAD).swapaxes(0, 1).reshape(TAPS, INNER)
    bias_x = params[:, TAPS * HEAD : (TAPS + 1) * HEAD].reshape(1, INNER)
    bias_dt, log_a, skip = (params[:, (TAPS + 1) * HEAD + i].reshape(1, HEADS) for i in range(3))
    bias_bc = conv_bc_bias.reshape(1, -1)
    skip_wide = jnp.repeat(skip, HEAD, axis=1)

    hidden = layer_in.astype(F32).reshape(ROWS, width)
    upstream = cotangent.reshape(ROWS, width)
    halo = jnp.pad(earlier, ((0, 0), (HALO - (TAPS - 1), 0), (0, 0))).reshape(SEQS * HALO, width).astype(F32)
    tokens = jnp.concatenate([hidden, halo], axis=0)
    inv = lax.rsqrt(jnp.mean(tokens * tokens, axis=-1, keepdims=True) + EPS)
    normed = (tokens * inv * gain_in[None, :]).astype(BF16)

    x_raw = mm(normed, full_x, NN).astype(BF16)
    small_raw = mm(normed, full_small, NN).astype(BF16)
    bc_raw, dt_raw = small_raw[:, : 2 * STATE], small_raw[:, 2 * STATE : 2 * STATE + HEADS]
    xc, bcc, dt, r, u, dt_wide, r_wide, r_rows = front(x_raw, bc_raw, dt_raw, taps_x, bias_x, conv_bc_weight, bias_bc, bias_dt, log_a)
    decay = jnp.exp(swap(r[TOK - 1 :: TOK].T))
    u_all = swap(u)
    y_in = inside(xc, bcc, dt_wide, r_wide, r_rows)
    gate = mm(normed[:ROWS], full_z, NN)
    d_mixed = mm(upstream, full_out, NT)
    start = swap(states(decay, u_all, False))
    mixed, d_y, d_gate, v, g_norm, row_dot = middle(
        y_in, xc, bcc, r_wide, start, skip_wide, gate, d_mixed, gain_norm.reshape(1, INNER)
    )
    layer_out = (hidden + mm(mixed, full_out, NN)).astype(BF16).reshape(SEQS, TOK, width)
    *gathered, input_grad, total = tail(
        v, decay, xc, d_y, bcc, dt, dt_wide, r_wide, r_rows, x_raw, start, bc_raw, dt_raw, row_dot,
        taps_x, bias_x, conv_bc_weight, bias_bc, bias_dt, log_a, skip_wide, g_norm,
        normed, d_gate, mixed, upstream, layer_in.reshape(ROWS, width), gain_in.reshape(1, width),
        full_z, full_x, full_small,
    )
    input_grad = input_grad.reshape(SEQS, TOK, width)
    grad_w_z, grad_w_x, grad_w_out, extra = unpack(*gathered)
    grad_w_out = grad_w_out.reshape(4 * PIECE, width)
    extra = extra.reshape(4, 2 * PIECE, 128)
    grad_w_bc = jnp.concatenate([extra[0], extra[1]], axis=1)
    grad_w_dt = extra[2][:, :HEADS]
    s_x = lax.dynamic_slice(total[: TAPS + 1], (0, place * HEAD), (TAPS + 1, HEAD))
    s_norm, s_in = total[8], total[9, :width]
    s_bc = total[10 : 10 + TAPS + 1, : 2 * STATE]
    s_heads = lax.dynamic_slice(total[10:13], (0, 2 * STATE + place), (3, 1))
    return (
        layer_out, input_grad, s_in, grad_w_z, grad_w_x, grad_w_bc, grad_w_dt,
        s_x[:TAPS], s_x[TAPS], s_bc[:TAPS], s_bc[TAPS], s_heads[0], s_heads[1], s_heads[2], s_norm, grad_w_out,
    )


def solution(mesh):
    rows, heads = P("wshard", None), P("seq")
    tokens = P("wshard", "seq", None)
    return jax.shard_map(
        shards,
        mesh=mesh,
        in_specs=(
            tokens, P(), rows, rows, rows, rows, P(None, "seq"), heads, P(), P(), heads, heads, heads, P(), rows, tokens,
        ),
        out_specs=(
            tokens, tokens, P(), rows, rows, rows, rows, P(None, "seq"), heads, P(), P(), heads, heads, heads, P(), rows,
        ),
        check_vma=False,
    )
```

```python
import functools

import jax
import jax.numpy as jnp
from jax import lax
from jax.experimental import pallas as pl
from jax.experimental.pallas import tpu as pltpu
from jax.sharding import PartitionSpec as P

F32 = jnp.float32
BF16 = jnp.bfloat16
EPS = 1e-05
HIGHEST = lax.Precision.HIGHEST
HEADS = 32
HEAD = 64
STATE = 128
TOK = 128
SEQS = 2
ROWS = SEQS * TOK
HALO = 8
ALL = ROWS + SEQS * HALO
PAIRS = HEADS // 2
INNER = HEADS * HEAD
TAPS = 4


def mm(a, b, dims, precision=None):
    return lax.dot_general(a, b, ((dims[0], dims[1]), ((), ())), precision=precision, preferred_element_type=F32)


NN = ((1,), (0,))
NT = ((1,), (1,))
TN = ((0,), (0,))


def iota(shape, dim):
    return lax.broadcasted_iota(jnp.int32, shape, dim)


def pair_matrix(pair):
    upper = (iota((HEADS, 128), 1) >= HEAD).astype(jnp.int32)
    return (iota((HEADS, 128), 0) == 2 * pair + upper).astype(F32)


def pair_rows(pair):
    return (iota((8, HEADS), 1) == 2 * pair + iota((8, HEADS), 0)).astype(F32)


def head_sums(values, ex):
    high = values.astype(BF16)
    low = (values - high.astype(F32)).astype(BF16)
    ex = ex.astype(BF16)
    return mm(jnp.concatenate([high, low], axis=1), jnp.concatenate([ex, ex], axis=1), NT)


def lane_sums(values):
    high = values.astype(BF16)
    low = (values - high.astype(F32)).astype(BF16)
    return mm(jnp.ones((8, 256), BF16), jnp.concatenate([high, low], axis=1), NT)[0:1, :]


def causal_mask():
    return iota((TOK, TOK), 0) >= iota((TOK, TOK), 1)


def shifted(padded, k):
    back = TAPS - 1 - k
    if back:
        padded = pltpu.roll(padded, back, 0)
    return padded[HALO:, :]


def padded_of(rows, b):
    return jnp.concatenate(
        [rows[ROWS + HALO * b : ROWS + HALO * (b + 1), :], rows[TOK * b : TOK * (b + 1), :]], axis=0
    )


def conv_pre(padded, taps, bias):
    total = bias
    for k in range(TAPS):
        total = total + taps[k : k + 1, :] * shifted(padded, k)
    return total


def conv_back(padded, taps, bias, grad):
    pre = conv_pre(padded, taps, bias)
    sig = jax.nn.sigmoid(pre)
    d_pre = grad * (sig * (1.0 + pre * (1.0 - sig)))
    low = jnp.concatenate([jnp.zeros((HALO, d_pre.shape[1]), F32), d_pre], axis=0)
    d_pad = taps[TAPS - 1 : TAPS, :] * low
    for k in range(TAPS - 1):
        d_pad = d_pad + taps[k : k + 1, :] * pltpu.roll(low, HALO + TOK - (TAPS - 1 - k), 0)
    d_taps = [jnp.sum(d_pre * shifted(padded, k), axis=0, keepdims=True) for k in range(TAPS)]
    return d_pad, d_taps, jnp.sum(d_pre, axis=0, keepdims=True)


def block_diagonal(pair_values):
    first = iota(pair_values.shape, 1) < HEAD
    zero = jnp.zeros_like(pair_values)
    return jnp.concatenate(
        [jnp.where(first, pair_values, zero), jnp.where(first, zero, pair_values)], axis=0
    )


def decay_pair(r_lanes, r_rows):
    mask = causal_mask()
    out = []
    for q in range(2):
        spread = r_lanes[:, HEAD * q : HEAD * q + 1] - r_rows[q : q + 1, :]
        out.append(jnp.exp(jnp.where(mask, spread, -1e30)))
    return out


def whole(shape):
    return pl.BlockSpec(shape, lambda *_: (0,) * len(shape))


def lanes(rows):
    return pl.BlockSpec((rows, 128), lambda j: (0, j))


STATES_SHAPE = (HEADS, SEQS, HEAD, STATE)
VMEM_LIMIT = 48 * 1024 * 1024


def call(kernel, outs, out_specs, in_specs, grid=(PAIRS,), scratch=(), cost=None):
    return pl.pallas_call(
        kernel,
        grid=grid,
        out_shape=[jax.ShapeDtypeStruct(s, d) for s, d in outs],
        in_specs=in_specs,
        out_specs=out_specs,
        scratch_shapes=scratch,
        compiler_params=pltpu.CompilerParams(
            vmem_limit_bytes=VMEM_LIMIT, dimension_semantics=("arbitrary",) * len(grid)
        ),
        cost_estimate=cost or pl.CostEstimate(flops=int(1e9), bytes_accessed=int(1e7), transcendentals=0),
    )


def chunk_copy(src, dst, send, recv, to, slot):
    return pltpu.make_async_remote_copy(
        src_ref=src.at[to], dst_ref=dst.at[slot], send_sem=send.at[to], recv_sem=recv.at[slot],
        device_id={"seq": to}, device_id_type=pl.DeviceIdType.MESH,
    )


def each_other(me, step):
    def go(d, _):
        step(lax.rem(me + d, HEADS))
        return 0

    lax.fori_loop(1, HEADS, go, 0)


def greet_chunks(me):
    barrier = pltpu.get_barrier_semaphore()
    each_other(
        me,
        lambda other: pl.semaphore_signal(
            barrier, inc=1, device_id={"seq": other}, device_id_type=pl.DeviceIdType.MESH
        ),
    )
    return barrier


def lane_block(j, size=128):
    return pl.ds(pl.multiple_of(j * size, size), size)


def head_kernel(
    x_raw, bc_raw, dt_raw, taps_x, bias_x, taps_bc, bias_bc, dt_bias, a_log,
    xc, bcc, dt, dt_wide, r_wide, r_rows, y_in, start, decay,
    r, scores, u, u_all, own_decay, s_own, u_send, u_recv, e_send, e_recv, s_send, s_recv,
):
    me = lax.axis_index("seq")
    barrier = greet_chunks(me)
    raw = bc_raw[...].astype(F32)
    dt[...] = jax.nn.softplus(dt_raw[0:ROWS, :].astype(F32) + dt_bias[...])
    tri = causal_mask().astype(F32)
    rates = dt[...] * (-jnp.exp(a_log[...]))
    for b in range(SEQS):
        span = slice(TOK * b, TOK * (b + 1))
        pre = conv_pre(padded_of(raw, b), taps_bc[...], bias_bc[...])
        bcc[span, :] = (pre * jax.nn.sigmoid(pre)).astype(BF16)
        r[span, :] = mm(tri, rates[span, :], NN, HIGHEST)
        scores[b] = mm(bcc[span, STATE:], bcc[span, 0:STATE], NT)
    first = iota((8, 128), 1) < HEAD
    pl.semaphore_wait(barrier, HEADS - 1)

    def front_pair(i, _):
        j = lax.rem(me // 2 + i, PAIRS)
        cols = lane_block(j)
        raw = x_raw[:, cols].astype(F32)
        both = mm(jnp.concatenate([r[...], dt[...]], axis=0), pair_matrix(j), NN, HIGHEST)
        r_wide[:, cols] = both[0:ROWS, :]
        dt_wide[:, cols] = both[ROWS:, :]
        r_rows[j] = mm(pair_rows(j), r[...], NT, HIGHEST)
        ends = []
        for b in range(SEQS):
            span = slice(TOK * b, TOK * (b + 1))
            pre = conv_pre(padded_of(raw, b), taps_x[:, cols], bias_x[:, cols])
            low = (pre * jax.nn.sigmoid(pre)).astype(BF16)
            xc[span, cols] = low
            r_lanes = both[span, :]
            dt_lanes = both[ROWS + TOK * b : ROWS + TOK * (b + 1), :]
            last = r_lanes[TOK - 1 : TOK, :]
            ends.append(last)
            scaled = (jnp.exp(last - r_lanes) * (dt_lanes * low.astype(F32))).astype(BF16)
            state = mm(scaled, bcc[span, 0:STATE], TN).astype(BF16)
            u[2 * j, b] = state[0:HEAD, :]
            u[2 * j + 1, b] = state[HEAD:, :]
        shrink = jnp.exp(jnp.concatenate([*ends, jnp.zeros((8 - SEQS, 128), F32)], axis=0))
        turned = pltpu.roll(shrink, HEAD, 1)
        own_decay[2 * j] = jnp.where(first, shrink, turned)
        own_decay[2 * j + 1] = jnp.where(first, turned, shrink)
        for q in range(2):
            to = 2 * j + q

            @pl.when(to != me)
            def _():
                chunk_copy(u, u_all, u_send, u_recv, to, me).start()
                chunk_copy(own_decay, decay, e_send, e_recv, to, me).start()

        return 0

    lax.fori_loop(0, PAIRS, front_pair, 0)
    u_all[me] = u[me]
    decay[me] = own_decay[me]

    def inside_pair(j, _):
        cols = lane_block(j)
        for b in range(SEQS):
            span = slice(TOK * b, TOK * (b + 1))
            one, two = decay_pair(r_wide[span, cols], r_rows[j, :, span])
            both = jnp.concatenate([scores[b] * one, scores[b] * two], axis=1).astype(BF16)
            stepped = (dt_wide[span, cols] * xc[span, cols].astype(F32)).astype(BF16)
            y_in[span, cols] = mm(both, block_diagonal(stepped), NN)
        return 0

    lax.fori_loop(0, 6, inside_pair, 0)
    each_other(me, lambda other: chunk_copy(u, u_all, u_send, u_recv, other, other).wait_recv())
    each_other(me, lambda other: chunk_copy(own_decay, decay, e_send, e_recv, other, other).wait_recv())

    def chunk_step(c, carry):
        after = []
        for b in range(SEQS):
            s_own[c, b] = carry[b].astype(BF16)
            after.append(decay[c, b : b + 1, :] * carry[b] + u_all[c, b].astype(F32))
        return tuple(after)

    lax.fori_loop(0, HEADS, chunk_step, tuple(jnp.zeros((HEAD, STATE), F32) for _ in range(SEQS)))
    each_other(me, lambda other: chunk_copy(s_own, start, s_send, s_recv, other, me).start())
    start[me] = s_own[me]
    lax.fori_loop(6, PAIRS, inside_pair, 0)
    each_other(me, lambda other: chunk_copy(s_own, start, s_send, s_recv, other, other).wait_recv())
    each_other(me, lambda other: chunk_copy(u, u_all, u_send, u_recv, other, me).wait_send())
    each_other(me, lambda other: chunk_copy(own_decay, decay, e_send, e_recv, other, me).wait_send())
    each_other(me, lambda other: chunk_copy(s_own, start, s_send, s_recv, other, me).wait_send())


def head(*args):
    vmem = pl.BlockSpec(memory_space=pltpu.VMEM)
    outs = [
        ((ROWS, INNER), BF16), ((ROWS, 2 * STATE), BF16), ((ROWS, HEADS), F32), ((ROWS, INNER), F32), ((ROWS, INNER), F32),
        ((PAIRS, 8, ROWS), F32), ((ROWS, INNER), F32), (STATES_SHAPE, BF16), ((HEADS, 8, 128), F32),
    ]
    return pl.pallas_call(
        head_kernel,
        out_shape=[jax.ShapeDtypeStruct(s, d) for s, d in outs],
        in_specs=[vmem] * len(args),
        out_specs=[vmem] * len(outs),
        scratch_shapes=[
            pltpu.VMEM((ROWS, HEADS), F32), pltpu.VMEM((SEQS, TOK, TOK), F32), *[pltpu.VMEM(STATES_SHAPE, BF16)] * 2,
            pltpu.VMEM((HEADS, 8, 128), F32), pltpu.VMEM(STATES_SHAPE, BF16),
            *[pltpu.SemaphoreType.DMA((HEADS,))] * 6,
        ],
        compiler_params=pltpu.CompilerParams(
            vmem_limit_bytes=VMEM_LIMIT, collective_id=3, has_side_effects=True
        ),
        cost_estimate=pl.CostEstimate(flops=int(2e9), bytes_accessed=int(2e7), transcendentals=0),
    )(*args)


WIDE = 512
QUADS = INNER // WIDE


def fold(values):
    return sum((values[:, 128 * i : 128 * (i + 1)] for i in range(1, WIDE // 128)), values[:, 0:128])


def middle_kernel(
    y_in, xc, bcc, r, start, d_skip, gate, d_mixed, gain,
    mixed, d_y, d_gate, own, d_gain, row_dot,
    y_all, square, cross, scale, slope,
):
    phase = pl.program_id(0)
    quad = pl.program_id(1)
    ex = (iota((HEADS, WIDE), 0) == 8 * quad + (iota((HEADS, WIDE), 1) >> 6)).astype(F32)
    skip = d_skip[...]
    z = gate[...]
    sig = jax.nn.sigmoid(z)
    pulled = d_mixed[...] * gain[...]

    @pl.when(phase == 0)
    def _():
        @pl.when(quad == 0)
        def _():
            square[...] = jnp.zeros_like(square)
            cross[...] = jnp.zeros_like(cross)

        for b in range(SEQS):
            span = slice(TOK * b, TOK * (b + 1))
            before = jnp.concatenate([start[h, b] for h in range(8)], axis=0)
            grown = jnp.exp(r[span, :])
            y_all[quad, span, :] = y_in[span, :] + grown * mm(bcc[span, STATE:], before, NT)
        y = (y_all[quad] + skip * xc[...].astype(F32)).astype(BF16).astype(F32)
        gated = y * (z * sig)
        square[...] += fold(gated * gated)
        cross[...] += fold(pulled * gated)

    @pl.when(phase == 1)
    def _():
        @pl.when(quad == 0)
        def _():
            inv = lax.rsqrt(jnp.sum(square[...], axis=1, keepdims=True) * (1.0 / INNER) + EPS)
            mean = jnp.sum(cross[...], axis=1, keepdims=True) * (1.0 / INNER)
            scale[...] = jnp.broadcast_to(inv, scale.shape)
            slope[...] = jnp.broadcast_to(inv * inv * inv * mean, slope.shape)
            row_dot[...] = jnp.zeros_like(row_dot)

        y = (y_all[quad] + skip * xc[...].astype(F32)).astype(BF16).astype(F32)
        silu = z * sig
        gated = y * silu
        inv = jnp.concatenate([scale[...]] * 4, axis=1)
        unit = gated * inv
        mixed[...] = (unit * gain[...]).astype(BF16)
        d_gain[...] = jnp.sum(d_mixed[...] * unit, axis=0, keepdims=True)
        d_gated = inv * pulled - gated * jnp.concatenate([slope[...]] * 4, axis=1)
        low = (d_gated * silu).astype(BF16)
        d_y[...] = low
        d_gate[...] = (d_gated * y * (sig * (1.0 + z * (1.0 - sig)))).astype(BF16)
        row_dot[...] += head_sums(low.astype(F32) * y_all[quad], ex)
        for b in range(SEQS):
            span = slice(TOK * b, TOK * (b + 1))
            grown = jnp.exp(r[span, :])
            state = mm((grown * low[span, :].astype(F32)).astype(BF16), bcc[span, STATE:], TN).astype(BF16)
            for h in range(8):
                own[h, b] = state[HEAD * h : HEAD * (h + 1), :]


def middle(y_in, xc, bcc, r, start, d_skip, gate, d_mixed, gain):
    def cols(rows):
        return pl.BlockSpec((rows, WIDE), lambda p, j: (0, j))

    def first(rows):
        return pl.BlockSpec((rows, WIDE), lambda p, j: (0, jnp.where(p == 0, j, QUADS - 1)))

    def second(rows):
        return pl.BlockSpec((rows, WIDE), lambda p, j: (0, jnp.where(p == 1, j, 0)))

    states_in = pl.BlockSpec((8, SEQS, HEAD, STATE), lambda p, j: (jnp.where(p == 0, j, QUADS - 1), 0, 0, 0))
    states_out = pl.BlockSpec((8, SEQS, HEAD, STATE), lambda p, j: (jnp.where(p == 1, j, 0), 0, 0, 0))
    return call(
        middle_kernel,
        [((ROWS, INNER), BF16), ((ROWS, INNER), BF16), ((ROWS, INNER), BF16), (STATES_SHAPE, BF16), ((1, INNER), F32), ((ROWS, HEADS), F32)],
        [second(ROWS), second(ROWS), second(ROWS), states_out, second(1), whole((ROWS, HEADS))],
        [first(ROWS), cols(ROWS), whole((ROWS, 2 * STATE)), cols(ROWS), states_in, cols(1), cols(ROWS), cols(ROWS), cols(1)],
        grid=(2, QUADS),
        scratch=[pltpu.VMEM((QUADS, ROWS, WIDE), F32)] + [pltpu.VMEM((ROWS, 128), F32)] * 4,
    )(y_in, xc, bcc, r, start, d_skip, gate, d_mixed, gain)


REDUCE = (("y", "z", "x"), ("z", "x", "y"), ("x", "y", "z")) + (("x", "y", "z"), ("y", "z", "x"), ("z", "x", "y"))
GATHER = (("l", "z", "x"), ("l", "x", "z"), ("x", "z", "l")) * 2
PIECE = 128
EXTRA = 32
PIECE_ROWS = (80, 48 + 32, 96, 48, 48, 32 + EXTRA)
EARLY, LATE = (0, 1, 2), (3, 4, 5)
SETS = len(PIECE_ROWS)
SMALL = 3 * 128
VECTOR = (16, INNER)


def position():
    seq, shard = lax.axis_index("seq"), lax.axis_index("wshard")
    high, core = shard // 2, shard % 2
    low = seq % 2
    return {"z": seq // 8, "x": (seq // 2) % 4, "y": high * 2 + low, "l": low, "core": core}


def device(at):
    return {"seq": at["z"] * 8 + at["x"] * 2 + at["y"] % 2, "wshard": (at["y"] // 2) * 2 + at["core"]}


def moved(at, axis, to):
    new = dict(at)
    if axis == "l":
        new["y"] = (at["y"] // 2) * 2 + to
        new["l"] = to
    else:
        new[axis] = to
        if axis == "y":
            new["l"] = to % 2
    return new


def peers(at, axis):
    size = 2 if axis in ("l", "core") else 4
    return [moved(at, axis, lax.rem(at[axis] + d, size)) for d in range(1, size)]


def greet(everyone):
    barrier = pltpu.get_barrier_semaphore()
    for other in everyone:
        pl.semaphore_signal(barrier, inc=1, device_id=device(other), device_id_type=pl.DeviceIdType.MESH)
    pl.semaphore_wait(barrier, len(everyone))


def tail_kernel(
    v, decay, xc, d_y, bcc, dt, dt_wide, r_wide, r_rows, x_raw, start, bc_raw, dt_raw, row_dot,
    taps_x, bias_x, taps_bc, bias_bc, dt_bias, a_log, d_skip, g_norm,
    normed, d_gate, mixed, cot, layer_in, gain_in, full_z, full_x, full_small,
    out_za, out_zb, out_zc, out_xa, out_xb, out_xc, input_grad, vector,
    weights, v_all, g_own, end, d_stepped, scores, d_scores, d_bc, sums, d_x_raw, d_small, g_x, g_bc, g_heads,
    d_normed, halo_out, halo_in, few_own, few_got,
    keep_n, keep_m, next_n, next_m, sib_n, sib_gate, sib_m, sib_cot, sib_wide, sib_small,
    parts_za, parts_zb, parts_zc, parts_xa, parts_xb, parts_xc,
    got_za1, got_zb1, got_zc1, got_xa1, got_xb1, got_xc1, sum_za1, sum_zb1, sum_zc1, sum_xa1, sum_xb1, sum_xc1,
    got_za2, got_zb2, got_zc2, got_xa2, got_xb2, got_xc2, sum_za2, sum_zb2, sum_zc2, sum_xa2, sum_xb2, sum_xc2,
    got_za3, got_zb3, got_zc3, got_xa3, got_xb3, got_xc3,
    v_send, v_recv, g_send, g_recv, sib_send, sib_recv, red_send, red_recv, all_send, all_recv,
    few_send, few_recv, halo_sem, load_sem,
):
    at = position()
    me = lax.axis_index("seq")
    core = at["core"]
    sibling = peers(at, "core")[0]
    barrier = greet_chunks(me)
    others = [sibling] + peers(at, "y")
    for other in others:
        pl.semaphore_signal(barrier, inc=1, device_id=device(other), device_id_type=pl.DeviceIdType.MESH)
    pl.semaphore_wait(barrier, HEADS - 1 + len(others))
    started = []

    def copy(src, dst, send, recv, to):
        one = pltpu.make_async_remote_copy(
            src_ref=src, dst_ref=dst, send_sem=send, recv_sem=recv,
            device_id=device(to), device_id_type=pl.DeviceIdType.MESH,
        )
        one.start()
        started.append(one)
        return one

    def swap_start(src, dst, send, recv):
        each_other(me, lambda other: chunk_copy(src, dst, send, recv, other, me).start())
        dst[me] = src[me]

    def swap_wait(src, dst, send, recv):
        each_other(me, lambda other: chunk_copy(src, dst, send, recv, other, other).wait_recv())

    def swap_sent(src, dst, send, recv):
        each_other(me, lambda other: chunk_copy(src, dst, send, recv, other, me).wait_send())

    swap_start(v, v_all, v_send, v_recv)

    def columns(ref, high, which, size):
        return ref.at[:, lane_block(2 * high + which, size)]

    def transposed(ref, high, which, size):
        return ref[:, lane_block(2 * high + which, size)].astype(F32).T.astype(BF16)

    pairs = [(columns(normed, h, 1 - core, 256), sib_n.at[h]) for h in range(2)] + [(d_gate, sib_gate)]
    pairs += [(columns(mixed, h, 1 - core, 512), sib_m.at[h]) for h in range(2)] + [(cot, sib_cot)]
    from_sibling = [copy(a, b, sib_send.at[i], sib_recv.at[i], sibling) for i, (a, b) in enumerate(pairs)]
    loading = pltpu.make_async_copy(full_z, weights, load_sem)
    loading.start()

    d_scores[...] = jnp.zeros_like(d_scores)
    for b in range(SEQS):
        span = slice(TOK * b, TOK * (b + 1))
        scores[b] = mm(bcc[span, STATE:], bcc[span, 0:STATE], NT)

    def inside_pair(j, _):
        cols = lane_block(j)
        for b in range(SEQS):
            span = slice(TOK * b, TOK * (b + 1))
            first, second = decay_pair(r_wide[span, cols], r_rows[j, :, span])
            both = jnp.concatenate([scores[b] * first, scores[b] * second], axis=0).astype(BF16)
            stepped = (dt_wide[span, cols] * xc[span, cols].astype(F32)).astype(BF16)
            wide = block_diagonal(d_y[span, cols])
            d_stepped[span, cols] = mm(both, wide, TN)
            d_both = mm(wide, stepped, NT)
            d_scores[b] += d_both[0:TOK, :] * first + d_both[TOK:, :] * second
        return 0

    lax.fori_loop(0, PAIRS, inside_pair, 0)
    for b in range(SEQS):
        span = slice(TOK * b, TOK * (b + 1))
        low = d_scores[b].astype(BF16)
        d_bc[span, 0:STATE] = mm(low, bcc[span, STATE:], TN)
        d_bc[span, STATE:] = mm(low, bcc[span, 0:STATE], NN)

    swap_wait(v, v_all, v_send, v_recv)

    def chunk_step(i, carry):
        c = HEADS - 1 - i
        after = []
        for b in range(SEQS):
            g_own[c, b] = carry[b].astype(BF16)
            after.append(decay[c, b : b + 1, :] * carry[b] + v_all[c, b].astype(F32))
        return tuple(after)

    lax.fori_loop(0, HEADS, chunk_step, tuple(jnp.zeros((HEAD, STATE), F32) for _ in range(SEQS)))
    swap_start(g_own, end, g_send, g_recv)

    parts = (parts_za, parts_zb, parts_zc, parts_xa, parts_xb, parts_xc)
    got = (
        (got_za1, got_zb1, got_zc1, got_xa1, got_xb1, got_xc1),
        (got_za2, got_zb2, got_zc2, got_xa2, got_xb2, got_xc2),
        (got_za3, got_zb3, got_zc3, got_xa3, got_xb3, got_xc3),
    )
    partial = (
        (sum_za1, sum_zb1, sum_zc1, sum_xa1, sum_xb1, sum_xc1),
        (sum_za2, sum_zb2, sum_zc2, sum_xa2, sum_xb2, sum_xc2),
    )
    outs = (out_za, out_zb, out_zc, out_xa, out_xb, out_xc)
    arriving = [None] * SETS

    def send_stage(stage, which, src):
        axis = REDUCE[which][stage]
        arriving[which] = [
            copy(
                src.at[to[axis]], got[stage][which].at[d],
                red_send.at[which, stage, d], red_recv.at[which, stage, d], to,
            )
            for d, to in enumerate(peers(at, axis))
        ]

    def arrived(which):
        for one in arriving[which]:
            one.wait_recv()

    def add_stage(stage, which):
        arrived(which)
        src = parts[which] if stage == 0 else partial[0][which]
        dst, came = partial[stage][which], got[stage][which]
        mine = at[REDUCE[which][stage]]

        def add(i, _):
            for j in range(4) if stage == 0 else ((),):
                index = (i, j) if stage == 0 else (i,)
                value = src[(mine, *index)].astype(F32)
                for d in range(3):
                    value = value + came[(d, *index)].astype(F32)
                dst[index] = value.astype(BF16)
            return 0

        lax.fori_loop(0, 4, add, 0)
        send_stage(stage + 1, which, dst)

    def gather_stage(stage, which):
        first, second, third = GATHER[which]
        index = (at[third], at[second], at[first])[: 3 - stage]
        ref = outs[which].at[index]
        arriving[which] = [
            copy(ref, ref, all_send.at[which, stage, d], all_recv.at[which, stage, d], to)
            for d, to in enumerate(peers(at, (first, second, third)[stage]))
        ]

    def last_add(which):
        arrived(which)
        first, second, third = GATHER[which]
        value = partial[1][which][at[REDUCE[which][2]]].astype(F32)
        for d in range(3):
            value = value + got[2][which][d].astype(F32)
        outs[which][at[third], at[second], at[first]] = value.astype(BF16)
        gather_stage(0, which)

    def gather_next(stage, which):
        arrived(which)
        gather_stage(stage, which)

    for h in range(2):
        keep_n[256 * h : 256 * (h + 1), :] = transposed(normed, h, core, 256)
        keep_m[512 * h : 512 * (h + 1), :] = transposed(mixed, h, core, 512)
    for one in from_sibling[:3]:
        one.wait_recv()
    for h in range(2):
        next_n[256 * h : 256 * (h + 1), :] = sib_n[h].astype(F32).T.astype(BF16)

    def tile_z(n, _):
        cols = lane_block(n, 256)
        res = mm(keep_n[:, 0:ROWS], d_gate[:, cols], NN) + mm(next_n[:, 0:ROWS], sib_gate[:, cols], NN)
        for y in range(4):
            for k in range(2):
                block = res[128 * y : 128 * y + 128, 128 * k : 128 * k + 128].astype(BF16)
                x, z = n // 2, (n % 2) * 2 + k
                parts_za[y, z, x] = block[0:80]
                parts_zb[z, x, y, 0:48] = block[80:128]
        return 0

    lax.fori_loop(0, 8, tile_z, 0)
    send_stage(0, 0, parts_za)
    for one in from_sibling[3:]:
        one.wait_recv()
    for h in range(2):
        next_m[512 * h : 512 * (h + 1), :] = sib_m[h].astype(F32).T.astype(BF16)

    def tile_out(n, _):
        cols = lane_block(n, 256)
        res = mm(keep_m[...], cot[:, cols], NN) + mm(next_m[...], sib_cot[:, cols], NN)
        for y in range(4):
            for half in range(2):
                for k in range(2):
                    row = 256 * y + 128 * half
                    block = res[row : row + 128, 128 * k : 128 * k + 128].astype(BF16)
                    x, z = half * 2 + n // 2, (n % 2) * 2 + k
                    parts_zb[z, x, y, 48:80] = block[0:32]
                    parts_zc[x, y, z] = block[32:128]
        return 0

    lax.fori_loop(0, 4, tile_out, 0)
    send_stage(0, 1, parts_zb)
    send_stage(0, 2, parts_zc)

    loading.wait()
    for n in range(4):
        cols = slice(256 * n, 256 * (n + 1))
        d_normed[0:ROWS, cols] = mm(d_gate[...], weights[cols, :], NT)
    loading = pltpu.make_async_copy(full_x, weights, load_sem)
    loading.start()

    swap_wait(g_own, end, g_send, g_recv)
    sums[...] = jnp.zeros_like(sums)

    def back_pair(j, _):
        cols = lane_block(j)
        ex = pair_matrix(j)
        skip = d_skip[:, cols]
        raw = x_raw[:, cols].astype(F32)
        halos, grads = [], None
        d_steps, dots, end_rows = [], [], []
        skip_sum = jnp.zeros((1, 128), F32)
        for b in range(SEQS):
            span = slice(TOK * b, TOK * (b + 1))
            r_lanes = r_wide[span, cols]
            dt_lanes = dt_wide[span, cols]
            last = r_lanes[TOK - 1 : TOK, :]
            grown = jnp.exp(r_lanes)
            to_end = jnp.exp(last - r_lanes)
            before = jnp.concatenate([start[2 * j, b], start[2 * j + 1, b]], axis=0)
            after = jnp.concatenate([end[2 * j, b], end[2 * j + 1, b]], axis=0)
            x = xc[span, cols].astype(F32)
            dy = d_y[span, cols].astype(F32)
            stepped = (dt_lanes * x).astype(BF16).astype(F32)
            carried = to_end * mm(bcc[span, 0:STATE], after, NT)
            d_step = d_stepped[span, cols] + carried
            dots.append(stepped * d_step)
            d_x = dt_lanes * d_step + skip * dy
            d_steps.append(x * d_step)
            inner = lane_sums(before.astype(F32) * after.astype(F32))
            end_rows.append(jnp.sum(stepped * carried, axis=0, keepdims=True) + jnp.exp(last) * inner)
            d_bc[span, STATE:] += mm((grown * dy).astype(BF16), before, NN)
            d_bc[span, 0:STATE] += mm((to_end * stepped).astype(BF16), after, NN)
            skip_sum = skip_sum + jnp.sum(dy * x, axis=0, keepdims=True)
            d_pad, d_taps, d_bias = conv_back(padded_of(raw, b), taps_x[:, cols], bias_x[:, cols], d_x)
            d_x_raw[span, cols] = d_pad[HALO:, :].astype(BF16)
            halos.append(d_pad[0:HALO, :])
            found = [*d_taps, d_bias]
            grads = found if grads is None else [g + p for g, p in zip(grads, found)]
        d_x_raw[ROWS:, cols] = jnp.concatenate(halos, axis=0).astype(BF16)
        g_x[:, cols] = jnp.concatenate([*grads, jnp.zeros((8 - TAPS - 1, 128), F32)], axis=0)
        few = jnp.concatenate([*end_rows, skip_sum, jnp.zeros((5, 128), F32)], axis=0)
        sums[...] += head_sums(jnp.concatenate([*d_steps, *dots, few], axis=0), ex)
        return 0

    wide_coming = []
    for quarter in range(4):
        lax.fori_loop(4 * quarter, 4 * quarter + 4, back_pair, 0)
        cols = slice(512 * quarter, 512 * (quarter + 1))
        wide_coming.append(
            copy(d_x_raw.at[:, cols], sib_wide.at[:, cols], sib_send.at[6 + quarter], sib_recv.at[6 + quarter], sibling)
        )
    raw = bc_raw[...].astype(F32)
    halos, grads = [], None
    for b in range(SEQS):
        span = slice(TOK * b, TOK * (b + 1))
        d_pad, d_taps, d_bias = conv_back(padded_of(raw, b), taps_bc[...], bias_bc[...], d_bc[span, :])
        d_small[span, 0 : 2 * STATE] = d_pad[HALO:, :].astype(BF16)
        halos.append(d_pad[0:HALO, :])
        found = [*d_taps, d_bias]
        grads = found if grads is None else [g + p for g, p in zip(grads, found)]
    d_small[ROWS:, 0 : 2 * STATE] = jnp.concatenate(halos, axis=0).astype(BF16)
    d_small[ROWS:, 2 * STATE :] = jnp.zeros((ALL - ROWS, SMALL - 2 * STATE), BF16)
    g_bc[...] = jnp.concatenate([*grads, jnp.zeros((8 - TAPS - 1, 2 * STATE), F32)], axis=0)
    rate = -jnp.exp(a_log[...])
    tri = causal_mask().astype(F32)
    is_last = iota((TOK, HEADS), 0) == TOK - 1
    bias_sum = jnp.zeros((1, HEADS), F32)
    log_sum = jnp.zeros((1, HEADS), F32)
    for b in range(SEQS):
        span = slice(TOK * b, TOK * (b + 1))
        step = dt[span, :]
        d_dt = sums[span, :]
        d_r = row_dot[span, :] - sums[ROWS + TOK * b : ROWS + TOK * (b + 1), :]
        d_r = d_r + jnp.where(is_last, sums[2 * ROWS + b : 2 * ROWS + b + 1, :], 0.0)
        d_log = mm(tri, d_r, TN, HIGHEST)
        d_pre = (d_dt + rate * d_log) * jax.nn.sigmoid(dt_raw[span, :].astype(F32) + dt_bias[...])
        d_small[span, 2 * STATE :] = jnp.concatenate(
            [d_pre, jnp.zeros((TOK, SMALL - 2 * STATE - HEADS), F32)], axis=1
        ).astype(BF16)
        bias_sum = bias_sum + jnp.sum(d_pre, axis=0, keepdims=True)
        log_sum = log_sum + jnp.sum(d_log * step, axis=0, keepdims=True) * rate
    g_heads[...] = jnp.concatenate(
        [bias_sum, log_sum, sums[2 * ROWS + 2 : 2 * ROWS + 3, :], jnp.zeros((5, HEADS), F32)], axis=0
    )
    small_coming = copy(d_small, sib_small, sib_send.at[10], sib_recv.at[10], sibling)

    for which in EARLY:
        add_stage(0, which)

    def tile_x(n, _):
        cols = lane_block(n, 256)
        res = mm(keep_n[...], d_x_raw[:, cols], NN) + mm(next_n[...], sib_wide[:, cols], NN)
        for y in range(4):
            for k in range(2):
                block = res[128 * y : 128 * y + 128, 128 * k : 128 * k + 128].astype(BF16)
                x, z = n // 2, (n % 2) * 2 + k
                parts_xa[x, y, z] = block[0:48]
                parts_xb[y, z, x] = block[48:96]
                parts_xc[z, x, y, 0:32] = block[96:128]
        return 0

    for quarter in range(4):
        wide_coming[quarter].wait_recv()
        lax.fori_loop(2 * quarter, 2 * quarter + 2, tile_x, 0)
    send_stage(0, 3, parts_xa)
    send_stage(0, 4, parts_xb)
    small_coming.wait_recv()
    res = mm(keep_n[...], d_small[...], NN) + mm(next_n[...], sib_small[...], NN)
    for y in range(4):
        for z in range(4):
            row = 128 * y + EXTRA * z
            for k in range(3):
                parts_xc[z, k, y, 32:] = res[row : row + EXTRA, 128 * k : 128 * k + 128].astype(BF16)
            parts_xc[z, 3, y, 32:] = jnp.zeros((EXTRA, 128), BF16)
    send_stage(0, 5, parts_xc)
    for which in EARLY:
        add_stage(1, which)

    loading.wait()
    d_normed[ROWS:, :] = jnp.zeros((ALL - ROWS, d_normed.shape[1]), F32)
    for n in range(4):
        cols = slice(256 * n, 256 * (n + 1))
        d_normed[:, cols] += mm(d_x_raw[...], weights[cols, :], NT) + mm(d_small[...], full_small[cols, :], NT)
    halo_out[...] = d_normed[ROWS:, :]
    halo = pltpu.make_async_remote_copy(
        src_ref=halo_out, dst_ref=halo_in, send_sem=halo_sem.at[0], recv_sem=halo_sem.at[1],
        device_id={"seq": lax.rem(me + HEADS - 1, HEADS)}, device_id_type=pl.DeviceIdType.MESH,
    )
    halo.start()
    started.append(halo)
    for which in EARLY:
        last_add(which)
    halo.wait_recv()
    inner = jnp.where(me == HEADS - 1, 0.0, 1.0)
    for b in range(SEQS):
        near = slice(TOK * (b + 1) - HALO, TOK * (b + 1))
        d_normed[near, :] += inner * halo_in[HALO * b : HALO * (b + 1), :]
    g_in = jnp.zeros((1, d_normed.shape[1]), F32)
    for n in range(4):
        span = slice(64 * n, 64 * (n + 1))
        hidden = layer_in[span, :].astype(F32)
        inv = lax.rsqrt(jnp.mean(hidden * hidden, axis=1, keepdims=True) + EPS)
        unit = hidden * inv
        grad = d_normed[span, :]
        g_in = g_in + jnp.sum(grad * unit, axis=0, keepdims=True)
        pulled = grad * gain_in[...]
        d_hidden = inv * (pulled - unit * jnp.mean(pulled * unit, axis=1, keepdims=True))
        input_grad[span, :] = cot[span, :].astype(F32) + d_hidden

    few_axes = ("core", "x", "z", "y")
    rest = jnp.concatenate(
        [
            g_bc[...], jnp.concatenate([g_heads[...], jnp.zeros((8, 128 - HEADS), F32)], axis=1),
            jnp.zeros((8, INNER - 2 * STATE - 128), F32),
        ],
        axis=1,
    )
    wide_in = jnp.concatenate([g_in, jnp.zeros((1, INNER - g_in.shape[1]), F32)], axis=1)
    few = jnp.concatenate([g_x[...], g_norm[...], wide_in, rest[0 : TAPS + 1], jnp.zeros((1, INNER), F32)], axis=0)

    few_coming = [None]

    def few_start(stage, value):
        few_own[stage] = value.astype(BF16)
        axis = few_axes[stage]
        few_got[stage, at[axis]] = few_own[stage]
        few_coming[0] = [
            copy(
                few_own.at[stage], few_got.at[stage, at[axis]],
                few_send.at[stage, d], few_recv.at[stage, d], to,
            )
            for d, to in enumerate(peers(at, axis))
        ]

    def few_sum(stage):
        for one in few_coming[0]:
            one.wait_recv()
        value = few_got[stage, 0].astype(F32)
        for i in range(1, 2 if stage == 0 else 4):
            value = value + few_got[stage, i].astype(F32)
        return value

    few_start(0, few)
    for which in EARLY:
        gather_next(1, which)
    for which in LATE:
        add_stage(0, which)
    few_start(1, few_sum(0))
    for which in LATE:
        add_stage(1, which)
    few_start(2, few_sum(1))
    for which in EARLY:
        gather_next(2, which)
    for which in LATE:
        last_add(which)
    few_start(3, few_sum(2))
    for which in LATE:
        gather_next(1, which)
    vector[...] = few_sum(3)
    for which in LATE:
        gather_next(2, which)
    for which in range(SETS):
        arrived(which)
    for one in started:
        one.wait_send()
    swap_sent(v, v_all, v_send, v_recv)
    swap_sent(g_own, end, g_send, g_recv)


def tail(*args):
    vmem = pl.BlockSpec(memory_space=pltpu.VMEM)
    hbm = pl.BlockSpec(memory_space=pl.ANY)
    specs = [vmem] * len(args)
    specs[-3] = specs[-2] = hbm
    width = args[-2].shape[0]
    dims = {"x": 4, "z": 4, "l": 2}
    out_shape = [
        jax.ShapeDtypeStruct((*(dims[a] for a in reversed(GATHER[i])), PIECE_ROWS[i], 128), BF16) for i in range(SETS)
    ]
    out_shape += [jax.ShapeDtypeStruct((ROWS, width), F32), jax.ShapeDtypeStruct(VECTOR, F32)]

    def bufs(*lead):
        return [pltpu.VMEM((*lead, PIECE_ROWS[i], 128), BF16) for i in range(SETS)]

    def sems(*shape):
        return [pltpu.SemaphoreType.DMA(shape)] * 2

    scratch = [
        pltpu.VMEM((width, INNER), BF16), *[pltpu.VMEM(STATES_SHAPE, BF16)] * 3, pltpu.VMEM((ROWS, INNER), F32),
        *[pltpu.VMEM((SEQS, TOK, TOK), F32)] * 2, pltpu.VMEM((ROWS, 2 * STATE), F32),
        pltpu.VMEM((2 * ROWS + 8, HEADS), F32), pltpu.VMEM((ALL, INNER), BF16), pltpu.VMEM((ALL, SMALL), BF16),
        pltpu.VMEM((8, INNER), F32), pltpu.VMEM((8, 2 * STATE), F32), pltpu.VMEM((8, HEADS), F32),
        pltpu.VMEM((ALL, width), F32), *[pltpu.VMEM((SEQS * HALO, width), F32)] * 2,
        pltpu.VMEM((4, *VECTOR), BF16), pltpu.VMEM((4, 4, *VECTOR), BF16),
        *[pltpu.VMEM((512, ALL), BF16), pltpu.VMEM((1024, ROWS), BF16)] * 2,
        pltpu.VMEM((2, ALL, 256), BF16), pltpu.VMEM((ROWS, INNER), BF16), pltpu.VMEM((2, ROWS, 512), BF16),
        pltpu.VMEM((ROWS, width), BF16), pltpu.VMEM((ALL, INNER), BF16), pltpu.VMEM((ALL, SMALL), BF16),
        *bufs(4, 4, 4), *bufs(3, 4, 4), *bufs(4, 4), *bufs(3, 4), *bufs(4), *bufs(3),
        *sems(HEADS), *sems(HEADS), *sems(11), *sems(SETS, 3, 3), *sems(SETS, 3, 3), *sems(4, 3),
        pltpu.SemaphoreType.DMA((2,)), pltpu.SemaphoreType.DMA,
    ]
    return pl.pallas_call(
        tail_kernel,
        out_shape=out_shape,
        in_specs=specs,
        out_specs=[vmem] * len(out_shape),
        scratch_shapes=scratch,
        compiler_params=pltpu.CompilerParams(
            vmem_limit_bytes=62 * 1024 * 1024, collective_id=1, has_side_effects=True
        ),
        cost_estimate=pl.CostEstimate(flops=int(8e9), bytes_accessed=int(4e7), transcendentals=0),
    )(*args)


def unpack_kernel(sum_za, sum_zb, sum_zc, sum_xa, sum_xb, sum_xc, out_z, out_x, out_out, out_extra):
    for low in range(2):
        base = PIECE * low
        out_z[base : base + 80, :] = sum_za[0, 0, low].astype(F32)
        out_z[base + 80 : base + 128, :] = sum_zb[0, 0, low, 0:48, :].astype(F32)
        out_out[low, 0, 0:32, :] = sum_zb[0, 0, low, 48:80, :].astype(F32)
        out_out[low, 0, 32:128, :] = sum_zc[low, 0, 0].astype(F32)
        out_x[base : base + 48, :] = sum_xa[0, 0, low].astype(F32)
        out_x[base + 48 : base + 96, :] = sum_xb[0, 0, low].astype(F32)
        out_x[base + 96 : base + 128, :] = sum_xc[low, 0, 0, 0:32, :].astype(F32)
        out_extra[0, low] = sum_xc[low, 0, 0, 32:, :].astype(F32)


def unpack(*gathered):
    specs = []
    for i in range(SETS):
        def where(n, order=GATHER[i]):
            return tuple({"x": n // 4, "z": n % 4, "l": 0}[a] for a in reversed(order)) + (0, 0)

        block = tuple(2 if a == "l" else 1 for a in reversed(GATHER[i])) + (PIECE_ROWS[i], 128)
        specs.append(pl.BlockSpec(block, where))
    return call(
        unpack_kernel,
        [((2 * PIECE, INNER), F32), ((2 * PIECE, INNER), F32), ((2, 2, PIECE, 8 * 128), F32), ((4, 2, 4 * EXTRA, 128), F32)],
        [
            lanes(2 * PIECE), lanes(2 * PIECE),
            pl.BlockSpec((2, 1, PIECE, 128), lambda i: (0, i // 8, 0, ((i // 4) % 2) * 4 + i % 4)),
            pl.BlockSpec((1, 2, EXTRA, 128), lambda i: (i // 4, 0, i % 4, 0)),
        ],
        specs,
    )(*gathered)


def gather_kernel(
    w_x, w_small, own, full_x, full_small, params, send, recv, here, own_send, own_recv,
):
    at = position()
    sibling = peers(at, "core")[0]
    partner = moved(at, "y", 3 - at["y"])
    everyone = [sibling, partner] + [p for axis in ("x", "z", "l") for p in peers(at, axis)]
    greet(everyone)
    started = []

    def copy(src, dst, which, to, sems=(send, recv)):
        one = pltpu.make_async_remote_copy(
            src_ref=src, dst_ref=dst, send_sem=sems[0].at[which], recv_sem=sems[1].at[which],
            device_id=device(to), device_id_type=pl.DeviceIdType.MESH,
        )
        one.start()
        started.append(one)
        return one

    high = at["y"] // 2
    mine, opposite = high * 2 + at["core"], (1 - high) * 2 + at["core"]
    half = INNER // 2
    flows = ((full_x, 0, half, "x", "z"), (full_x, half, half, "z", "x"), (full_small, 0, SMALL, "x", "z"))

    def view(ref, shard, row, count, first, size):
        row = pl.multiple_of(row, 16)
        if shard is None:
            return ref.at[pl.ds(row, count), first : first + size]
        return ref.at[shard, pl.ds(row, count), first : first + size]

    arriving = []
    for i, (ref, first, size, a, b) in enumerate(flows):
        row = (at[b] * 4 + at[a]) * 16
        src = w_small if i == 2 else w_x
        arriving.append(copy(view(src, None, row, 16, first, size), view(ref, mine, row, 16, first, size), i, partner))
    params_here = pltpu.make_async_copy(own, params.at[at["z"], at["x"], at["l"]], here.at[2])
    local = [
        pltpu.make_async_copy(w_x, full_x.at[mine], here.at[0]),
        pltpu.make_async_copy(w_small, full_small.at[mine], here.at[1]),
        params_here,
    ]
    for one in local:
        one.start()
    last = [
        copy(w_x, full_x.at[mine], 24, sibling),
        copy(w_small, full_small.at[mine], 25, sibling),
    ]
    params_here.wait()

    def share(stage):
        axis = ("l", "x", "z")[stage]
        ref = params.at[(at["z"], at["x"], at["l"])[: 3 - stage]]
        return [copy(ref, ref, 3 * stage + d, to, (own_send, own_recv)) for d, to in enumerate(peers(at, axis))]

    shared = share(0)
    second = []
    for i, (ref, first, size, a, b) in enumerate(flows):
        arriving[i].wait_recv()
        piece = view(ref, opposite, (at[b] * 4 + at[a]) * 16, 16, first, size)
        second.append([copy(piece, piece, 3 + 3 * i + d, to) for d, to in enumerate(peers(at, a))])
    for one in shared:
        one.wait_recv()
    shared = share(1)
    third = []
    for i, (ref, first, size, a, b) in enumerate(flows):
        for one in second[i]:
            one.wait_recv()
        block = view(ref, opposite, at[b] * 64, 64, first, size)
        third.append([copy(block, block, 12 + 3 * i + d, to) for d, to in enumerate(peers(at, b))])
        last.append(copy(block, block, 21 + i, sibling))
    for one in shared:
        one.wait_recv()
    shared = share(2)
    for i, (ref, first, size, a, b) in enumerate(flows):
        for d in range(3):
            third[i][d].wait_recv()
            block = view(ref, opposite, lax.rem(at[b] + 3 - d, 4) * 64, 64, first, size)
            last.append(copy(block, block, 26 + 3 * i + d, sibling))
    for one in last + shared:
        one.wait_recv()
    for one in local[:2]:
        one.wait()
    for one in started:
        one.wait_send()


def gather_weights(w_x, w_small, own):
    vmem = pl.BlockSpec(memory_space=pltpu.VMEM)
    return pl.pallas_call(
        gather_kernel,
        out_shape=[
            jax.ShapeDtypeStruct((4, *w_x.shape), BF16),
            jax.ShapeDtypeStruct((4, *w_small.shape), BF16),
            jax.ShapeDtypeStruct((4, 4, 2, 8, 128), F32),
        ],
        in_specs=[vmem] * 3,
        out_specs=[vmem] * 3,
        scratch_shapes=[
            pltpu.SemaphoreType.DMA((35,)), pltpu.SemaphoreType.DMA((35,)), pltpu.SemaphoreType.DMA((3,)),
            pltpu.SemaphoreType.DMA((9,)), pltpu.SemaphoreType.DMA((9,)),
        ],
        compiler_params=pltpu.CompilerParams(
            vmem_limit_bytes=VMEM_LIMIT, collective_id=2, has_side_effects=True
        ),
        cost_estimate=pl.CostEstimate(flops=int(1e6), bytes_accessed=int(4e7), transcendentals=0),
    )(w_x, w_small, own)


def gather_rows(shard):
    return lax.all_gather(shard, "wshard", axis=0, tiled=True)


def shards(
    layer_in, gain_in, w_z, w_x, w_bc, w_dt, conv_x_weight, conv_x_bias, conv_bc_weight, conv_bc_bias,
    dt_bias, a_log, d_skip, gain_norm, w_out, cotangent,
):
    width = layer_in.shape[2]
    chunks = lax.axis_size("seq")
    place = lax.axis_index("seq")
    earlier = lax.ppermute(layer_in[:, TOK - (TAPS - 1) :, :], "seq", [(i, i + 1) for i in range(chunks - 1)])
    full_z = gather_rows(w_z)
    full_out = gather_rows(w_out)
    own = jnp.concatenate([conv_x_weight.reshape(-1), conv_x_bias, dt_bias, a_log, d_skip, jnp.zeros((701,), F32)])
    small = jnp.concatenate([w_bc, w_dt, jnp.zeros((w_bc.shape[0], SMALL - 2 * STATE - HEADS), BF16)], axis=1)
    full_x, full_small, params = gather_weights(w_x, small, own.reshape(8, 128))
    full_x = full_x.reshape(width, INNER)
    full_small = full_small.reshape(width, SMALL)
    params = params.reshape(HEADS, -1)
    taps_x = params[:, : TAPS * HEAD].reshape(HEADS, TAPS, HEAD).swapaxes(0, 1).reshape(TAPS, INNER)
    bias_x = params[:, TAPS * HEAD : (TAPS + 1) * HEAD].reshape(1, INNER)
    bias_dt, log_a, skip = (params[:, (TAPS + 1) * HEAD + i].reshape(1, HEADS) for i in range(3))
    bias_bc = conv_bc_bias.reshape(1, -1)
    skip_wide = jnp.repeat(skip, HEAD, axis=1)

    hidden = layer_in.astype(F32).reshape(ROWS, width)
    upstream = cotangent.reshape(ROWS, width)
    halo = jnp.pad(earlier, ((0, 0), (HALO - (TAPS - 1), 0), (0, 0))).reshape(SEQS * HALO, width).astype(F32)
    tokens = jnp.concatenate([hidden, halo], axis=0)
    inv = lax.rsqrt(jnp.mean(tokens * tokens, axis=-1, keepdims=True) + EPS)
    normed = (tokens * inv * gain_in[None, :]).astype(BF16)

    x_raw = mm(normed, full_x, NN).astype(BF16)
    small_raw = mm(normed, full_small, NN).astype(BF16)
    bc_raw, dt_raw = small_raw[:, : 2 * STATE], small_raw[:, 2 * STATE : 2 * STATE + HEADS]
    xc, bcc, dt, dt_wide, r_wide, r_rows, y_in, start, decay = head(
        x_raw, bc_raw, dt_raw, taps_x, bias_x, conv_bc_weight, bias_bc, bias_dt, log_a
    )
    gate = mm(normed[:ROWS], full_z, NN)
    d_mixed = mm(upstream, full_out, NT)
    mixed, d_y, d_gate, v, g_norm, row_dot = middle(
        y_in, xc, bcc, r_wide, start, skip_wide, gate, d_mixed, gain_norm.reshape(1, INNER)
    )
    layer_out = (hidden + mm(mixed, full_out, NN)).astype(BF16).reshape(SEQS, TOK, width)
    *gathered, input_grad, total = tail(
        v, decay, xc, d_y, bcc, dt, dt_wide, r_wide, r_rows, x_raw, start, bc_raw, dt_raw, row_dot,
        taps_x, bias_x, conv_bc_weight, bias_bc, bias_dt, log_a, skip_wide, g_norm,
        normed, d_gate, mixed, upstream, layer_in.reshape(ROWS, width), gain_in.reshape(1, width),
        full_z, full_x, full_small,
    )
    input_grad = input_grad.reshape(SEQS, TOK, width)
    grad_w_z, grad_w_x, grad_w_out, extra = unpack(*gathered)
    grad_w_out = grad_w_out.reshape(4 * PIECE, width)
    extra = extra.reshape(4, 2 * PIECE, 128)
    grad_w_bc = jnp.concatenate([extra[0], extra[1]], axis=1)
    grad_w_dt = extra[2][:, :HEADS]
    s_x = lax.dynamic_slice(total[: TAPS + 1], (0, place * HEAD), (TAPS + 1, HEAD))
    s_norm, s_in = total[8], total[9, :width]
    s_bc = total[10 : 10 + TAPS + 1, : 2 * STATE]
    s_heads = lax.dynamic_slice(total[10:13], (0, 2 * STATE + place), (3, 1))
    return (
        layer_out, input_grad, s_in, grad_w_z, grad_w_x, grad_w_bc, grad_w_dt,
        s_x[:TAPS], s_x[TAPS], s_bc[:TAPS], s_bc[TAPS], s_heads[0], s_heads[1], s_heads[2], s_norm, grad_w_out,
    )


def solution(mesh):
    rows, heads = P("wshard", None), P("seq")
    tokens = P("wshard", "seq", None)
    return jax.shard_map(
        shards,
        mesh=mesh,
        in_specs=(
            tokens, P(), rows, rows, rows, rows, P(None, "seq"), heads, P(), P(), heads, heads, heads, P(), rows, tokens,
        ),
        out_specs=(
            tokens, tokens, P(), rows, rows, rows, rows, P(None, "seq"), heads, P(), P(), heads, heads, heads, P(), rows,
        ),
        check_vma=False,
    )
```

```python
import functools

import jax
import jax.numpy as jnp
from jax import lax
from jax.experimental import pallas as pl
from jax.experimental.pallas import tpu as pltpu
from jax.sharding import PartitionSpec as P

F32 = jnp.float32
BF16 = jnp.bfloat16
EPS = 1e-05
HIGHEST = lax.Precision.HIGHEST
HEADS = 32
HEAD = 64
STATE = 128
TOK = 128
SEQS = 2
ROWS = SEQS * TOK
HALO = 8
ALL = ROWS + SEQS * HALO
PAIRS = HEADS // 2
INNER = HEADS * HEAD
TAPS = 4


def mm(a, b, dims, precision=None):
    return lax.dot_general(a, b, ((dims[0], dims[1]), ((), ())), precision=precision, preferred_element_type=F32)


NN = ((1,), (0,))
NT = ((1,), (1,))
TN = ((0,), (0,))


def iota(shape, dim):
    return lax.broadcasted_iota(jnp.int32, shape, dim)


def pair_matrix(pair):
    upper = (iota((HEADS, 128), 1) >= HEAD).astype(jnp.int32)
    return (iota((HEADS, 128), 0) == 2 * pair + upper).astype(F32)


def pair_rows(pair):
    return (iota((8, HEADS), 1) == 2 * pair + iota((8, HEADS), 0)).astype(F32)


def head_sums(values, ex):
    high = values.astype(BF16)
    low = (values - high.astype(F32)).astype(BF16)
    ex = ex.astype(BF16)
    return mm(jnp.concatenate([high, low], axis=1), jnp.concatenate([ex, ex], axis=1), NT)


def lane_sums(values):
    high = values.astype(BF16)
    low = (values - high.astype(F32)).astype(BF16)
    return mm(jnp.ones((8, 256), BF16), jnp.concatenate([high, low], axis=1), NT)[0:1, :]


def causal_mask():
    return iota((TOK, TOK), 0) >= iota((TOK, TOK), 1)


def shifted(padded, k):
    back = TAPS - 1 - k
    if back:
        padded = pltpu.roll(padded, back, 0)
    return padded[HALO:, :]


def padded_of(rows, b):
    return jnp.concatenate(
        [rows[ROWS + HALO * b : ROWS + HALO * (b + 1), :], rows[TOK * b : TOK * (b + 1), :]], axis=0
    )


def conv_pre(padded, taps, bias):
    total = bias
    for k in range(TAPS):
        total = total + taps[k : k + 1, :] * shifted(padded, k)
    return total


def conv_back(padded, taps, bias, grad):
    pre = conv_pre(padded, taps, bias)
    sig = jax.nn.sigmoid(pre)
    d_pre = grad * (sig * (1.0 + pre * (1.0 - sig)))
    low = jnp.concatenate([jnp.zeros((HALO, d_pre.shape[1]), F32), d_pre], axis=0)
    d_pad = taps[TAPS - 1 : TAPS, :] * low
    for k in range(TAPS - 1):
        d_pad = d_pad + taps[k : k + 1, :] * pltpu.roll(low, HALO + TOK - (TAPS - 1 - k), 0)
    d_taps = [jnp.sum(d_pre * shifted(padded, k), axis=0, keepdims=True) for k in range(TAPS)]
    return d_pad, d_taps, jnp.sum(d_pre, axis=0, keepdims=True)


def block_diagonal(pair_values):
    first = iota(pair_values.shape, 1) < HEAD
    zero = jnp.zeros_like(pair_values)
    return jnp.concatenate(
        [jnp.where(first, pair_values, zero), jnp.where(first, zero, pair_values)], axis=0
    )


def decay_pair(r_lanes, r_rows):
    mask = causal_mask()
    out = []
    for q in range(2):
        spread = r_lanes[:, HEAD * q : HEAD * q + 1] - r_rows[q : q + 1, :]
        out.append(jnp.exp(jnp.where(mask, spread, -1e30)))
    return out


def whole(shape):
    return pl.BlockSpec(shape, lambda *_: (0,) * len(shape))


def lanes(rows):
    return pl.BlockSpec((rows, 128), lambda j: (0, j))


STATES_SHAPE = (HEADS, SEQS, HEAD, STATE)
VMEM_LIMIT = 62 * 1024 * 1024


def call(kernel, outs, out_specs, in_specs, grid=(PAIRS,), scratch=(), cost=None):
    return pl.pallas_call(
        kernel,
        grid=grid,
        out_shape=[jax.ShapeDtypeStruct(s, d) for s, d in outs],
        in_specs=in_specs,
        out_specs=out_specs,
        scratch_shapes=scratch,
        compiler_params=pltpu.CompilerParams(
            vmem_limit_bytes=VMEM_LIMIT, dimension_semantics=("arbitrary",) * len(grid)
        ),
        cost_estimate=cost or pl.CostEstimate(flops=int(1e9), bytes_accessed=int(1e7), transcendentals=0),
    )


def position():
    seq, shard = lax.axis_index("seq"), lax.axis_index("wshard")
    high, core = shard // 2, shard % 2
    low = seq % 2
    return {"z": seq // 8, "x": (seq // 2) % 4, "y": high * 2 + low, "l": low, "core": core}


def device(at):
    return {"seq": at["z"] * 8 + at["x"] * 2 + at["y"] % 2, "wshard": (at["y"] // 2) * 2 + at["core"]}


def moved(at, axis, to):
    new = dict(at)
    if axis == "l":
        new["y"] = (at["y"] // 2) * 2 + to
        new["l"] = to
    else:
        new[axis] = to
        if axis == "y":
            new["l"] = to % 2
    return new


def peers(at, axis):
    size = 2 if axis in ("l", "core") else 4
    return [moved(at, axis, lax.rem(at[axis] + d, size)) for d in range(1, size)]


def greet(everyone, more=0):
    barrier = pltpu.get_barrier_semaphore()
    for other in everyone:
        pl.semaphore_signal(barrier, inc=1, device_id=device(other), device_id_type=pl.DeviceIdType.MESH)
    pl.semaphore_wait(barrier, len(everyone) + more)


class Flows:
    def __init__(self, at, flows, copy):
        self.at, self.flows, self.copy = at, flows, copy
        high = at["y"] // 2
        self.mine, self.opposite = high * 2 + at["core"], (1 - high) * 2 + at["core"]
        self.sibling = peers(at, "core")[0]
        self.partner = moved(at, "y", 3 - at["y"])
        self.last = []

    def view(self, ref, shard, row, count, first, size):
        row = pl.multiple_of(row, 16)
        if shard is None:
            return ref.at[pl.ds(row, count), first : first + size]
        return ref.at[shard, pl.ds(row, count), first : first + size]

    def begin(self):
        self.arriving = []
        for i, (src, ref, first, size, a, b, rows) in enumerate(self.flows):
            row = (self.at[b] * 4 + self.at[a]) * rows
            here = self.view(src, None, row, rows, first, size)
            there = self.view(ref, self.mine, row, rows, first, size)
            self.arriving.append(self.copy(here, there, i, self.partner))

    def spread(self):
        n = len(self.flows)
        self.second = []
        for i, (src, ref, first, size, a, b, rows) in enumerate(self.flows):
            self.arriving[i].wait_recv()
            piece = self.view(ref, self.opposite, (self.at[b] * 4 + self.at[a]) * rows, rows, first, size)
            self.second.append([self.copy(piece, piece, n + 3 * i + d, to) for d, to in enumerate(peers(self.at, a))])

    def spread_more(self):
        n = len(self.flows)
        self.third = []
        for i, (src, ref, first, size, a, b, rows) in enumerate(self.flows):
            for one in self.second[i]:
                one.wait_recv()
            block = self.view(ref, self.opposite, self.at[b] * 4 * rows, 4 * rows, first, size)
            self.third.append([self.copy(block, block, 4 * n + 3 * i + d, to) for d, to in enumerate(peers(self.at, b))])
            self.last.append(self.copy(block, block, 7 * n + i, self.sibling))

    def forward(self):
        n = len(self.flows)
        for i, (src, ref, first, size, a, b, rows) in enumerate(self.flows):
            for d in range(3):
                self.third[i][d].wait_recv()
                block = self.view(ref, self.opposite, lax.rem(self.at[b] + 3 - d, 4) * 4 * rows, 4 * rows, first, size)
                self.last.append(self.copy(block, block, 8 * n + 3 * i + d, self.sibling))

    def own(self, pairs):
        n = len(self.flows)
        for j, (src, ref) in enumerate(pairs):
            self.last.append(self.copy(src, ref.at[self.mine], 11 * n + j, self.sibling))

    def finish(self):
        for one in self.last:
            one.wait_recv()


def chunk_copy(src, dst, send, recv, to, slot):
    return pltpu.make_async_remote_copy(
        src_ref=src.at[to], dst_ref=dst.at[slot], send_sem=send.at[to], recv_sem=recv.at[slot],
        device_id={"seq": to}, device_id_type=pl.DeviceIdType.MESH,
    )


def each_other(me, step):
    def go(d, _):
        step(lax.rem(me + d, HEADS))
        return 0

    lax.fori_loop(1, HEADS, go, 0)


def greet_chunks(me):
    barrier = pltpu.get_barrier_semaphore()
    each_other(
        me,
        lambda other: pl.semaphore_signal(
            barrier, inc=1, device_id={"seq": other}, device_id_type=pl.DeviceIdType.MESH
        ),
    )
    return barrier


def lane_block(j, size=128):
    return pl.ds(pl.multiple_of(j * size, size), size)


def pairs_loop(first, last, body):
    def two(i, _):
        body(2 * i, 0)
        body(2 * i + 1, 0)
        return 0

    lax.fori_loop(first // 2, last // 2, two, 0)


def head_kernel(
    x_raw, bc_raw, dt_raw, taps_x, bias_x, taps_bc, bias_bc, dt_bias, a_log,
    xc, bcc, dt, dt_wide, r_wide, r_rows, y_in, start, decay,
    r, scores, u, u_all, own_decay, s_own, u_send, u_recv, e_send, e_recv, s_send, s_recv,
):
    me = lax.axis_index("seq")
    barrier = greet_chunks(me)
    raw = bc_raw[...].astype(F32)
    dt[...] = jax.nn.softplus(dt_raw[0:ROWS, :].astype(F32) + dt_bias[...])
    tri = causal_mask().astype(F32)
    rates = dt[...] * (-jnp.exp(a_log[...]))
    for b in range(SEQS):
        span = slice(TOK * b, TOK * (b + 1))
        pre = conv_pre(padded_of(raw, b), taps_bc[...], bias_bc[...])
        bcc[span, :] = (pre * jax.nn.sigmoid(pre)).astype(BF16)
        r[span, :] = mm(tri, rates[span, :], NN, HIGHEST)
        scores[b] = mm(bcc[span, STATE:], bcc[span, 0:STATE], NT)
    first = iota((8, 128), 1) < HEAD
    pl.semaphore_wait(barrier, HEADS - 1)

    def front_pair(i, _):
        j = lax.rem(me // 2 + i, PAIRS)
        cols = lane_block(j)
        raw = x_raw[:, cols].astype(F32)
        both = mm(jnp.concatenate([r[...], dt[...]], axis=0), pair_matrix(j), NN, HIGHEST)
        r_wide[:, cols] = both[0:ROWS, :]
        dt_wide[:, cols] = both[ROWS:, :]
        r_rows[j] = mm(pair_rows(j), r[...], NT, HIGHEST)
        ends = []
        for b in range(SEQS):
            span = slice(TOK * b, TOK * (b + 1))
            pre = conv_pre(padded_of(raw, b), taps_x[:, cols], bias_x[:, cols])
            low = (pre * jax.nn.sigmoid(pre)).astype(BF16)
            xc[span, cols] = low
            r_lanes = both[span, :]
            dt_lanes = both[ROWS + TOK * b : ROWS + TOK * (b + 1), :]
            last = r_lanes[TOK - 1 : TOK, :]
            ends.append(last)
            scaled = (jnp.exp(last - r_lanes) * (dt_lanes * low.astype(F32))).astype(BF16)
            state = mm(scaled, bcc[span, 0:STATE], TN).astype(BF16)
            u[2 * j, b] = state[0:HEAD, :]
            u[2 * j + 1, b] = state[HEAD:, :]
        shrink = jnp.exp(jnp.concatenate([*ends, jnp.zeros((8 - SEQS, 128), F32)], axis=0))
        turned = pltpu.roll(shrink, HEAD, 1)
        own_decay[2 * j] = jnp.where(first, shrink, turned)
        own_decay[2 * j + 1] = jnp.where(first, turned, shrink)
        for q in range(2):
            to = 2 * j + q

            @pl.when(to != me)
            def _():
                chunk_copy(u, u_all, u_send, u_recv, to, me).start()
                chunk_copy(own_decay, decay, e_send, e_recv, to, me).start()

        return 0

    pairs_loop(0, PAIRS, front_pair)
    u_all[me] = u[me]
    decay[me] = own_decay[me]

    def inside_pair(j, _):
        cols = lane_block(j)
        for b in range(SEQS):
            span = slice(TOK * b, TOK * (b + 1))
            one, two = decay_pair(r_wide[span, cols], r_rows[j, :, span])
            both = jnp.concatenate([scores[b] * one, scores[b] * two], axis=1).astype(BF16)
            stepped = (dt_wide[span, cols] * xc[span, cols].astype(F32)).astype(BF16)
            y_in[span, cols] = mm(both, block_diagonal(stepped), NN)
        return 0

    pairs_loop(0, 6, inside_pair)
    each_other(me, lambda other: chunk_copy(u, u_all, u_send, u_recv, other, other).wait_recv())
    each_other(me, lambda other: chunk_copy(own_decay, decay, e_send, e_recv, other, other).wait_recv())

    def chunk_step(c, carry):
        after = []
        for b in range(SEQS):
            s_own[c, b] = carry[b].astype(BF16)
            after.append(decay[c, b : b + 1, :] * carry[b] + u_all[c, b].astype(F32))
        return tuple(after)

    lax.fori_loop(0, HEADS, chunk_step, tuple(jnp.zeros((HEAD, STATE), F32) for _ in range(SEQS)))
    each_other(me, lambda other: chunk_copy(s_own, start, s_send, s_recv, other, me).start())
    start[me] = s_own[me]
    pairs_loop(6, PAIRS, inside_pair)
    each_other(me, lambda other: chunk_copy(s_own, start, s_send, s_recv, other, other).wait_recv())
    each_other(me, lambda other: chunk_copy(u, u_all, u_send, u_recv, other, me).wait_send())
    each_other(me, lambda other: chunk_copy(own_decay, decay, e_send, e_recv, other, me).wait_send())
    each_other(me, lambda other: chunk_copy(s_own, start, s_send, s_recv, other, me).wait_send())


def head(*args):
    vmem = pl.BlockSpec(memory_space=pltpu.VMEM)
    outs = [
        ((ROWS, INNER), BF16), ((ROWS, 2 * STATE), BF16), ((ROWS, HEADS), F32), ((ROWS, INNER), F32), ((ROWS, INNER), F32),
        ((PAIRS, 8, ROWS), F32), ((ROWS, INNER), F32), (STATES_SHAPE, BF16), ((HEADS, 8, 128), F32),
    ]
    return pl.pallas_call(
        head_kernel,
        out_shape=[jax.ShapeDtypeStruct(s, d) for s, d in outs],
        in_specs=[vmem] * len(args),
        out_specs=[vmem] * len(outs),
        scratch_shapes=[
            pltpu.VMEM((ROWS, HEADS), F32), pltpu.VMEM((SEQS, TOK, TOK), F32), *[pltpu.VMEM(STATES_SHAPE, BF16)] * 2,
            pltpu.VMEM((HEADS, 8, 128), F32), pltpu.VMEM(STATES_SHAPE, BF16),
            *[pltpu.SemaphoreType.DMA((HEADS,))] * 6,
        ],
        compiler_params=pltpu.CompilerParams(
            vmem_limit_bytes=VMEM_LIMIT, collective_id=3, has_side_effects=True
        ),
        cost_estimate=pl.CostEstimate(flops=int(2e9), bytes_accessed=int(2e7), transcendentals=0),
    )(*args)


WIDE = 512
QUADS = INNER // WIDE


def fold(values):
    return sum((values[:, 128 * i : 128 * (i + 1)] for i in range(1, WIDE // 128)), values[:, 0:128])


def middle_kernel(
    y_in, xc, bcc, r, start, d_skip, normed, cot, w_z, w_out, gain,
    mixed, d_y, d_gate, own, d_gain, row_dot,
    y_all, gate, d_mixed, square, cross, scale, slope,
):
    phase = pl.program_id(0)
    quad = pl.program_id(1)
    ex = (iota((HEADS, WIDE), 0) == 8 * quad + (iota((HEADS, WIDE), 1) >> 6)).astype(F32)
    skip = d_skip[...]

    @pl.when(phase == 0)
    def _():
        gate[quad] = mm(normed[0:ROWS, :], w_z[...], NN)
        d_mixed[quad] = mm(cot[...], w_out[...], NT)

    z = gate[quad]
    sig = jax.nn.sigmoid(z)
    pulled = d_mixed[quad] * gain[...]

    @pl.when(phase == 0)
    def _():
        @pl.when(quad == 0)
        def _():
            square[...] = jnp.zeros_like(square)
            cross[...] = jnp.zeros_like(cross)

        for b in range(SEQS):
            span = slice(TOK * b, TOK * (b + 1))
            before = jnp.concatenate([start[h, b] for h in range(8)], axis=0)
            grown = jnp.exp(r[span, :])
            y_all[quad, span, :] = y_in[span, :] + grown * mm(bcc[span, STATE:], before, NT)
        y = (y_all[quad] + skip * xc[...].astype(F32)).astype(BF16).astype(F32)
        gated = y * (z * sig)
        square[...] += fold(gated * gated)
        cross[...] += fold(pulled * gated)

    @pl.when(phase == 1)
    def _():
        @pl.when(quad == 0)
        def _():
            inv = lax.rsqrt(jnp.sum(square[...], axis=1, keepdims=True) * (1.0 / INNER) + EPS)
            mean = jnp.sum(cross[...], axis=1, keepdims=True) * (1.0 / INNER)
            scale[...] = jnp.broadcast_to(inv, scale.shape)
            slope[...] = jnp.broadcast_to(inv * inv * inv * mean, slope.shape)
            row_dot[...] = jnp.zeros_like(row_dot)

        y = (y_all[quad] + skip * xc[...].astype(F32)).astype(BF16).astype(F32)
        silu = z * sig
        gated = y * silu
        inv = jnp.concatenate([scale[...]] * 4, axis=1)
        unit = gated * inv
        mixed[...] = (unit * gain[...]).astype(BF16)
        d_gain[...] = jnp.sum(d_mixed[quad] * unit, axis=0, keepdims=True)
        d_gated = inv * pulled - gated * jnp.concatenate([slope[...]] * 4, axis=1)
        low = (d_gated * silu).astype(BF16)
        d_y[...] = low
        d_gate[...] = (d_gated * y * (sig * (1.0 + z * (1.0 - sig)))).astype(BF16)
        row_dot[...] += head_sums(low.astype(F32) * y_all[quad], ex)
        for b in range(SEQS):
            span = slice(TOK * b, TOK * (b + 1))
            grown = jnp.exp(r[span, :])
            state = mm((grown * low[span, :].astype(F32)).astype(BF16), bcc[span, STATE:], TN).astype(BF16)
            for h in range(8):
                own[h, b] = state[HEAD * h : HEAD * (h + 1), :]


def middle(y_in, xc, bcc, r, start, d_skip, normed, cot, w_z, w_out, gain):
    def cols(rows):
        return pl.BlockSpec((rows, WIDE), lambda p, j: (0, j))

    def first(rows):
        return pl.BlockSpec((rows, WIDE), lambda p, j: (0, jnp.where(p == 0, j, QUADS - 1)))

    def second(rows):
        return pl.BlockSpec((rows, WIDE), lambda p, j: (0, jnp.where(p == 1, j, 0)))

    out_rows = pl.BlockSpec((WIDE, w_out.shape[1]), lambda p, j: (jnp.where(p == 0, j, QUADS - 1), 0))
    states_in = pl.BlockSpec((8, SEQS, HEAD, STATE), lambda p, j: (jnp.where(p == 0, j, QUADS - 1), 0, 0, 0))
    states_out = pl.BlockSpec((8, SEQS, HEAD, STATE), lambda p, j: (jnp.where(p == 1, j, 0), 0, 0, 0))
    return call(
        middle_kernel,
        [((ROWS, INNER), BF16), ((ROWS, INNER), BF16), ((ROWS, INNER), BF16), (STATES_SHAPE, BF16), ((1, INNER), F32), ((ROWS, HEADS), F32)],
        [second(ROWS), second(ROWS), second(ROWS), states_out, second(1), whole((ROWS, HEADS))],
        [first(ROWS), cols(ROWS), whole((ROWS, 2 * STATE)), cols(ROWS), states_in, cols(1), whole(normed.shape), whole(cot.shape), first(w_z.shape[0]), out_rows, cols(1)],
        grid=(2, QUADS),
        scratch=[pltpu.VMEM((QUADS, ROWS, WIDE), F32)] * 3 + [pltpu.VMEM((ROWS, 128), F32)] * 4,
    )(y_in, xc, bcc, r, start, d_skip, normed, cot, w_z, w_out, gain)


REDUCE = (("y", "z", "x"), ("z", "x", "y"), ("x", "y", "z")) + (("x", "y", "z"), ("y", "z", "x"), ("z", "x", "y"))
GATHER = (("l", "z", "x"), ("l", "x", "z"), ("x", "z", "l")) * 2
PIECE = 128
EXTRA = 32
PIECE_ROWS = (80, 48 + 32, 96, 48, 48, 32 + EXTRA)
EARLY, LATE = (0, 1, 2), (3, 4, 5)
SETS = len(PIECE_ROWS)
SMALL = 3 * 128
VECTOR = (16, INNER)


def tail_kernel(
    v, decay, xc, d_y, bcc, dt, dt_wide, r_wide, r_rows, x_raw, start, bc_raw, dt_raw, row_dot,
    taps_x, bias_x, taps_bc, bias_bc, dt_bias, a_log, d_skip, g_norm,
    normed, d_gate, mixed, cot, layer_in, gain_in, full_z, full_x, full_out, full_small,
    out_za, out_zb, out_zc, out_xa, out_xb, out_xc, input_grad, layer_out, vector,
    weights, v_all, g_own, end, d_stepped, scores, d_scores, d_bc, sums, d_x_raw, d_small, g_x, g_bc, g_heads,
    d_normed, halo_out, halo_in, few_own, few_got,
    keep_n, keep_m, next_n, next_m, sib_n, sib_gate, sib_m, sib_cot, sib_wide, sib_small,
    parts_za, parts_zb, parts_zc, parts_xa, parts_xb, parts_xc,
    got_za1, got_zb1, got_zc1, got_xa1, got_xb1, got_xc1, sum_za1, sum_zb1, sum_zc1, sum_xa1, sum_xb1, sum_xc1,
    got_za2, got_zb2, got_zc2, got_xa2, got_xb2, got_xc2, sum_za2, sum_zb2, sum_zc2, sum_xa2, sum_xb2, sum_xc2,
    got_za3, got_zb3, got_zc3, got_xa3, got_xb3, got_xc3,
    v_send, v_recv, g_send, g_recv, sib_send, sib_recv, red_send, red_recv, all_send, all_recv,
    few_send, few_recv, halo_sem, load_sem,
):
    at = position()
    me = lax.axis_index("seq")
    core = at["core"]
    sibling = peers(at, "core")[0]
    barrier = greet_chunks(me)
    others = [sibling] + peers(at, "y")
    for other in others:
        pl.semaphore_signal(barrier, inc=1, device_id=device(other), device_id_type=pl.DeviceIdType.MESH)
    pl.semaphore_wait(barrier, HEADS - 1 + len(others))
    started = []

    def copy(src, dst, send, recv, to):
        one = pltpu.make_async_remote_copy(
            src_ref=src, dst_ref=dst, send_sem=send, recv_sem=recv,
            device_id=device(to), device_id_type=pl.DeviceIdType.MESH,
        )
        one.start()
        started.append(one)
        return one

    def swap_start(src, dst, send, recv):
        each_other(me, lambda other: chunk_copy(src, dst, send, recv, other, me).start())
        dst[me] = src[me]

    def swap_wait(src, dst, send, recv):
        each_other(me, lambda other: chunk_copy(src, dst, send, recv, other, other).wait_recv())

    def swap_sent(src, dst, send, recv):
        each_other(me, lambda other: chunk_copy(src, dst, send, recv, other, me).wait_send())

    swap_start(v, v_all, v_send, v_recv)

    def columns(ref, high, which, size):
        return ref.at[:, lane_block(2 * high + which, size)]

    def transposed(ref, high, which, size):
        return ref[:, lane_block(2 * high + which, size)].astype(F32).T.astype(BF16)

    pairs = [(columns(normed, h, 1 - core, 256), sib_n.at[h]) for h in range(2)] + [(d_gate, sib_gate)]
    pairs += [(columns(mixed, h, 1 - core, 512), sib_m.at[h]) for h in range(2)] + [(cot, sib_cot)]
    from_sibling = [copy(a, b, sib_send.at[i], sib_recv.at[i], sibling) for i, (a, b) in enumerate(pairs)]

    half = weights.shape[2]
    halves = (slice(0, half), slice(half, 2 * half))

    def load(views):
        going = [pltpu.make_async_copy(views[h], weights.at[h], load_sem.at[h]) for h in range(2)]
        for one in going:
            one.start()
        return going

    loading = load([full_z.at[:, h] for h in halves])

    d_scores[...] = jnp.zeros_like(d_scores)
    for b in range(SEQS):
        span = slice(TOK * b, TOK * (b + 1))
        scores[b] = mm(bcc[span, STATE:], bcc[span, 0:STATE], NT)

    def inside_pair(j, _):
        cols = lane_block(j)
        for b in range(SEQS):
            span = slice(TOK * b, TOK * (b + 1))
            first, second = decay_pair(r_wide[span, cols], r_rows[j, :, span])
            both = jnp.concatenate([scores[b] * first, scores[b] * second], axis=0).astype(BF16)
            stepped = (dt_wide[span, cols] * xc[span, cols].astype(F32)).astype(BF16)
            wide = block_diagonal(d_y[span, cols])
            d_stepped[span, cols] = mm(both, wide, TN)
            d_both = mm(wide, stepped, NT)
            d_scores[b] += d_both[0:TOK, :] * first + d_both[TOK:, :] * second
        return 0

    pairs_loop(0, PAIRS, inside_pair)
    for b in range(SEQS):
        span = slice(TOK * b, TOK * (b + 1))
        low = d_scores[b].astype(BF16)
        d_bc[span, 0:STATE] = mm(low, bcc[span, STATE:], TN)
        d_bc[span, STATE:] = mm(low, bcc[span, 0:STATE], NN)

    swap_wait(v, v_all, v_send, v_recv)

    def chunk_step(i, carry):
        c = HEADS - 1 - i
        after = []
        for b in range(SEQS):
            g_own[c, b] = carry[b].astype(BF16)
            after.append(decay[c, b : b + 1, :] * carry[b] + v_all[c, b].astype(F32))
        return tuple(after)

    lax.fori_loop(0, HEADS, chunk_step, tuple(jnp.zeros((HEAD, STATE), F32) for _ in range(SEQS)))
    swap_start(g_own, end, g_send, g_recv)

    parts = (parts_za, parts_zb, parts_zc, parts_xa, parts_xb, parts_xc)
    got = (
        (got_za1, got_zb1, got_zc1, got_xa1, got_xb1, got_xc1),
        (got_za2, got_zb2, got_zc2, got_xa2, got_xb2, got_xc2),
        (got_za3, got_zb3, got_zc3, got_xa3, got_xb3, got_xc3),
    )
    partial = (
        (sum_za1, sum_zb1, sum_zc1, sum_xa1, sum_xb1, sum_xc1),
        (sum_za2, sum_zb2, sum_zc2, sum_xa2, sum_xb2, sum_xc2),
    )
    outs = (out_za, out_zb, out_zc, out_xa, out_xb, out_xc)
    arriving = [None] * SETS

    def send_stage(stage, which, src):
        axis = REDUCE[which][stage]
        arriving[which] = [
            copy(
                src.at[to[axis]], got[stage][which].at[d],
                red_send.at[which, stage, d], red_recv.at[which, stage, d], to,
            )
            for d, to in enumerate(peers(at, axis))
        ]

    def arrived(which):
        for one in arriving[which]:
            one.wait_recv()

    def add_stage(stage, which):
        arrived(which)
        src = parts[which] if stage == 0 else partial[0][which]
        dst, came = partial[stage][which], got[stage][which]
        mine = at[REDUCE[which][stage]]

        def add(i, _):
            for j in range(4) if stage == 0 else ((),):
                index = (i, j) if stage == 0 else (i,)
                value = src[(mine, *index)].astype(F32)
                for d in range(3):
                    value = value + came[(d, *index)].astype(F32)
                dst[index] = value.astype(BF16)
            return 0

        lax.fori_loop(0, 4, add, 0)
        send_stage(stage + 1, which, dst)

    def gather_stage(stage, which):
        first, second, third = GATHER[which]
        index = (at[third], at[second], at[first])[: 3 - stage]
        ref = outs[which].at[index]
        arriving[which] = [
            copy(ref, ref, all_send.at[which, stage, d], all_recv.at[which, stage, d], to)
            for d, to in enumerate(peers(at, (first, second, third)[stage]))
        ]

    def last_add(which):
        arrived(which)
        first, second, third = GATHER[which]
        value = partial[1][which][at[REDUCE[which][2]]].astype(F32)
        for d in range(3):
            value = value + got[2][which][d].astype(F32)
        outs[which][at[third], at[second], at[first]] = value.astype(BF16)
        gather_stage(0, which)

    def gather_next(stage, which):
        arrived(which)
        gather_stage(stage, which)

    for h in range(2):
        keep_n[256 * h : 256 * (h + 1), :] = transposed(normed, h, core, 256)
        keep_m[512 * h : 512 * (h + 1), :] = transposed(mixed, h, core, 512)
    for one in from_sibling[:3]:
        one.wait_recv()
    for h in range(2):
        next_n[256 * h : 256 * (h + 1), :] = sib_n[h].astype(F32).T.astype(BF16)

    def tile_z(n, _):
        cols = lane_block(n, 256)
        res = mm(keep_n[:, 0:ROWS], d_gate[:, cols], NN) + mm(next_n[:, 0:ROWS], sib_gate[:, cols], NN)
        for y in range(4):
            for k in range(2):
                block = res[128 * y : 128 * y + 128, 128 * k : 128 * k + 128].astype(BF16)
                x, z = n // 2, (n % 2) * 2 + k
                parts_za[y, z, x] = block[0:80]
                parts_zb[z, x, y, 0:48] = block[80:128]
        return 0

    lax.fori_loop(0, 8, tile_z, 0)
    send_stage(0, 0, parts_za)
    for one in from_sibling[3:]:
        one.wait_recv()
    for h in range(2):
        next_m[512 * h : 512 * (h + 1), :] = sib_m[h].astype(F32).T.astype(BF16)

    def tile_out(n, _):
        cols = lane_block(n, 256)
        res = mm(keep_m[...], cot[:, cols], NN) + mm(next_m[...], sib_cot[:, cols], NN)
        for y in range(4):
            for half in range(2):
                for k in range(2):
                    row = 256 * y + 128 * half
                    block = res[row : row + 128, 128 * k : 128 * k + 128].astype(BF16)
                    x, z = half * 2 + n // 2, (n % 2) * 2 + k
                    parts_zb[z, x, y, 48:80] = block[0:32]
                    parts_zc[x, y, z] = block[32:128]
        return 0

    lax.fori_loop(0, 4, tile_out, 0)
    send_stage(0, 1, parts_zb)
    send_stage(0, 2, parts_zc)

    for one in loading:
        one.wait()
    for n in range(4):
        cols = slice(256 * n, 256 * (n + 1))
        d_normed[0:ROWS, cols] = sum(mm(d_gate[:, h], weights[i, cols, :], NT) for i, h in enumerate(halves))
    loading = load([full_x.at[:, h] for h in halves])

    swap_wait(g_own, end, g_send, g_recv)
    sums[...] = jnp.zeros_like(sums)

    def back_pair(j, _):
        cols = lane_block(j)
        ex = pair_matrix(j)
        skip = d_skip[:, cols]
        raw = x_raw[:, cols].astype(F32)
        halos, grads = [], None
        d_steps, dots, end_rows = [], [], []
        skip_sum = jnp.zeros((1, 128), F32)
        for b in range(SEQS):
            span = slice(TOK * b, TOK * (b + 1))
            r_lanes = r_wide[span, cols]
            dt_lanes = dt_wide[span, cols]
            last = r_lanes[TOK - 1 : TOK, :]
            grown = jnp.exp(r_lanes)
            to_end = jnp.exp(last - r_lanes)
            before = jnp.concatenate([start[2 * j, b], start[2 * j + 1, b]], axis=0)
            after = jnp.concatenate([end[2 * j, b], end[2 * j + 1, b]], axis=0)
            x = xc[span, cols].astype(F32)
            dy = d_y[span, cols].astype(F32)
            stepped = (dt_lanes * x).astype(BF16).astype(F32)
            carried = to_end * mm(bcc[span, 0:STATE], after, NT)
            d_step = d_stepped[span, cols] + carried
            dots.append(stepped * d_step)
            d_x = dt_lanes * d_step + skip * dy
            d_steps.append(x * d_step)
            inner = lane_sums(before.astype(F32) * after.astype(F32))
            end_rows.append(jnp.sum(stepped * carried, axis=0, keepdims=True) + jnp.exp(last) * inner)
            d_bc[span, STATE:] += mm((grown * dy).astype(BF16), before, NN)
            d_bc[span, 0:STATE] += mm((to_end * stepped).astype(BF16), after, NN)
            skip_sum = skip_sum + jnp.sum(dy * x, axis=0, keepdims=True)
            d_pad, d_taps, d_bias = conv_back(padded_of(raw, b), taps_x[:, cols], bias_x[:, cols], d_x)
            d_x_raw[span, cols] = d_pad[HALO:, :].astype(BF16)
            halos.append(d_pad[0:HALO, :])
            found = [*d_taps, d_bias]
            grads = found if grads is None else [g + p for g, p in zip(grads, found)]
        d_x_raw[ROWS:, cols] = jnp.concatenate(halos, axis=0).astype(BF16)
        g_x[:, cols] = jnp.concatenate([*grads, jnp.zeros((8 - TAPS - 1, 128), F32)], axis=0)
        few = jnp.concatenate([*end_rows, skip_sum, jnp.zeros((5, 128), F32)], axis=0)
        sums[...] += head_sums(jnp.concatenate([*d_steps, *dots, few], axis=0), ex)
        return 0

    wide_coming = []
    for quarter in range(4):
        pairs_loop(4 * quarter, 4 * quarter + 4, back_pair)
        cols = slice(512 * quarter, 512 * (quarter + 1))
        wide_coming.append(
            copy(d_x_raw.at[:, cols], sib_wide.at[:, cols], sib_send.at[6 + quarter], sib_recv.at[6 + quarter], sibling)
        )
    raw = bc_raw[...].astype(F32)
    halos, grads = [], None
    for b in range(SEQS):
        span = slice(TOK * b, TOK * (b + 1))
        d_pad, d_taps, d_bias = conv_back(padded_of(raw, b), taps_bc[...], bias_bc[...], d_bc[span, :])
        d_small[span, 0 : 2 * STATE] = d_pad[HALO:, :].astype(BF16)
        halos.append(d_pad[0:HALO, :])
        found = [*d_taps, d_bias]
        grads = found if grads is None else [g + p for g, p in zip(grads, found)]
    d_small[ROWS:, 0 : 2 * STATE] = jnp.concatenate(halos, axis=0).astype(BF16)
    d_small[ROWS:, 2 * STATE :] = jnp.zeros((ALL - ROWS, SMALL - 2 * STATE), BF16)
    g_bc[...] = jnp.concatenate([*grads, jnp.zeros((8 - TAPS - 1, 2 * STATE), F32)], axis=0)
    rate = -jnp.exp(a_log[...])
    tri = causal_mask().astype(F32)
    is_last = iota((TOK, HEADS), 0) == TOK - 1
    bias_sum = jnp.zeros((1, HEADS), F32)
    log_sum = jnp.zeros((1, HEADS), F32)
    for b in range(SEQS):
        span = slice(TOK * b, TOK * (b + 1))
        step = dt[span, :]
        d_dt = sums[span, :]
        d_r = row_dot[span, :] - sums[ROWS + TOK * b : ROWS + TOK * (b + 1), :]
        d_r = d_r + jnp.where(is_last, sums[2 * ROWS + b : 2 * ROWS + b + 1, :], 0.0)
        d_log = mm(tri, d_r, TN, HIGHEST)
        d_pre = (d_dt + rate * d_log) * jax.nn.sigmoid(dt_raw[span, :].astype(F32) + dt_bias[...])
        d_small[span, 2 * STATE :] = jnp.concatenate(
            [d_pre, jnp.zeros((TOK, SMALL - 2 * STATE - HEADS), F32)], axis=1
        ).astype(BF16)
        bias_sum = bias_sum + jnp.sum(d_pre, axis=0, keepdims=True)
        log_sum = log_sum + jnp.sum(d_log * step, axis=0, keepdims=True) * rate
    g_heads[...] = jnp.concatenate(
        [bias_sum, log_sum, sums[2 * ROWS + 2 : 2 * ROWS + 3, :], jnp.zeros((5, HEADS), F32)], axis=0
    )
    small_coming = copy(d_small, sib_small, sib_send.at[10], sib_recv.at[10], sibling)

    for which in EARLY:
        add_stage(0, which)

    def tile_x(n, _):
        cols = lane_block(n, 256)
        res = mm(keep_n[...], d_x_raw[:, cols], NN) + mm(next_n[...], sib_wide[:, cols], NN)
        for y in range(4):
            for k in range(2):
                block = res[128 * y : 128 * y + 128, 128 * k : 128 * k + 128].astype(BF16)
                x, z = n // 2, (n % 2) * 2 + k
                parts_xa[x, y, z] = block[0:48]
                parts_xb[y, z, x] = block[48:96]
                parts_xc[z, x, y, 0:32] = block[96:128]
        return 0

    for quarter in range(4):
        wide_coming[quarter].wait_recv()
        lax.fori_loop(2 * quarter, 2 * quarter + 2, tile_x, 0)
    send_stage(0, 3, parts_xa)
    send_stage(0, 4, parts_xb)
    small_coming.wait_recv()
    res = mm(keep_n[...], d_small[...], NN) + mm(next_n[...], sib_small[...], NN)
    for y in range(4):
        for z in range(4):
            row = 128 * y + EXTRA * z
            for k in range(3):
                parts_xc[z, k, y, 32:] = res[row : row + EXTRA, 128 * k : 128 * k + 128].astype(BF16)
            parts_xc[z, 3, y, 32:] = jnp.zeros((EXTRA, 128), BF16)
    send_stage(0, 5, parts_xc)
    for which in EARLY:
        add_stage(1, which)

    for one in loading:
        one.wait()
    d_normed[ROWS:, :] = jnp.zeros((ALL - ROWS, d_normed.shape[1]), F32)
    for n in range(4):
        cols = slice(256 * n, 256 * (n + 1))
        d_normed[:, cols] += mm(d_small[...], full_small[cols, :], NT) + sum(
            mm(d_x_raw[:, h], weights[i, cols, :], NT) for i, h in enumerate(halves)
        )
    loading = load([full_out.at[h, :] for h in halves])
    halo_out[...] = d_normed[ROWS:, :]
    halo = pltpu.make_async_remote_copy(
        src_ref=halo_out, dst_ref=halo_in, send_sem=halo_sem.at[0], recv_sem=halo_sem.at[1],
        device_id={"seq": lax.rem(me + HEADS - 1, HEADS)}, device_id_type=pl.DeviceIdType.MESH,
    )
    halo.start()
    started.append(halo)
    for which in EARLY:
        last_add(which)
    halo.wait_recv()
    inner = jnp.where(me == HEADS - 1, 0.0, 1.0)
    for b in range(SEQS):
        near = slice(TOK * (b + 1) - HALO, TOK * (b + 1))
        d_normed[near, :] += inner * halo_in[HALO * b : HALO * (b + 1), :]
    g_in = jnp.zeros((1, d_normed.shape[1]), F32)
    for n in range(4):
        span = slice(64 * n, 64 * (n + 1))
        hidden = layer_in[span, :].astype(F32)
        inv = lax.rsqrt(jnp.mean(hidden * hidden, axis=1, keepdims=True) + EPS)
        unit = hidden * inv
        grad = d_normed[span, :]
        g_in = g_in + jnp.sum(grad * unit, axis=0, keepdims=True)
        pulled = grad * gain_in[...]
        d_hidden = inv * (pulled - unit * jnp.mean(pulled * unit, axis=1, keepdims=True))
        input_grad[span, :] = cot[span, :].astype(F32) + d_hidden

    few_axes = ("core", "x", "z", "y")
    rest = jnp.concatenate(
        [
            g_bc[...], jnp.concatenate([g_heads[...], jnp.zeros((8, 128 - HEADS), F32)], axis=1),
            jnp.zeros((8, INNER - 2 * STATE - 128), F32),
        ],
        axis=1,
    )
    wide_in = jnp.concatenate([g_in, jnp.zeros((1, INNER - g_in.shape[1]), F32)], axis=1)
    few = jnp.concatenate([g_x[...], g_norm[...], wide_in, rest[0 : TAPS + 1], jnp.zeros((1, INNER), F32)], axis=0)

    few_coming = [None]

    def few_start(stage, value):
        few_own[stage] = value.astype(BF16)
        axis = few_axes[stage]
        few_got[stage, at[axis]] = few_own[stage]
        few_coming[0] = [
            copy(
                few_own.at[stage], few_got.at[stage, at[axis]],
                few_send.at[stage, d], few_recv.at[stage, d], to,
            )
            for d, to in enumerate(peers(at, axis))
        ]

    def few_sum(stage):
        for one in few_coming[0]:
            one.wait_recv()
        value = few_got[stage, 0].astype(F32)
        for i in range(1, 2 if stage == 0 else 4):
            value = value + few_got[stage, i].astype(F32)
        return value

    few_start(0, few)
    for which in EARLY:
        gather_next(1, which)
    for which in LATE:
        add_stage(0, which)
    few_start(1, few_sum(0))
    for which in LATE:
        add_stage(1, which)
    few_start(2, few_sum(1))
    for which in EARLY:
        gather_next(2, which)
    for one in loading:
        one.wait()
    for n in range(4):
        cols = slice(256 * n, 256 * (n + 1))
        product = sum(mm(mixed[:, h], weights[i, :, cols], NN) for i, h in enumerate(halves))
        layer_out[:, cols] = (layer_in[:, cols].astype(F32) + product).astype(BF16)
    for which in LATE:
        last_add(which)
    few_start(3, few_sum(2))
    for which in LATE:
        gather_next(1, which)
    vector[...] = few_sum(3)
    for which in LATE:
        gather_next(2, which)
    for which in range(SETS):
        arrived(which)
    for one in started:
        one.wait_send()
    swap_sent(v, v_all, v_send, v_recv)
    swap_sent(g_own, end, g_send, g_recv)


def tail(*args):
    vmem = pl.BlockSpec(memory_space=pltpu.VMEM)
    hbm = pl.BlockSpec(memory_space=pl.ANY)
    specs = [vmem] * len(args)
    specs[-4] = specs[-3] = specs[-2] = hbm
    width = args[-1].shape[0]
    dims = {"x": 4, "z": 4, "l": 2}
    out_shape = [
        jax.ShapeDtypeStruct((*(dims[a] for a in reversed(GATHER[i])), PIECE_ROWS[i], 128), BF16) for i in range(SETS)
    ]
    out_shape += [jax.ShapeDtypeStruct((ROWS, width), d) for d in (F32, BF16)] + [jax.ShapeDtypeStruct(VECTOR, F32)]

    def bufs(*lead):
        return [pltpu.VMEM((*lead, PIECE_ROWS[i], 128), BF16) for i in range(SETS)]

    def sems(*shape):
        return [pltpu.SemaphoreType.DMA(shape)] * 2

    scratch = [
        pltpu.VMEM((2, width, INNER // 2), BF16), *[pltpu.VMEM(STATES_SHAPE, BF16)] * 3, pltpu.VMEM((ROWS, INNER), F32),
        *[pltpu.VMEM((SEQS, TOK, TOK), F32)] * 2, pltpu.VMEM((ROWS, 2 * STATE), F32),
        pltpu.VMEM((2 * ROWS + 8, HEADS), F32), pltpu.VMEM((ALL, INNER), BF16), pltpu.VMEM((ALL, SMALL), BF16),
        pltpu.VMEM((8, INNER), F32), pltpu.VMEM((8, 2 * STATE), F32), pltpu.VMEM((8, HEADS), F32),
        pltpu.VMEM((ALL, width), F32), *[pltpu.VMEM((SEQS * HALO, width), F32)] * 2,
        pltpu.VMEM((4, *VECTOR), BF16), pltpu.VMEM((4, 4, *VECTOR), BF16),
        *[pltpu.VMEM((512, ALL), BF16), pltpu.VMEM((1024, ROWS), BF16)] * 2,
        pltpu.VMEM((2, ALL, 256), BF16), pltpu.VMEM((ROWS, INNER), BF16), pltpu.VMEM((2, ROWS, 512), BF16),
        pltpu.VMEM((ROWS, width), BF16), pltpu.VMEM((ALL, INNER), BF16), pltpu.VMEM((ALL, SMALL), BF16),
        *bufs(4, 4, 4), *bufs(3, 4, 4), *bufs(4, 4), *bufs(3, 4), *bufs(4), *bufs(3),
        *sems(HEADS), *sems(HEADS), *sems(11), *sems(SETS, 3, 3), *sems(SETS, 3, 3), *sems(4, 3),
        pltpu.SemaphoreType.DMA((2,)), pltpu.SemaphoreType.DMA((2,)),
    ]
    return pl.pallas_call(
        tail_kernel,
        out_shape=out_shape,
        in_specs=specs,
        out_specs=[vmem] * len(out_shape),
        scratch_shapes=scratch,
        compiler_params=pltpu.CompilerParams(
            vmem_limit_bytes=VMEM_LIMIT, collective_id=1, has_side_effects=True
        ),
        cost_estimate=pl.CostEstimate(flops=int(8e9), bytes_accessed=int(4e7), transcendentals=0),
    )(*args)


def unpack_kernel(
    sum_za, sum_zb, sum_zc, sum_xa, sum_xb, sum_xc, total,
    out_z, out_x, out_out, out_extra, g_x, g_norm, g_in, g_bc, g_heads,
):
    for low in range(2):
        base = PIECE * low
        for z in range(4):
            cols = slice(128 * z, 128 * (z + 1))
            out_z[base : base + 80, cols] = sum_za[0, z, low].astype(F32)
            out_z[base + 80 : base + 128, cols] = sum_zb[z, 0, low, 0:48, :].astype(F32)
            out_out[low, 0, 0:32, cols] = sum_zb[z, 0, low, 48:80, :].astype(F32)
            out_out[low, 0, 32:128, cols] = sum_zc[low, z, 0].astype(F32)
            out_x[base : base + 48, cols] = sum_xa[0, z, low].astype(F32)
            out_x[base + 48 : base + 96, cols] = sum_xb[z, 0, low].astype(F32)
            out_x[base + 96 : base + 128, cols] = sum_xc[low, z, 0, 0:32, :].astype(F32)
            out_extra[0, low, EXTRA * z : EXTRA * (z + 1), :] = sum_xc[low, z, 0, 32:, :].astype(F32)

    @pl.when(pl.program_id(0) == 0)
    def _():
        g_x[...] = total[0:8, :]
        rest = total[8:16, :]
        g_norm[...] = rest[0:1, :]
        g_in[...] = rest[1:2, 0 : g_in.shape[1]]
        g_bc[...] = rest[2 : 2 + TAPS + 1, 0 : 2 * STATE]
        g_heads[...] = rest[2:5, 2 * STATE : 2 * STATE + 128]


def unpack(width, *gathered):
    few = ((8, INNER), (1, INNER), (1, width), (TAPS + 1, 2 * STATE), (3, 128))
    specs = []
    for i in range(SETS):
        def where(n, order=GATHER[i]):
            return tuple({"x": n, "z": 0, "l": 0}[a] for a in reversed(order)) + (0, 0)

        block = tuple({"x": 1, "z": 4, "l": 2}[a] for a in reversed(GATHER[i])) + (PIECE_ROWS[i], 128)
        specs.append(pl.BlockSpec(block, where))
    wide = pl.BlockSpec((2 * PIECE, WIDE), lambda i: (0, i))
    return call(
        unpack_kernel,
        [((2 * PIECE, INNER), F32), ((2 * PIECE, INNER), F32), ((2, 2, PIECE, 8 * 128), F32), ((4, 2, 4 * EXTRA, 128), F32)]
        + [(d, F32) for d in few],
        [
            wide, wide,
            pl.BlockSpec((2, 1, PIECE, WIDE), lambda i: (0, i // 2, 0, i % 2)),
            pl.BlockSpec((1, 2, 4 * EXTRA, 128), lambda i: (i, 0, 0, 0)), *[whole(d) for d in few],
        ],
        [*specs, whole(VECTOR)],
        grid=(4,),
    )(*gathered)


def gather_kernel(
    w_x, w_small, own, tokens, w_z, w_out, full_x, full_small, params, earlier, full_z, full_out, send, recv, here, own_send, own_recv, near_send, near_recv,
):
    at = position()
    sibling = peers(at, "core")[0]
    partner = moved(at, "y", 3 - at["y"])
    everyone = [sibling, partner] + [p for axis in ("x", "z", "l") for p in peers(at, axis)]
    me = lax.axis_index("seq")
    after, before = lax.rem(me + 1, HEADS), lax.rem(me + HEADS - 1, HEADS)
    barrier = pltpu.get_barrier_semaphore()
    for chunk in (after, before):
        pl.semaphore_signal(barrier, inc=1, device_id={"seq": chunk}, device_id_type=pl.DeviceIdType.MESH)
    greet(everyone, 2)
    started = []
    near = []
    for b in range(SEQS):
        one = pltpu.make_async_remote_copy(
            src_ref=tokens.at[b, TOK - 16 :], dst_ref=earlier.at[b], send_sem=near_send.at[b], recv_sem=near_recv.at[b],
            device_id={"seq": after}, device_id_type=pl.DeviceIdType.MESH,
        )
        one.start()
        started.append(one)
        near.append(one)

    def copy(src, dst, which, to, sems=(send, recv)):
        one = pltpu.make_async_remote_copy(
            src_ref=src, dst_ref=dst, send_sem=sems[0].at[which], recv_sem=sems[1].at[which],
            device_id=device(to), device_id_type=pl.DeviceIdType.MESH,
        )
        one.start()
        started.append(one)
        return one

    half, quarter = INNER // 2, w_out.shape[1] // 2
    flows = Flows(
        at,
        (
            (w_x, full_x, 0, half, "x", "z", 16), (w_x, full_x, half, half, "z", "x", 16),
            (w_small, full_small, 0, SMALL, "x", "z", 16),
            (w_z, full_z, 0, half, "x", "z", 16), (w_z, full_z, half, half, "z", "x", 16),
            (w_out, full_out, 0, quarter, "x", "z", 32), (w_out, full_out, quarter, quarter, "z", "x", 32),
        ),
        copy,
    )
    flows.begin()
    params_here = pltpu.make_async_copy(own, params.at[at["z"], at["x"], at["l"]], here.at[2])
    local = [
        pltpu.make_async_copy(w_x, full_x.at[flows.mine], here.at[0]),
        pltpu.make_async_copy(w_small, full_small.at[flows.mine], here.at[1]),
        params_here,
        pltpu.make_async_copy(w_z, full_z.at[flows.mine], here.at[3]),
        pltpu.make_async_copy(w_out, full_out.at[flows.mine], here.at[4]),
    ]
    for one in local:
        one.start()
    flows.own([(w_x, full_x), (w_small, full_small), (w_z, full_z), (w_out, full_out)])
    params_here.wait()

    def share(stage):
        axis = ("l", "x", "z")[stage]
        ref = params.at[(at["z"], at["x"], at["l"])[: 3 - stage]]
        return [copy(ref, ref, 3 * stage + d, to, (own_send, own_recv)) for d, to in enumerate(peers(at, axis))]

    shared = share(0)
    flows.spread()
    for one in shared:
        one.wait_recv()
    shared = share(1)
    flows.spread_more()
    for one in shared:
        one.wait_recv()
    shared = share(2)
    flows.forward()
    flows.finish()
    for one in shared + near:
        one.wait_recv()
    for one in (*local[:2], *local[3:]):
        one.wait()
    for one in started:
        one.wait_send()


def gather_weights(w_x, w_small, own, tokens, w_z, w_out):
    vmem = pl.BlockSpec(memory_space=pltpu.VMEM)
    hbm = pl.BlockSpec(memory_space=pl.ANY)
    return pl.pallas_call(
        gather_kernel,
        out_shape=[
            jax.ShapeDtypeStruct((4, *w_x.shape), BF16),
            jax.ShapeDtypeStruct((4, *w_small.shape), BF16),
            jax.ShapeDtypeStruct((4, 4, 2, 8, 128), F32),
            jax.ShapeDtypeStruct((SEQS, 16, tokens.shape[2]), BF16),
            jax.ShapeDtypeStruct((4, *w_z.shape), BF16),
            jax.ShapeDtypeStruct((4, *w_out.shape), BF16),
        ],
        in_specs=[vmem] * 4 + [hbm] * 2,
        out_specs=[vmem] * 4 + [hbm] * 2,
        scratch_shapes=[
            pltpu.SemaphoreType.DMA((81,)), pltpu.SemaphoreType.DMA((81,)), pltpu.SemaphoreType.DMA((5,)),
            pltpu.SemaphoreType.DMA((9,)), pltpu.SemaphoreType.DMA((9,)), pltpu.SemaphoreType.DMA((2,)), pltpu.SemaphoreType.DMA((2,)),
        ],
        compiler_params=pltpu.CompilerParams(
            vmem_limit_bytes=48 * 1024 * 1024, collective_id=2, has_side_effects=True
        ),
        cost_estimate=pl.CostEstimate(flops=int(1e6), bytes_accessed=int(4e7), transcendentals=0),
    )(w_x, w_small, own, tokens, w_z, w_out)


def shards(
    layer_in, gain_in, w_z, w_x, w_bc, w_dt, conv_x_weight, conv_x_bias, conv_bc_weight, conv_bc_bias,
    dt_bias, a_log, d_skip, gain_norm, w_out, cotangent,
):
    width = layer_in.shape[2]
    place = lax.axis_index("seq")
    own = jnp.concatenate([conv_x_weight.reshape(-1), conv_x_bias, dt_bias, a_log, d_skip, jnp.zeros((701,), F32)])
    small = jnp.concatenate([w_bc, w_dt, jnp.zeros((w_bc.shape[0], SMALL - 2 * STATE - HEADS), BF16)], axis=1)
    full_x, full_small, params, earlier, full_z, full_out = gather_weights(
        w_x, small, own.reshape(8, 128), layer_in, w_z, w_out
    )
    full_x = full_x.reshape(width, INNER)
    full_small = full_small.reshape(width, SMALL)
    params = params.reshape(HEADS, -1)
    taps_x = params[:, : TAPS * HEAD].reshape(HEADS, TAPS, HEAD).swapaxes(0, 1).reshape(TAPS, INNER)
    bias_x = params[:, TAPS * HEAD : (TAPS + 1) * HEAD].reshape(1, INNER)
    bias_dt, log_a, skip = (params[:, (TAPS + 1) * HEAD + i].reshape(1, HEADS) for i in range(3))
    bias_bc = conv_bc_bias.reshape(1, -1)
    skip_wide = jnp.repeat(skip, HEAD, axis=1)

    hidden = layer_in.astype(F32).reshape(ROWS, width)
    upstream = cotangent.reshape(ROWS, width)
    halo = earlier[:, HALO:].astype(F32)
    kept = (lax.broadcasted_iota(jnp.int32, halo.shape, 1) >= HALO - (TAPS - 1)) & (place > 0)
    halo = jnp.where(kept, halo, 0.0).reshape(SEQS * HALO, width)
    tokens = jnp.concatenate([hidden, halo], axis=0)
    inv = lax.rsqrt(jnp.mean(tokens * tokens, axis=-1, keepdims=True) + EPS)
    normed = (tokens * inv * gain_in[None, :]).astype(BF16)

    x_raw = mm(normed, full_x, NN).astype(BF16)
    small_raw = mm(normed, full_small, NN).astype(BF16)
    bc_raw, dt_raw = small_raw[:, : 2 * STATE], small_raw[:, 2 * STATE : 2 * STATE + HEADS]
    xc, bcc, dt, dt_wide, r_wide, r_rows, y_in, start, decay = head(
        x_raw, bc_raw, dt_raw, taps_x, bias_x, conv_bc_weight, bias_bc, bias_dt, log_a
    )
    full_z = full_z.reshape(width, INNER)
    full_out = full_out.reshape(INNER, width)
    mixed, d_y, d_gate, v, g_norm, row_dot = middle(
        y_in, xc, bcc, r_wide, start, skip_wide, normed, upstream, full_z, full_out, gain_norm.reshape(1, INNER)
    )
    *gathered, input_grad, layer_out, total = tail(
        v, decay, xc, d_y, bcc, dt, dt_wide, r_wide, r_rows, x_raw, start, bc_raw, dt_raw, row_dot,
        taps_x, bias_x, conv_bc_weight, bias_bc, bias_dt, log_a, skip_wide, g_norm,
        normed, d_gate, mixed, upstream, layer_in.reshape(ROWS, width), gain_in.reshape(1, width),
        full_z, full_x, full_out, full_small,
    )
    layer_out = layer_out.reshape(SEQS, TOK, width)
    input_grad = input_grad.reshape(SEQS, TOK, width)
    grad_w_z, grad_w_x, grad_w_out, extra, s_x, s_norm, s_in, s_bc, s_heads = unpack(width, *gathered, total)
    grad_w_out = grad_w_out.reshape(4 * PIECE, width)
    extra = extra.reshape(4, 2 * PIECE, 128)
    grad_w_bc = jnp.concatenate([extra[0], extra[1]], axis=1)
    grad_w_dt = extra[2][:, :HEADS]
    s_x = lax.dynamic_slice(s_x, (0, place * HEAD), (TAPS + 1, HEAD))
    s_norm, s_in = s_norm.reshape(INNER), s_in.reshape(width)
    s_heads = lax.dynamic_slice(s_heads, (0, place), (3, 1))
    return (
        layer_out, input_grad, s_in, grad_w_z, grad_w_x, grad_w_bc, grad_w_dt,
        s_x[:TAPS], s_x[TAPS], s_bc[:TAPS], s_bc[TAPS], s_heads[0], s_heads[1], s_heads[2], s_norm, grad_w_out,
    )


def solution(mesh):
    rows, heads = P("wshard", None), P("seq")
    tokens = P("wshard", "seq", None)
    return jax.shard_map(
        shards,
        mesh=mesh,
        in_specs=(
            tokens, P(), rows, rows, rows, rows, P(None, "seq"), heads, P(), P(), heads, heads, heads, P(), rows, tokens,
        ),
        out_specs=(
            tokens, tokens, P(), rows, rows, rows, rows, P(None, "seq"), heads, P(), P(), heads, heads, heads, P(), rows,
        ),
        check_vma=False,
    )
```

```python
import functools

import jax
import jax.numpy as jnp
from jax import lax
from jax.experimental import pallas as pl
from jax.experimental.pallas import tpu as pltpu
from jax.sharding import PartitionSpec as P

F32 = jnp.float32
BF16 = jnp.bfloat16
EPS = 1e-05
HIGHEST = lax.Precision.HIGHEST
HEADS = 32
HEAD = 64
STATE = 128
TOK = 128
SEQS = 2
ROWS = SEQS * TOK
HALO = 8
ALL = ROWS + SEQS * HALO
PAIRS = HEADS // 2
INNER = HEADS * HEAD
TAPS = 4


def mm(a, b, dims, precision=None):
    return lax.dot_general(a, b, ((dims[0], dims[1]), ((), ())), precision=precision, preferred_element_type=F32)


NN = ((1,), (0,))
NT = ((1,), (1,))
TN = ((0,), (0,))


def iota(shape, dim):
    return lax.broadcasted_iota(jnp.int32, shape, dim)


def pair_matrix(pair):
    upper = (iota((HEADS, 128), 1) >= HEAD).astype(jnp.int32)
    return (iota((HEADS, 128), 0) == 2 * pair + upper).astype(F32)


def pair_rows(pair):
    return (iota((8, HEADS), 1) == 2 * pair + iota((8, HEADS), 0)).astype(F32)


def head_sums(values, ex):
    high = values.astype(BF16)
    low = (values - high.astype(F32)).astype(BF16)
    ex = ex.astype(BF16)
    return mm(jnp.concatenate([high, low], axis=1), jnp.concatenate([ex, ex], axis=1), NT)


def three_terms(values):
    high = values.astype(BF16)
    rest = values - high.astype(F32)
    middle = rest.astype(BF16)
    low = (rest - middle.astype(F32)).astype(BF16)
    return jnp.concatenate([high, middle, low], axis=1)


def lane_sums(values):
    high = values.astype(BF16)
    low = (values - high.astype(F32)).astype(BF16)
    return mm(jnp.ones((8, 256), BF16), jnp.concatenate([high, low], axis=1), NT)[0:1, :]


def causal_mask():
    return iota((TOK, TOK), 0) >= iota((TOK, TOK), 1)


def shifted(padded, k):
    back = TAPS - 1 - k
    if back:
        padded = pltpu.roll(padded, back, 0)
    return padded[HALO:, :]


def padded_of(rows, b):
    return jnp.concatenate(
        [rows[ROWS + HALO * b : ROWS + HALO * (b + 1), :], rows[TOK * b : TOK * (b + 1), :]], axis=0
    )


def conv_pre(padded, taps, bias):
    total = bias
    for k in range(TAPS):
        total = total + taps[k : k + 1, :] * shifted(padded, k)
    return total


def conv_back(padded, taps, bias, grad):
    pre = conv_pre(padded, taps, bias)
    sig = jax.nn.sigmoid(pre)
    d_pre = grad * (sig * (1.0 + pre * (1.0 - sig)))
    low = jnp.concatenate([jnp.zeros((HALO, d_pre.shape[1]), F32), d_pre], axis=0)
    d_pad = taps[TAPS - 1 : TAPS, :] * low
    for k in range(TAPS - 1):
        d_pad = d_pad + taps[k : k + 1, :] * pltpu.roll(low, HALO + TOK - (TAPS - 1 - k), 0)
    d_taps = [jnp.sum(d_pre * shifted(padded, k), axis=0, keepdims=True) for k in range(TAPS)]
    return d_pad, d_taps, jnp.sum(d_pre, axis=0, keepdims=True)


def block_diagonal(pair_values):
    first = iota(pair_values.shape, 1) < HEAD
    zero = jnp.zeros_like(pair_values)
    return jnp.concatenate(
        [jnp.where(first, pair_values, zero), jnp.where(first, zero, pair_values)], axis=0
    )


def decay_pair(r_lanes, r_rows):
    mask = causal_mask()
    out = []
    for q in range(2):
        spread = r_lanes[:, HEAD * q : HEAD * q + 1] - r_rows[q : q + 1, :]
        out.append(jnp.exp(jnp.where(mask, spread, -1e30)))
    return out


def whole(shape):
    return pl.BlockSpec(shape, lambda *_: (0,) * len(shape))


def lanes(rows):
    return pl.BlockSpec((rows, 128), lambda j: (0, j))


STATES_SHAPE = (HEADS, SEQS, HEAD, STATE)
VMEM_LIMIT = 62 * 1024 * 1024


def call(kernel, outs, out_specs, in_specs, grid=(PAIRS,), scratch=(), cost=None):
    return pl.pallas_call(
        kernel,
        grid=grid,
        out_shape=[jax.ShapeDtypeStruct(s, d) for s, d in outs],
        in_specs=in_specs,
        out_specs=out_specs,
        scratch_shapes=scratch,
        compiler_params=pltpu.CompilerParams(
            vmem_limit_bytes=VMEM_LIMIT, dimension_semantics=("arbitrary",) * len(grid)
        ),
        cost_estimate=cost or pl.CostEstimate(flops=int(1e9), bytes_accessed=int(1e7), transcendentals=0),
    )


def position():
    seq, shard = lax.axis_index("seq"), lax.axis_index("wshard")
    high, core = shard // 2, shard % 2
    low = seq % 2
    return {"z": seq // 8, "x": (seq // 2) % 4, "y": high * 2 + low, "l": low, "core": core}


def device(at):
    return {"seq": at["z"] * 8 + at["x"] * 2 + at["y"] % 2, "wshard": (at["y"] // 2) * 2 + at["core"]}


def moved(at, axis, to):
    new = dict(at)
    if axis == "l":
        new["y"] = (at["y"] // 2) * 2 + to
        new["l"] = to
    else:
        new[axis] = to
        if axis == "y":
            new["l"] = to % 2
    return new


def peers(at, axis):
    size = 2 if axis in ("l", "core") else 4
    return [moved(at, axis, lax.rem(at[axis] + d, size)) for d in range(1, size)]


def greet(everyone, more=0):
    barrier = pltpu.get_barrier_semaphore()
    for other in everyone:
        pl.semaphore_signal(barrier, inc=1, device_id=device(other), device_id_type=pl.DeviceIdType.MESH)
    pl.semaphore_wait(barrier, len(everyone) + more)


class Flows:
    def __init__(self, at, flows, copy):
        self.at, self.flows, self.copy = at, flows, copy
        high = at["y"] // 2
        self.mine, self.opposite = high * 2 + at["core"], (1 - high) * 2 + at["core"]
        self.sibling = peers(at, "core")[0]
        self.partner = moved(at, "y", 3 - at["y"])
        self.last = []

    def view(self, ref, shard, row, count, first, size):
        row = pl.multiple_of(row, 16)
        if shard is None:
            return ref.at[pl.ds(row, count), first : first + size]
        return ref.at[shard, pl.ds(row, count), first : first + size]

    def begin(self):
        self.arriving = []
        for i, (src, ref, first, size, a, b, rows) in enumerate(self.flows):
            row = (self.at[b] * 4 + self.at[a]) * rows
            here = self.view(src, None, row, rows, first, size)
            there = self.view(ref, self.mine, row, rows, first, size)
            self.arriving.append(self.copy(here, there, i, self.partner))

    def spread(self):
        n = len(self.flows)
        self.second = []
        for i, (src, ref, first, size, a, b, rows) in enumerate(self.flows):
            self.arriving[i].wait_recv()
            piece = self.view(ref, self.opposite, (self.at[b] * 4 + self.at[a]) * rows, rows, first, size)
            self.second.append([self.copy(piece, piece, n + 3 * i + d, to) for d, to in enumerate(peers(self.at, a))])

    def spread_more(self):
        n = len(self.flows)
        self.third = []
        for i, (src, ref, first, size, a, b, rows) in enumerate(self.flows):
            for one in self.second[i]:
                one.wait_recv()
            block = self.view(ref, self.opposite, self.at[b] * 4 * rows, 4 * rows, first, size)
            self.third.append([self.copy(block, block, 4 * n + 3 * i + d, to) for d, to in enumerate(peers(self.at, b))])
            self.last.append(self.copy(block, block, 7 * n + i, self.sibling))

    def forward(self):
        n = len(self.flows)
        for i, (src, ref, first, size, a, b, rows) in enumerate(self.flows):
            for d in range(3):
                self.third[i][d].wait_recv()
                block = self.view(ref, self.opposite, lax.rem(self.at[b] + 3 - d, 4) * 4 * rows, 4 * rows, first, size)
                self.last.append(self.copy(block, block, 8 * n + 3 * i + d, self.sibling))

    def own(self, pairs):
        n = len(self.flows)
        for j, (src, ref) in enumerate(pairs):
            self.last.append(self.copy(src, ref.at[self.mine], 11 * n + j, self.sibling))

    def finish(self):
        for one in self.last:
            one.wait_recv()


def chunk_copy(src, dst, send, recv, to, slot):
    return pltpu.make_async_remote_copy(
        src_ref=src.at[to], dst_ref=dst.at[slot], send_sem=send, recv_sem=recv,
        device_id={"seq": to}, device_id_type=pl.DeviceIdType.MESH,
    )


def wait_others(ref, sem):
    rest = ref.at[pl.ds(0, HEADS - 1)]
    pltpu.make_async_copy(rest, rest, sem).wait()


def each_other(me, step):
    def go(d, _):
        step(lax.rem(me + d, HEADS))
        return 0

    lax.fori_loop(1, HEADS, go, 0)


def greet_chunks(me):
    barrier = pltpu.get_barrier_semaphore()
    each_other(
        me,
        lambda other: pl.semaphore_signal(
            barrier, inc=1, device_id={"seq": other}, device_id_type=pl.DeviceIdType.MESH
        ),
    )
    return barrier


def lane_block(j, size=128):
    return pl.ds(pl.multiple_of(j * size, size), size)


def pairs_loop(first, last, body):
    def two(i, _):
        body(2 * i, 0)
        body(2 * i + 1, 0)
        return 0

    lax.fori_loop(first // 2, last // 2, two, 0)


def head_kernel(
    x_raw, bc_raw, dt_raw, taps_x, bias_x, taps_bc, bias_bc, dt_bias, a_log,
    xc, bcc, dt, dt_wide, r_wide, r_rows, y_in, start, decay,
    r, terms, scores, u, u_all, own_decay, s_own, u_send, u_recv, e_send, e_recv, s_send, s_recv,
):
    me = lax.axis_index("seq")
    barrier = greet_chunks(me)
    raw = bc_raw[...].astype(F32)
    dt[...] = jax.nn.softplus(dt_raw[0:ROWS, :].astype(F32) + dt_bias[...])
    tri = causal_mask().astype(F32)
    rates = dt[...] * (-jnp.exp(a_log[...]))
    for b in range(SEQS):
        span = slice(TOK * b, TOK * (b + 1))
        pre = conv_pre(padded_of(raw, b), taps_bc[...], bias_bc[...])
        bcc[span, :] = (pre * jax.nn.sigmoid(pre)).astype(BF16)
        r[span, :] = mm(tri, rates[span, :], NN, HIGHEST)
        scores[b] = mm(bcc[span, STATE:], bcc[span, 0:STATE], NT)
    terms[...] = three_terms(jnp.concatenate([r[...], dt[...]], axis=0))
    first = iota((8, 128), 1) < HEAD
    pl.semaphore_wait(barrier, HEADS - 1)

    def front_pair(i, _):
        j = lax.rem(me // 2 + i, PAIRS)
        cols = lane_block(j)
        raw = x_raw[:, cols].astype(F32)
        ex = pair_matrix(j).astype(BF16)
        both = mm(terms[...], jnp.concatenate([ex] * 3, axis=0), NN)
        r_wide[:, cols] = both[0:ROWS, :]
        dt_wide[:, cols] = both[ROWS:, :]
        rows = pair_rows(j).astype(BF16)
        r_rows[j] = mm(jnp.concatenate([rows] * 3, axis=1), terms[0:ROWS, :], NT)
        ends = []
        for b in range(SEQS):
            span = slice(TOK * b, TOK * (b + 1))
            pre = conv_pre(padded_of(raw, b), taps_x[:, cols], bias_x[:, cols])
            low = (pre * jax.nn.sigmoid(pre)).astype(BF16)
            xc[span, cols] = low
            r_lanes = both[span, :]
            dt_lanes = both[ROWS + TOK * b : ROWS + TOK * (b + 1), :]
            last = r_lanes[TOK - 1 : TOK, :]
            ends.append(last)
            scaled = (jnp.exp(last - r_lanes) * (dt_lanes * low.astype(F32))).astype(BF16)
            state = mm(scaled, bcc[span, 0:STATE], TN).astype(BF16)
            u[2 * j, b] = state[0:HEAD, :]
            u[2 * j + 1, b] = state[HEAD:, :]
        shrink = jnp.exp(jnp.concatenate([*ends, jnp.zeros((8 - SEQS, 128), F32)], axis=0))
        turned = pltpu.roll(shrink, HEAD, 1)
        own_decay[2 * j] = jnp.where(first, shrink, turned)
        own_decay[2 * j + 1] = jnp.where(first, turned, shrink)
        for q in range(2):
            to = 2 * j + q

            @pl.when(to != me)
            def _():
                chunk_copy(u, u_all, u_send, u_recv, to, me).start()
                chunk_copy(own_decay, decay, e_send, e_recv, to, me).start()

        return 0

    pairs_loop(0, PAIRS, front_pair)
    u_all[me] = u[me]
    decay[me] = own_decay[me]

    def inside_pair(j, _):
        cols = lane_block(j)
        for b in range(SEQS):
            span = slice(TOK * b, TOK * (b + 1))
            one, two = decay_pair(r_wide[span, cols], r_rows[j, :, span])
            both = jnp.concatenate([scores[b] * one, scores[b] * two], axis=1).astype(BF16)
            stepped = (dt_wide[span, cols] * xc[span, cols].astype(F32)).astype(BF16)
            y_in[span, cols] = mm(both, block_diagonal(stepped), NN)
        return 0

    pairs_loop(0, 6, inside_pair)
    wait_others(u_all, u_recv)
    wait_others(decay, e_recv)

    def chunk_step(c, carry):
        after = []
        for b in range(SEQS):
            s_own[c, b] = carry[b].astype(BF16)
            after.append(decay[c, b : b + 1, :] * carry[b] + u_all[c, b].astype(F32))
        return tuple(after)

    lax.fori_loop(0, HEADS, chunk_step, tuple(jnp.zeros((HEAD, STATE), F32) for _ in range(SEQS)))
    each_other(me, lambda other: chunk_copy(s_own, start, s_send, s_recv, other, me).start())
    start[me] = s_own[me]
    pairs_loop(6, PAIRS, inside_pair)
    wait_others(start, s_recv)
    wait_others(u, u_send)
    wait_others(own_decay, e_send)
    wait_others(s_own, s_send)


def head(*args):
    vmem = pl.BlockSpec(memory_space=pltpu.VMEM)
    outs = [
        ((ROWS, INNER), BF16), ((ROWS, 2 * STATE), BF16), ((ROWS, HEADS), F32), ((ROWS, INNER), F32), ((ROWS, INNER), F32),
        ((PAIRS, 8, ROWS), F32), ((ROWS, INNER), F32), (STATES_SHAPE, BF16), ((HEADS, 8, 128), F32),
    ]
    return pl.pallas_call(
        head_kernel,
        out_shape=[jax.ShapeDtypeStruct(s, d) for s, d in outs],
        in_specs=[vmem] * len(args),
        out_specs=[vmem] * len(outs),
        scratch_shapes=[
            pltpu.VMEM((ROWS, HEADS), F32), pltpu.VMEM((2 * ROWS, 3 * HEADS), BF16), pltpu.VMEM((SEQS, TOK, TOK), F32),
            *[pltpu.VMEM(STATES_SHAPE, BF16)] * 2,
            pltpu.VMEM((HEADS, 8, 128), F32), pltpu.VMEM(STATES_SHAPE, BF16),
            *[pltpu.SemaphoreType.DMA] * 6,
        ],
        compiler_params=pltpu.CompilerParams(
            vmem_limit_bytes=VMEM_LIMIT, collective_id=3, has_side_effects=True
        ),
        cost_estimate=pl.CostEstimate(flops=int(2e9), bytes_accessed=int(2e7), transcendentals=0),
    )(*args)


WIDE = 512
QUADS = INNER // WIDE


def fold(values):
    return sum((values[:, 128 * i : 128 * (i + 1)] for i in range(1, WIDE // 128)), values[:, 0:128])


def middle_kernel(
    y_in, xc, bcc, r, start, d_skip, normed, cot, w_z, w_out, gain,
    mixed, d_y, d_gate, own, d_gain, row_dot,
    y_all, gate, d_mixed, square, cross, scale, slope,
):
    phase = pl.program_id(0)
    quad = pl.program_id(1)
    ex = (iota((HEADS, WIDE), 0) == 8 * quad + (iota((HEADS, WIDE), 1) >> 6)).astype(F32)
    skip = d_skip[...]

    @pl.when(phase == 0)
    def _():
        gate[quad] = mm(normed[0:ROWS, :], w_z[...], NN)
        d_mixed[quad] = mm(cot[...], w_out[...], NT)

    z = gate[quad]
    sig = jax.nn.sigmoid(z)
    pulled = d_mixed[quad] * gain[...]

    @pl.when(phase == 0)
    def _():
        @pl.when(quad == 0)
        def _():
            square[...] = jnp.zeros_like(square)
            cross[...] = jnp.zeros_like(cross)

        for b in range(SEQS):
            span = slice(TOK * b, TOK * (b + 1))
            before = jnp.concatenate([start[h, b] for h in range(8)], axis=0)
            grown = jnp.exp(r[span, :])
            y_all[quad, span, :] = y_in[span, :] + grown * mm(bcc[span, STATE:], before, NT)
        y = (y_all[quad] + skip * xc[...].astype(F32)).astype(BF16).astype(F32)
        gated = y * (z * sig)
        square[...] += fold(gated * gated)
        cross[...] += fold(pulled * gated)

    @pl.when(phase == 1)
    def _():
        @pl.when(quad == 0)
        def _():
            inv = lax.rsqrt(jnp.sum(square[...], axis=1, keepdims=True) * (1.0 / INNER) + EPS)
            mean = jnp.sum(cross[...], axis=1, keepdims=True) * (1.0 / INNER)
            scale[...] = jnp.broadcast_to(inv, scale.shape)
            slope[...] = jnp.broadcast_to(inv * inv * inv * mean, slope.shape)
            row_dot[...] = jnp.zeros_like(row_dot)

        y = (y_all[quad] + skip * xc[...].astype(F32)).astype(BF16).astype(F32)
        silu = z * sig
        gated = y * silu
        inv = jnp.concatenate([scale[...]] * 4, axis=1)
        unit = gated * inv
        mixed[...] = (unit * gain[...]).astype(BF16)
        d_gain[...] = jnp.sum(d_mixed[quad] * unit, axis=0, keepdims=True)
        d_gated = inv * pulled - gated * jnp.concatenate([slope[...]] * 4, axis=1)
        low = (d_gated * silu).astype(BF16)
        d_y[...] = low
        d_gate[...] = (d_gated * y * (sig * (1.0 + z * (1.0 - sig)))).astype(BF16)
        row_dot[...] += head_sums(low.astype(F32) * y_all[quad], ex)
        for b in range(SEQS):
            span = slice(TOK * b, TOK * (b + 1))
            grown = jnp.exp(r[span, :])
            state = mm((grown * low[span, :].astype(F32)).astype(BF16), bcc[span, STATE:], TN).astype(BF16)
            for h in range(8):
                own[h, b] = state[HEAD * h : HEAD * (h + 1), :]


def middle(y_in, xc, bcc, r, start, d_skip, normed, cot, w_z, w_out, gain):
    def cols(rows):
        return pl.BlockSpec((rows, WIDE), lambda p, j: (0, j))

    def first(rows):
        return pl.BlockSpec((rows, WIDE), lambda p, j: (0, jnp.where(p == 0, j, QUADS - 1)))

    def second(rows):
        return pl.BlockSpec((rows, WIDE), lambda p, j: (0, jnp.where(p == 1, j, 0)))

    out_rows = pl.BlockSpec((WIDE, w_out.shape[1]), lambda p, j: (jnp.where(p == 0, j, QUADS - 1), 0))
    states_in = pl.BlockSpec((8, SEQS, HEAD, STATE), lambda p, j: (jnp.where(p == 0, j, QUADS - 1), 0, 0, 0))
    states_out = pl.BlockSpec((8, SEQS, HEAD, STATE), lambda p, j: (jnp.where(p == 1, j, 0), 0, 0, 0))
    return call(
        middle_kernel,
        [((ROWS, INNER), BF16), ((ROWS, INNER), BF16), ((ROWS, INNER), BF16), (STATES_SHAPE, BF16), ((1, INNER), F32), ((ROWS, HEADS), F32)],
        [second(ROWS), second(ROWS), second(ROWS), states_out, second(1), whole((ROWS, HEADS))],
        [first(ROWS), cols(ROWS), whole((ROWS, 2 * STATE)), cols(ROWS), states_in, cols(1), whole(normed.shape), whole(cot.shape), first(w_z.shape[0]), out_rows, cols(1)],
        grid=(2, QUADS),
        scratch=[pltpu.VMEM((QUADS, ROWS, WIDE), F32)] * 3 + [pltpu.VMEM((ROWS, 128), F32)] * 4,
    )(y_in, xc, bcc, r, start, d_skip, normed, cot, w_z, w_out, gain)


REDUCE = (("y", "z", "x"), ("z", "x", "y"), ("x", "y", "z")) + (("x", "y", "z"), ("y", "z", "x"), ("z", "x", "y"))
GATHER = (("l", "z", "x"), ("l", "x", "z"), ("x", "z", "l")) * 2
PIECE = 128
EXTRA = 32
PIECE_ROWS = (80, 48 + 32, 96, 48, 48, 32 + EXTRA)
EARLY, LATE = (0, 1, 2), (3, 4, 5)
SETS = len(PIECE_ROWS)
SMALL = 3 * 128
VECTOR = (16, INNER)


def tail_kernel(
    v, decay, xc, d_y, bcc, dt, dt_wide, r_wide, r_rows, x_raw, start, bc_raw, dt_raw, row_dot,
    taps_x, bias_x, taps_bc, bias_bc, dt_bias, a_log, d_skip, g_norm,
    normed, d_gate, mixed, cot, layer_in, gain_in, full_z, full_x, full_out, full_small,
    out_za, out_zb, out_zc, out_xa, out_xb, out_xc, input_grad, layer_out, vector,
    weights, v_all, g_own, end, d_stepped, scores, d_scores, d_bc, sums, d_x_raw, d_small, g_x, g_bc, g_heads,
    d_normed, halo_out, halo_in, few_own, few_got,
    keep_n, keep_m, next_n, next_m, sib_n, sib_gate, sib_m, sib_cot, sib_wide, sib_small,
    parts_za, parts_zb, parts_zc, parts_xa, parts_xb, parts_xc,
    got_za1, got_zb1, got_zc1, got_xa1, got_xb1, got_xc1, sum_za1, sum_zb1, sum_zc1, sum_xa1, sum_xb1, sum_xc1,
    got_za2, got_zb2, got_zc2, got_xa2, got_xb2, got_xc2, sum_za2, sum_zb2, sum_zc2, sum_xa2, sum_xb2, sum_xc2,
    got_za3, got_zb3, got_zc3, got_xa3, got_xb3, got_xc3,
    v_send, v_recv, g_send, g_recv, sib_send, sib_recv, red_send, red_recv, all_send, all_recv,
    few_send, few_recv, halo_sem, load_sem,
):
    at = position()
    me = lax.axis_index("seq")
    core = at["core"]
    sibling = peers(at, "core")[0]
    barrier = greet_chunks(me)
    others = [sibling] + peers(at, "y")
    for other in others:
        pl.semaphore_signal(barrier, inc=1, device_id=device(other), device_id_type=pl.DeviceIdType.MESH)
    pl.semaphore_wait(barrier, HEADS - 1 + len(others))
    started = []

    def copy(src, dst, send, recv, to):
        one = pltpu.make_async_remote_copy(
            src_ref=src, dst_ref=dst, send_sem=send, recv_sem=recv,
            device_id=device(to), device_id_type=pl.DeviceIdType.MESH,
        )
        one.start()
        started.append(one)
        return one

    def swap_start(src, dst, send, recv):
        each_other(me, lambda other: chunk_copy(src, dst, send, recv, other, me).start())
        dst[me] = src[me]

    swap_start(v, v_all, v_send, v_recv)

    def columns(ref, high, which, size):
        return ref.at[:, lane_block(2 * high + which, size)]

    def transposed(ref, high, which, size):
        return ref[:, lane_block(2 * high + which, size)].astype(F32).T.astype(BF16)

    pairs = [(columns(normed, h, 1 - core, 256), sib_n.at[h]) for h in range(2)] + [(d_gate, sib_gate)]
    pairs += [(columns(mixed, h, 1 - core, 512), sib_m.at[h]) for h in range(2)] + [(cot, sib_cot)]
    from_sibling = [copy(a, b, sib_send.at[i], sib_recv.at[i], sibling) for i, (a, b) in enumerate(pairs)]

    half = weights.shape[2]
    halves = (slice(0, half), slice(half, 2 * half))

    def load(views):
        going = [pltpu.make_async_copy(views[h], weights.at[h], load_sem.at[h]) for h in range(2)]
        for one in going:
            one.start()
        return going

    loading = load([full_z.at[:, h] for h in halves])

    d_scores[...] = jnp.zeros_like(d_scores)
    for b in range(SEQS):
        span = slice(TOK * b, TOK * (b + 1))
        scores[b] = mm(bcc[span, STATE:], bcc[span, 0:STATE], NT)

    def inside_pair(j, _):
        cols = lane_block(j)
        for b in range(SEQS):
            span = slice(TOK * b, TOK * (b + 1))
            first, second = decay_pair(r_wide[span, cols], r_rows[j, :, span])
            both = jnp.concatenate([scores[b] * first, scores[b] * second], axis=0).astype(BF16)
            stepped = (dt_wide[span, cols] * xc[span, cols].astype(F32)).astype(BF16)
            wide = block_diagonal(d_y[span, cols])
            d_stepped[span, cols] = mm(both, wide, TN)
            d_both = mm(wide, stepped, NT)
            d_scores[b] += d_both[0:TOK, :] * first + d_both[TOK:, :] * second
        return 0

    pairs_loop(0, PAIRS, inside_pair)
    for b in range(SEQS):
        span = slice(TOK * b, TOK * (b + 1))
        low = d_scores[b].astype(BF16)
        d_bc[span, 0:STATE] = mm(low, bcc[span, STATE:], TN)
        d_bc[span, STATE:] = mm(low, bcc[span, 0:STATE], NN)

    wait_others(v_all, v_recv)

    def chunk_step(i, carry):
        c = HEADS - 1 - i
        after = []
        for b in range(SEQS):
            g_own[c, b] = carry[b].astype(BF16)
            after.append(decay[c, b : b + 1, :] * carry[b] + v_all[c, b].astype(F32))
        return tuple(after)

    lax.fori_loop(0, HEADS, chunk_step, tuple(jnp.zeros((HEAD, STATE), F32) for _ in range(SEQS)))
    swap_start(g_own, end, g_send, g_recv)

    parts = (parts_za, parts_zb, parts_zc, parts_xa, parts_xb, parts_xc)
    got = (
        (got_za1, got_zb1, got_zc1, got_xa1, got_xb1, got_xc1),
        (got_za2, got_zb2, got_zc2, got_xa2, got_xb2, got_xc2),
        (got_za3, got_zb3, got_zc3, got_xa3, got_xb3, got_xc3),
    )
    partial = (
        (sum_za1, sum_zb1, sum_zc1, sum_xa1, sum_xb1, sum_xc1),
        (sum_za2, sum_zb2, sum_zc2, sum_xa2, sum_xb2, sum_xc2),
    )
    outs = (out_za, out_zb, out_zc, out_xa, out_xb, out_xc)
    arriving = [None] * SETS

    def send_stage(stage, which, src):
        axis = REDUCE[which][stage]
        arriving[which] = [
            copy(
                src.at[to[axis]], got[stage][which].at[d],
                red_send.at[which, stage, d], red_recv.at[which, stage, d], to,
            )
            for d, to in enumerate(peers(at, axis))
        ]

    def arrived(which):
        for one in arriving[which]:
            one.wait_recv()

    def add_stage(stage, which):
        arrived(which)
        src = parts[which] if stage == 0 else partial[0][which]
        dst, came = partial[stage][which], got[stage][which]
        mine = at[REDUCE[which][stage]]

        def add(i, _):
            for j in range(4) if stage == 0 else ((),):
                index = (i, j) if stage == 0 else (i,)
                value = src[(mine, *index)].astype(F32)
                for d in range(3):
                    value = value + came[(d, *index)].astype(F32)
                dst[index] = value.astype(BF16)
            return 0

        lax.fori_loop(0, 4, add, 0)
        send_stage(stage + 1, which, dst)

    def gather_stage(stage, which):
        first, second, third = GATHER[which]
        index = (at[third], at[second], at[first])[: 3 - stage]
        ref = outs[which].at[index]
        arriving[which] = [
            copy(ref, ref, all_send.at[which, stage, d], all_recv.at[which, stage, d], to)
            for d, to in enumerate(peers(at, (first, second, third)[stage]))
        ]

    def last_add(which):
        arrived(which)
        first, second, third = GATHER[which]
        value = partial[1][which][at[REDUCE[which][2]]].astype(F32)
        for d in range(3):
            value = value + got[2][which][d].astype(F32)
        outs[which][at[third], at[second], at[first]] = value.astype(BF16)
        gather_stage(0, which)

    def gather_next(stage, which):
        arrived(which)
        gather_stage(stage, which)

    for h in range(2):
        keep_n[256 * h : 256 * (h + 1), :] = transposed(normed, h, core, 256)
        keep_m[512 * h : 512 * (h + 1), :] = transposed(mixed, h, core, 512)
    for one in from_sibling[:3]:
        one.wait_recv()
    for h in range(2):
        next_n[256 * h : 256 * (h + 1), :] = sib_n[h].astype(F32).T.astype(BF16)

    def tile_z(n, _):
        cols = lane_block(n, 256)
        res = mm(keep_n[:, 0:ROWS], d_gate[:, cols], NN) + mm(next_n[:, 0:ROWS], sib_gate[:, cols], NN)
        for y in range(4):
            for k in range(2):
                block = res[128 * y : 128 * y + 128, 128 * k : 128 * k + 128].astype(BF16)
                x, z = n // 2, (n % 2) * 2 + k
                parts_za[y, z, x] = block[0:80]
                parts_zb[z, x, y, 0:48] = block[80:128]
        return 0

    lax.fori_loop(0, 8, tile_z, 0)
    send_stage(0, 0, parts_za)
    for one in from_sibling[3:]:
        one.wait_recv()
    for h in range(2):
        next_m[512 * h : 512 * (h + 1), :] = sib_m[h].astype(F32).T.astype(BF16)

    def tile_out(n, _):
        cols = lane_block(n, 256)
        res = mm(keep_m[...], cot[:, cols], NN) + mm(next_m[...], sib_cot[:, cols], NN)
        for y in range(4):
            for half in range(2):
                for k in range(2):
                    row = 256 * y + 128 * half
                    block = res[row : row + 128, 128 * k : 128 * k + 128].astype(BF16)
                    x, z = half * 2 + n // 2, (n % 2) * 2 + k
                    parts_zb[z, x, y, 48:80] = block[0:32]
                    parts_zc[x, y, z] = block[32:128]
        return 0

    lax.fori_loop(0, 4, tile_out, 0)
    send_stage(0, 1, parts_zb)
    send_stage(0, 2, parts_zc)

    for one in loading:
        one.wait()
    for n in range(4):
        cols = slice(256 * n, 256 * (n + 1))
        d_normed[0:ROWS, cols] = sum(mm(d_gate[:, h], weights[i, cols, :], NT) for i, h in enumerate(halves))
    loading = load([full_x.at[:, h] for h in halves])

    wait_others(end, g_recv)
    sums[...] = jnp.zeros_like(sums)

    def back_pair(j, _):
        cols = lane_block(j)
        ex = pair_matrix(j)
        skip = d_skip[:, cols]
        raw = x_raw[:, cols].astype(F32)
        halos, grads = [], None
        d_steps, dots, end_rows = [], [], []
        skip_sum = jnp.zeros((1, 128), F32)
        for b in range(SEQS):
            span = slice(TOK * b, TOK * (b + 1))
            r_lanes = r_wide[span, cols]
            dt_lanes = dt_wide[span, cols]
            last = r_lanes[TOK - 1 : TOK, :]
            grown = jnp.exp(r_lanes)
            to_end = jnp.exp(last - r_lanes)
            before = jnp.concatenate([start[2 * j, b], start[2 * j + 1, b]], axis=0)
            after = jnp.concatenate([end[2 * j, b], end[2 * j + 1, b]], axis=0)
            x = xc[span, cols].astype(F32)
            dy = d_y[span, cols].astype(F32)
            stepped = (dt_lanes * x).astype(BF16).astype(F32)
            carried = to_end * mm(bcc[span, 0:STATE], after, NT)
            d_step = d_stepped[span, cols] + carried
            dots.append(stepped * d_step)
            d_x = dt_lanes * d_step + skip * dy
            d_steps.append(x * d_step)
            inner = lane_sums(before.astype(F32) * after.astype(F32))
            end_rows.append(jnp.sum(stepped * carried, axis=0, keepdims=True) + jnp.exp(last) * inner)
            d_bc[span, STATE:] += mm((grown * dy).astype(BF16), before, NN)
            d_bc[span, 0:STATE] += mm((to_end * stepped).astype(BF16), after, NN)
            skip_sum = skip_sum + jnp.sum(dy * x, axis=0, keepdims=True)
            d_pad, d_taps, d_bias = conv_back(padded_of(raw, b), taps_x[:, cols], bias_x[:, cols], d_x)
            d_x_raw[span, cols] = d_pad[HALO:, :].astype(BF16)
            halos.append(d_pad[0:HALO, :])
            found = [*d_taps, d_bias]
            grads = found if grads is None else [g + p for g, p in zip(grads, found)]
        d_x_raw[ROWS:, cols] = jnp.concatenate(halos, axis=0).astype(BF16)
        g_x[:, cols] = jnp.concatenate([*grads, jnp.zeros((8 - TAPS - 1, 128), F32)], axis=0)
        few = jnp.concatenate([*end_rows, skip_sum, jnp.zeros((5, 128), F32)], axis=0)
        sums[...] += head_sums(jnp.concatenate([*d_steps, *dots, few], axis=0), ex)
        return 0

    wide_coming = []
    for quarter in range(4):
        pairs_loop(4 * quarter, 4 * quarter + 4, back_pair)
        cols = slice(512 * quarter, 512 * (quarter + 1))
        wide_coming.append(
            copy(d_x_raw.at[:, cols], sib_wide.at[:, cols], sib_send.at[6 + quarter], sib_recv.at[6 + quarter], sibling)
        )
    raw = bc_raw[...].astype(F32)
    halos, grads = [], None
    for b in range(SEQS):
        span = slice(TOK * b, TOK * (b + 1))
        d_pad, d_taps, d_bias = conv_back(padded_of(raw, b), taps_bc[...], bias_bc[...], d_bc[span, :])
        d_small[span, 0 : 2 * STATE] = d_pad[HALO:, :].astype(BF16)
        halos.append(d_pad[0:HALO, :])
        found = [*d_taps, d_bias]
        grads = found if grads is None else [g + p for g, p in zip(grads, found)]
    d_small[ROWS:, 0 : 2 * STATE] = jnp.concatenate(halos, axis=0).astype(BF16)
    d_small[ROWS:, 2 * STATE :] = jnp.zeros((ALL - ROWS, SMALL - 2 * STATE), BF16)
    g_bc[...] = jnp.concatenate([*grads, jnp.zeros((8 - TAPS - 1, 2 * STATE), F32)], axis=0)
    rate = -jnp.exp(a_log[...])
    tri = causal_mask().astype(F32)
    is_last = iota((TOK, HEADS), 0) == TOK - 1
    bias_sum = jnp.zeros((1, HEADS), F32)
    log_sum = jnp.zeros((1, HEADS), F32)
    for b in range(SEQS):
        span = slice(TOK * b, TOK * (b + 1))
        step = dt[span, :]
        d_dt = sums[span, :]
        d_r = row_dot[span, :] - sums[ROWS + TOK * b : ROWS + TOK * (b + 1), :]
        d_r = d_r + jnp.where(is_last, sums[2 * ROWS + b : 2 * ROWS + b + 1, :], 0.0)
        d_log = mm(tri, d_r, TN, HIGHEST)
        d_pre = (d_dt + rate * d_log) * jax.nn.sigmoid(dt_raw[span, :].astype(F32) + dt_bias[...])
        d_small[span, 2 * STATE :] = jnp.concatenate(
            [d_pre, jnp.zeros((TOK, SMALL - 2 * STATE - HEADS), F32)], axis=1
        ).astype(BF16)
        bias_sum = bias_sum + jnp.sum(d_pre, axis=0, keepdims=True)
        log_sum = log_sum + jnp.sum(d_log * step, axis=0, keepdims=True) * rate
    g_heads[...] = jnp.concatenate(
        [bias_sum, log_sum, sums[2 * ROWS + 2 : 2 * ROWS + 3, :], jnp.zeros((5, HEADS), F32)], axis=0
    )
    small_coming = copy(d_small, sib_small, sib_send.at[10], sib_recv.at[10], sibling)

    for which in EARLY:
        add_stage(0, which)

    def tile_x(n, _):
        cols = lane_block(n, 256)
        res = mm(keep_n[...], d_x_raw[:, cols], NN) + mm(next_n[...], sib_wide[:, cols], NN)
        for y in range(4):
            for k in range(2):
                block = res[128 * y : 128 * y + 128, 128 * k : 128 * k + 128].astype(BF16)
                x, z = n // 2, (n % 2) * 2 + k
                parts_xa[x, y, z] = block[0:48]
                parts_xb[y, z, x] = block[48:96]
                parts_xc[z, x, y, 0:32] = block[96:128]
        return 0

    for quarter in range(4):
        wide_coming[quarter].wait_recv()
        lax.fori_loop(2 * quarter, 2 * quarter + 2, tile_x, 0)
    send_stage(0, 3, parts_xa)
    send_stage(0, 4, parts_xb)
    small_coming.wait_recv()
    res = mm(keep_n[...], d_small[...], NN) + mm(next_n[...], sib_small[...], NN)
    for y in range(4):
        for z in range(4):
            row = 128 * y + EXTRA * z
            for k in range(3):
                parts_xc[z, k, y, 32:] = res[row : row + EXTRA, 128 * k : 128 * k + 128].astype(BF16)
            parts_xc[z, 3, y, 32:] = jnp.zeros((EXTRA, 128), BF16)
    send_stage(0, 5, parts_xc)
    for which in EARLY:
        add_stage(1, which)

    for one in loading:
        one.wait()
    d_normed[ROWS:, :] = jnp.zeros((ALL - ROWS, d_normed.shape[1]), F32)
    for n in range(4):
        cols = slice(256 * n, 256 * (n + 1))
        d_normed[:, cols] += mm(d_small[...], full_small[cols, :], NT) + sum(
            mm(d_x_raw[:, h], weights[i, cols, :], NT) for i, h in enumerate(halves)
        )
    loading = load([full_out.at[h, :] for h in halves])
    halo_out[...] = d_normed[ROWS:, :]
    halo = pltpu.make_async_remote_copy(
        src_ref=halo_out, dst_ref=halo_in, send_sem=halo_sem.at[0], recv_sem=halo_sem.at[1],
        device_id={"seq": lax.rem(me + HEADS - 1, HEADS)}, device_id_type=pl.DeviceIdType.MESH,
    )
    halo.start()
    started.append(halo)
    for which in EARLY:
        last_add(which)
    halo.wait_recv()
    inner = jnp.where(me == HEADS - 1, 0.0, 1.0)
    for b in range(SEQS):
        near = slice(TOK * (b + 1) - HALO, TOK * (b + 1))
        d_normed[near, :] += inner * halo_in[HALO * b : HALO * (b + 1), :]
    g_in = jnp.zeros((1, d_normed.shape[1]), F32)
    for n in range(4):
        span = slice(64 * n, 64 * (n + 1))
        hidden = layer_in[span, :].astype(F32)
        inv = lax.rsqrt(jnp.mean(hidden * hidden, axis=1, keepdims=True) + EPS)
        unit = hidden * inv
        grad = d_normed[span, :]
        g_in = g_in + jnp.sum(grad * unit, axis=0, keepdims=True)
        pulled = grad * gain_in[...]
        d_hidden = inv * (pulled - unit * jnp.mean(pulled * unit, axis=1, keepdims=True))
        input_grad[span, :] = cot[span, :].astype(F32) + d_hidden

    few_axes = ("core", "x", "z", "y")
    rest = jnp.concatenate(
        [
            g_bc[...], jnp.concatenate([g_heads[...], jnp.zeros((8, 128 - HEADS), F32)], axis=1),
            jnp.zeros((8, INNER - 2 * STATE - 128), F32),
        ],
        axis=1,
    )
    wide_in = jnp.concatenate([g_in, jnp.zeros((1, INNER - g_in.shape[1]), F32)], axis=1)
    few = jnp.concatenate([g_x[...], g_norm[...], wide_in, rest[0 : TAPS + 1], jnp.zeros((1, INNER), F32)], axis=0)

    few_coming = [None]

    def few_start(stage, value):
        few_own[stage] = value.astype(BF16)
        axis = few_axes[stage]
        few_got[stage, at[axis]] = few_own[stage]
        few_coming[0] = [
            copy(
                few_own.at[stage], few_got.at[stage, at[axis]],
                few_send.at[stage, d], few_recv.at[stage, d], to,
            )
            for d, to in enumerate(peers(at, axis))
        ]

    def few_sum(stage):
        for one in few_coming[0]:
            one.wait_recv()
        value = few_got[stage, 0].astype(F32)
        for i in range(1, 2 if stage == 0 else 4):
            value = value + few_got[stage, i].astype(F32)
        return value

    few_start(0, few)
    for which in EARLY:
        gather_next(1, which)
    for which in LATE:
        add_stage(0, which)
    few_start(1, few_sum(0))
    for which in LATE:
        add_stage(1, which)
    few_start(2, few_sum(1))
    for which in EARLY:
        gather_next(2, which)
    for one in loading:
        one.wait()
    for n in range(4):
        cols = slice(256 * n, 256 * (n + 1))
        product = sum(mm(mixed[:, h], weights[i, :, cols], NN) for i, h in enumerate(halves))
        layer_out[:, cols] = (layer_in[:, cols].astype(F32) + product).astype(BF16)
    for which in LATE:
        last_add(which)
    few_start(3, few_sum(2))
    for which in LATE:
        gather_next(1, which)
    vector[...] = few_sum(3)
    for which in LATE:
        gather_next(2, which)
    for which in range(SETS):
        arrived(which)
    for one in started:
        one.wait_send()
    wait_others(v, v_send)
    wait_others(g_own, g_send)


def tail(*args):
    vmem = pl.BlockSpec(memory_space=pltpu.VMEM)
    hbm = pl.BlockSpec(memory_space=pl.ANY)
    specs = [vmem] * len(args)
    specs[-4] = specs[-3] = specs[-2] = hbm
    width = args[-1].shape[0]
    dims = {"x": 4, "z": 4, "l": 2}
    out_shape = [
        jax.ShapeDtypeStruct((*(dims[a] for a in reversed(GATHER[i])), PIECE_ROWS[i], 128), BF16) for i in range(SETS)
    ]
    out_shape += [jax.ShapeDtypeStruct((ROWS, width), d) for d in (F32, BF16)] + [jax.ShapeDtypeStruct(VECTOR, F32)]

    def bufs(*lead):
        return [pltpu.VMEM((*lead, PIECE_ROWS[i], 128), BF16) for i in range(SETS)]

    def sems(*shape):
        return [pltpu.SemaphoreType.DMA(shape)] * 2

    scratch = [
        pltpu.VMEM((2, width, INNER // 2), BF16), *[pltpu.VMEM(STATES_SHAPE, BF16)] * 3, pltpu.VMEM((ROWS, INNER), F32),
        *[pltpu.VMEM((SEQS, TOK, TOK), F32)] * 2, pltpu.VMEM((ROWS, 2 * STATE), F32),
        pltpu.VMEM((2 * ROWS + 8, HEADS), F32), pltpu.VMEM((ALL, INNER), BF16), pltpu.VMEM((ALL, SMALL), BF16),
        pltpu.VMEM((8, INNER), F32), pltpu.VMEM((8, 2 * STATE), F32), pltpu.VMEM((8, HEADS), F32),
        pltpu.VMEM((ALL, width), F32), *[pltpu.VMEM((SEQS * HALO, width), F32)] * 2,
        pltpu.VMEM((4, *VECTOR), BF16), pltpu.VMEM((4, 4, *VECTOR), BF16),
        *[pltpu.VMEM((512, ALL), BF16), pltpu.VMEM((1024, ROWS), BF16)] * 2,
        pltpu.VMEM((2, ALL, 256), BF16), pltpu.VMEM((ROWS, INNER), BF16), pltpu.VMEM((2, ROWS, 512), BF16),
        pltpu.VMEM((ROWS, width), BF16), pltpu.VMEM((ALL, INNER), BF16), pltpu.VMEM((ALL, SMALL), BF16),
        *bufs(4, 4, 4), *bufs(3, 4, 4), *bufs(4, 4), *bufs(3, 4), *bufs(4), *bufs(3),
        *[pltpu.SemaphoreType.DMA] * 4, *sems(11), *sems(SETS, 3, 3), *sems(SETS, 3, 3), *sems(4, 3),
        pltpu.SemaphoreType.DMA((2,)), pltpu.SemaphoreType.DMA((2,)),
    ]
    return pl.pallas_call(
        tail_kernel,
        out_shape=out_shape,
        in_specs=specs,
        out_specs=[vmem] * len(out_shape),
        scratch_shapes=scratch,
        compiler_params=pltpu.CompilerParams(
            vmem_limit_bytes=VMEM_LIMIT, collective_id=1, has_side_effects=True
        ),
        cost_estimate=pl.CostEstimate(flops=int(8e9), bytes_accessed=int(4e7), transcendentals=0),
    )(*args)


def unpack_kernel(
    sum_za, sum_zb, sum_zc, sum_xa, sum_xb, sum_xc, total,
    out_z, out_x, out_out, out_extra, g_x, g_norm, g_in, g_bc, g_heads,
):
    for low in range(2):
        base = PIECE * low
        for z in range(4):
            cols = slice(128 * z, 128 * (z + 1))
            out_z[base : base + 80, cols] = sum_za[0, z, low].astype(F32)
            out_z[base + 80 : base + 128, cols] = sum_zb[z, 0, low, 0:48, :].astype(F32)
            out_out[low, 0, 0:32, cols] = sum_zb[z, 0, low, 48:80, :].astype(F32)
            out_out[low, 0, 32:128, cols] = sum_zc[low, z, 0].astype(F32)
            out_x[base : base + 48, cols] = sum_xa[0, z, low].astype(F32)
            out_x[base + 48 : base + 96, cols] = sum_xb[z, 0, low].astype(F32)
            out_x[base + 96 : base + 128, cols] = sum_xc[low, z, 0, 0:32, :].astype(F32)
            out_extra[0, low, EXTRA * z : EXTRA * (z + 1), :] = sum_xc[low, z, 0, 32:, :].astype(F32)

    @pl.when(pl.program_id(0) == 0)
    def _():
        g_x[...] = total[0:8, :]
        rest = total[8:16, :]
        g_norm[...] = rest[0:1, :]
        g_in[...] = rest[1:2, 0 : g_in.shape[1]]
        g_bc[...] = rest[2 : 2 + TAPS + 1, 0 : 2 * STATE]
        g_heads[...] = rest[2:5, 2 * STATE : 2 * STATE + 128]


def unpack(width, *gathered):
    few = ((8, INNER), (1, INNER), (1, width), (TAPS + 1, 2 * STATE), (3, 128))
    specs = []
    for i in range(SETS):
        def where(n, order=GATHER[i]):
            return tuple({"x": n, "z": 0, "l": 0}[a] for a in reversed(order)) + (0, 0)

        block = tuple({"x": 1, "z": 4, "l": 2}[a] for a in reversed(GATHER[i])) + (PIECE_ROWS[i], 128)
        specs.append(pl.BlockSpec(block, where))
    wide = pl.BlockSpec((2 * PIECE, WIDE), lambda i: (0, i))
    return call(
        unpack_kernel,
        [((2 * PIECE, INNER), F32), ((2 * PIECE, INNER), F32), ((2, 2, PIECE, 8 * 128), F32), ((4, 2, 4 * EXTRA, 128), F32)]
        + [(d, F32) for d in few],
        [
            wide, wide,
            pl.BlockSpec((2, 1, PIECE, WIDE), lambda i: (0, i // 2, 0, i % 2)),
            pl.BlockSpec((1, 2, 4 * EXTRA, 128), lambda i: (i, 0, 0, 0)), *[whole(d) for d in few],
        ],
        [*specs, whole(VECTOR)],
        grid=(4,),
    )(*gathered)


def gather_kernel(
    w_x, w_small, own, tokens, w_z, w_out, full_x, full_small, params, earlier, full_z, full_out, send, recv, here, own_send, own_recv, near_send, near_recv,
):
    at = position()
    sibling = peers(at, "core")[0]
    partner = moved(at, "y", 3 - at["y"])
    everyone = [sibling, partner] + [p for axis in ("x", "z", "l") for p in peers(at, axis)]
    me = lax.axis_index("seq")
    after, before = lax.rem(me + 1, HEADS), lax.rem(me + HEADS - 1, HEADS)
    barrier = pltpu.get_barrier_semaphore()
    for chunk in (after, before):
        pl.semaphore_signal(barrier, inc=1, device_id={"seq": chunk}, device_id_type=pl.DeviceIdType.MESH)
    greet(everyone, 2)
    started = []
    near = []
    for b in range(SEQS):
        one = pltpu.make_async_remote_copy(
            src_ref=tokens.at[b, TOK - 16 :], dst_ref=earlier.at[b], send_sem=near_send.at[b], recv_sem=near_recv.at[b],
            device_id={"seq": after}, device_id_type=pl.DeviceIdType.MESH,
        )
        one.start()
        started.append(one)
        near.append(one)

    def copy(src, dst, which, to, sems=(send, recv)):
        one = pltpu.make_async_remote_copy(
            src_ref=src, dst_ref=dst, send_sem=sems[0].at[which], recv_sem=sems[1].at[which],
            device_id=device(to), device_id_type=pl.DeviceIdType.MESH,
        )
        one.start()
        started.append(one)
        return one

    half, quarter = INNER // 2, w_out.shape[1] // 2
    flows = Flows(
        at,
        (
            (w_x, full_x, 0, half, "x", "z", 16), (w_x, full_x, half, half, "z", "x", 16),
            (w_small, full_small, 0, SMALL, "x", "z", 16),
            (w_z, full_z, 0, half, "x", "z", 16), (w_z, full_z, half, half, "z", "x", 16),
            (w_out, full_out, 0, quarter, "x", "z", 32), (w_out, full_out, quarter, quarter, "z", "x", 32),
        ),
        copy,
    )
    flows.begin()
    params_here = pltpu.make_async_copy(own, params.at[at["z"], at["x"], at["l"]], here.at[2])
    local = [
        pltpu.make_async_copy(w_x, full_x.at[flows.mine], here.at[0]),
        pltpu.make_async_copy(w_small, full_small.at[flows.mine], here.at[1]),
        params_here,
        pltpu.make_async_copy(w_z, full_z.at[flows.mine], here.at[3]),
        pltpu.make_async_copy(w_out, full_out.at[flows.mine], here.at[4]),
    ]
    for one in local:
        one.start()
    flows.own([(w_x, full_x), (w_small, full_small), (w_z, full_z), (w_out, full_out)])
    params_here.wait()

    def share(stage):
        axis = ("l", "x", "z")[stage]
        ref = params.at[(at["z"], at["x"], at["l"])[: 3 - stage]]
        return [copy(ref, ref, 3 * stage + d, to, (own_send, own_recv)) for d, to in enumerate(peers(at, axis))]

    shared = share(0)
    flows.spread()
    for one in shared:
        one.wait_recv()
    shared = share(1)
    flows.spread_more()
    for one in shared:
        one.wait_recv()
    shared = share(2)
    flows.forward()
    flows.finish()
    for one in shared + near:
        one.wait_recv()
    for one in (*local[:2], *local[3:]):
        one.wait()
    for one in started:
        one.wait_send()


def gather_weights(w_x, w_small, own, tokens, w_z, w_out):
    vmem = pl.BlockSpec(memory_space=pltpu.VMEM)
    hbm = pl.BlockSpec(memory_space=pl.ANY)
    return pl.pallas_call(
        gather_kernel,
        out_shape=[
            jax.ShapeDtypeStruct((4, *w_x.shape), BF16),
            jax.ShapeDtypeStruct((4, *w_small.shape), BF16),
            jax.ShapeDtypeStruct((4, 4, 2, 8, 128), F32),
            jax.ShapeDtypeStruct((SEQS, 16, tokens.shape[2]), BF16),
            jax.ShapeDtypeStruct((4, *w_z.shape), BF16),
            jax.ShapeDtypeStruct((4, *w_out.shape), BF16),
        ],
        in_specs=[vmem] * 4 + [hbm] * 2,
        out_specs=[vmem] * 4 + [hbm] * 2,
        scratch_shapes=[
            pltpu.SemaphoreType.DMA((81,)), pltpu.SemaphoreType.DMA((81,)), pltpu.SemaphoreType.DMA((5,)),
            pltpu.SemaphoreType.DMA((9,)), pltpu.SemaphoreType.DMA((9,)), pltpu.SemaphoreType.DMA((2,)), pltpu.SemaphoreType.DMA((2,)),
        ],
        compiler_params=pltpu.CompilerParams(
            vmem_limit_bytes=48 * 1024 * 1024, collective_id=2, has_side_effects=True
        ),
        cost_estimate=pl.CostEstimate(flops=int(1e6), bytes_accessed=int(4e7), transcendentals=0),
    )(w_x, w_small, own, tokens, w_z, w_out)


def shards(
    layer_in, gain_in, w_z, w_x, w_bc, w_dt, conv_x_weight, conv_x_bias, conv_bc_weight, conv_bc_bias,
    dt_bias, a_log, d_skip, gain_norm, w_out, cotangent,
):
    width = layer_in.shape[2]
    place = lax.axis_index("seq")
    own = jnp.concatenate([conv_x_weight.reshape(-1), conv_x_bias, dt_bias, a_log, d_skip, jnp.zeros((701,), F32)])
    small = jnp.concatenate([w_bc, w_dt, jnp.zeros((w_bc.shape[0], SMALL - 2 * STATE - HEADS), BF16)], axis=1)
    full_x, full_small, params, earlier, full_z, full_out = gather_weights(
        w_x, small, own.reshape(8, 128), layer_in, w_z, w_out
    )
    full_x = full_x.reshape(width, INNER)
    full_small = full_small.reshape(width, SMALL)
    params = params.reshape(HEADS, -1)
    taps_x = params[:, : TAPS * HEAD].reshape(HEADS, TAPS, HEAD).swapaxes(0, 1).reshape(TAPS, INNER)
    bias_x = params[:, TAPS * HEAD : (TAPS + 1) * HEAD].reshape(1, INNER)
    bias_dt, log_a, skip = (params[:, (TAPS + 1) * HEAD + i].reshape(1, HEADS) for i in range(3))
    bias_bc = conv_bc_bias.reshape(1, -1)
    skip_wide = jnp.repeat(skip, HEAD, axis=1)

    hidden = layer_in.astype(F32).reshape(ROWS, width)
    upstream = cotangent.reshape(ROWS, width)
    halo = earlier[:, HALO:].astype(F32)
    kept = (lax.broadcasted_iota(jnp.int32, halo.shape, 1) >= HALO - (TAPS - 1)) & (place > 0)
    halo = jnp.where(kept, halo, 0.0).reshape(SEQS * HALO, width)
    tokens = jnp.concatenate([hidden, halo], axis=0)
    inv = lax.rsqrt(jnp.mean(tokens * tokens, axis=-1, keepdims=True) + EPS)
    normed = (tokens * inv * gain_in[None, :]).astype(BF16)

    x_raw = mm(normed, full_x, NN).astype(BF16)
    small_raw = mm(normed, full_small, NN).astype(BF16)
    bc_raw, dt_raw = small_raw[:, : 2 * STATE], small_raw[:, 2 * STATE : 2 * STATE + HEADS]
    xc, bcc, dt, dt_wide, r_wide, r_rows, y_in, start, decay = head(
        x_raw, bc_raw, dt_raw, taps_x, bias_x, conv_bc_weight, bias_bc, bias_dt, log_a
    )
    full_z = full_z.reshape(width, INNER)
    full_out = full_out.reshape(INNER, width)
    mixed, d_y, d_gate, v, g_norm, row_dot = middle(
        y_in, xc, bcc, r_wide, start, skip_wide, normed, upstream, full_z, full_out, gain_norm.reshape(1, INNER)
    )
    *gathered, input_grad, layer_out, total = tail(
        v, decay, xc, d_y, bcc, dt, dt_wide, r_wide, r_rows, x_raw, start, bc_raw, dt_raw, row_dot,
        taps_x, bias_x, conv_bc_weight, bias_bc, bias_dt, log_a, skip_wide, g_norm,
        normed, d_gate, mixed, upstream, layer_in.reshape(ROWS, width), gain_in.reshape(1, width),
        full_z, full_x, full_out, full_small,
    )
    layer_out = layer_out.reshape(SEQS, TOK, width)
    input_grad = input_grad.reshape(SEQS, TOK, width)
    grad_w_z, grad_w_x, grad_w_out, extra, s_x, s_norm, s_in, s_bc, s_heads = unpack(width, *gathered, total)
    grad_w_out = grad_w_out.reshape(4 * PIECE, width)
    extra = extra.reshape(4, 2 * PIECE, 128)
    grad_w_bc = jnp.concatenate([extra[0], extra[1]], axis=1)
    grad_w_dt = extra[2][:, :HEADS]
    s_x = lax.dynamic_slice(s_x, (0, place * HEAD), (TAPS + 1, HEAD))
    s_norm, s_in = s_norm.reshape(INNER), s_in.reshape(width)
    s_heads = lax.dynamic_slice(s_heads, (0, place), (3, 1))
    return (
        layer_out, input_grad, s_in, grad_w_z, grad_w_x, grad_w_bc, grad_w_dt,
        s_x[:TAPS], s_x[TAPS], s_bc[:TAPS], s_bc[TAPS], s_heads[0], s_heads[1], s_heads[2], s_norm, grad_w_out,
    )


def solution(mesh):
    rows, heads = P("wshard", None), P("seq")
    tokens = P("wshard", "seq", None)
    return jax.shard_map(
        shards,
        mesh=mesh,
        in_specs=(
            tokens, P(), rows, rows, rows, rows, P(None, "seq"), heads, P(), P(), heads, heads, heads, P(), rows, tokens,
        ),
        out_specs=(
            tokens, tokens, P(), rows, rows, rows, rows, P(None, "seq"), heads, P(), P(), heads, heads, heads, P(), rows,
        ),
        check_vma=False,
    )
```
